32 devices in a mesh: dp: 16 (over z, y, core), tensor: 2 (over x).
Axes of the slice: x: 2, y: 2, z: 4, core: 2. Of those that a mesh axis runs over, the one named last changes fastest.
Arguments:
- tokens: bfloat16 [8192, 1536], P(('dp', 'tensor')), may hold values from -6 to 6
- cotangent: bfloat16 [8192, 1536], P(('dp', 'tensor')), may hold values from -6 to 6
- segments: int32 [8192], P('dp'), may hold values from 0 to 4, as said below
- small_params: float32 [5120], replicated, as said below
- small_first: float32 [5120], replicated
- small_second: float32 [5120], replicated, as said below
- qkv_weight: float32 [1536, 2048], P('dp', 'tensor'), may hold values from -0.15625 to 0.15625
- qkv_first: float32 [1536, 2048], P('dp', 'tensor')
- qkv_second: float32 [1536, 2048], P('dp', 'tensor'), as said below
- out_weight: float32 [1536, 1536], P('tensor', 'dp')
- out_first: float32 [1536, 1536], P('tensor', 'dp')
- out_second: float32 [1536, 1536], P('tensor', 'dp'), as said below
- gateup_weight: float32 [2, 1536, 8960], P(None, 'dp', 'tensor'), may hold values from -0.15625 to 0.15625
- gateup_first: float32 [2, 1536, 8960], P(None, 'dp', 'tensor')
- gateup_second: float32 [2, 1536, 8960], P(None, 'dp', 'tensor'), as said below
- down_weight: float32 [8960, 1536], P('tensor', 'dp')
- down_first: float32 [8960, 1536], P('tensor', 'dp')
- down_second: float32 [8960, 1536], P('tensor', 'dp'), as said below
Outputs:
- block_out: bfloat16 [8192, 1536], P(('dp', 'tensor'))
- input_grad: float32 [8192, 1536], P(('dp', 'tensor'))
- grad_norm: float32 [], replicated
- new_small: float32 [5120], replicated
- new_small_first: float32 [5120], replicated
- new_small_second: float32 [5120], replicated
- new_qkv: float32 [1536, 2048], P('dp', 'tensor')
- new_qkv_first: float32 [1536, 2048], P('dp', 'tensor')
- new_qkv_second: float32 [1536, 2048], P('dp', 'tensor')
- new_out: float32 [1536, 1536], P('tensor', 'dp')
- new_out_first: float32 [1536, 1536], P('tensor', 'dp')
- new_out_second: float32 [1536, 1536], P('tensor', 'dp')
- new_gateup: float32 [2, 1536, 8960], P(None, 'dp', 'tensor')
- new_gateup_first: float32 [2, 1536, 8960], P(None, 'dp', 'tensor')
- new_gateup_second: float32 [2, 1536, 8960], P(None, 'dp', 'tensor')
- new_down: float32 [8960, 1536], P('tensor', 'dp')
- new_down_first: float32 [8960, 1536], P('tensor', 'dp')
- new_down_second: float32 [8960, 1536], P('tensor', 'dp')
The draws below stay inside these ranges and needn't reach their ends.
Inputs may be any that keep to these rules, and one draw needn't show every extreme that they name: `segments`: within each sequence of 1024 tokens the numbers start at 0, never fall and rise by one at each document's start; every sequence holds five documents, and the one that holds the sequence's middle token starts in its first quarter and ends in its last. `small_params`: the first 3072 entries are positive. `small_second`: positive. `qkv_second`: positive. `out_second`: positive. `gateup_second`: positive. `down_second`: positive.
All inputs are finite; a program needn't handle non-finite values.
Results may differ from the reference program's by a relative error of at most 0.015.
Values may be sent and summed in bfloat16 or wider, within the bound.
No kernel may reach another device: no remote copies, remote signals or barrier semaphores. Data moves between devices by JAX's collectives and lax.ppermute only.
A program may use at most 384 MiB of HBM per device.

```python
import math
import jax
import jax.numpy as jnp
from jax import lax

D = 1536
FF = 8960
QUERY_HEADS = 12
KEY_VALUE_HEADS = 2
HEAD_WIDTH = 128
STEP = 10
QKV = 2048
SEQUENCE_LENGTH = 1024
TOKENS = 8192


MAX_NORM = 1.0


def grad_size():
    param_count = D * QKV + QUERY_HEADS * HEAD_WIDTH * D + 3 * D * FF + 2 * D + QKV
    return MAX_NORM / math.sqrt(param_count)


def first_moment(key, shape):
    return 0.111 * grad_size() * jax.random.normal(key, shape, jnp.float32)


def second_moment(key, shape):
    factor = jnp.exp(jax.random.uniform(key, shape, jnp.float32, math.log(0.5), math.log(2.0)))
    return 0.002 * grad_size() * grad_size() * factor


def rising_rows(row_count, growth):
    across = jnp.arange(row_count, dtype=jnp.float32) / (row_count - 1)
    return growth ** (0.5 * across)


def draw_segments(key, part):
    key = jax.random.fold_in(key, 11)
    sequence_count = TOKENS // SEQUENCE_LENGTH
    eighth = SEQUENCE_LENGTH // 8
    key_one, key_two, key_three, key_four = jax.random.split(key, 4)
    cut_one = jax.random.randint(key_one, (sequence_count, 1), 1, eighth + 1)
    cut_two = jax.random.randint(key_two, (sequence_count, 1), eighth + 1, 2 * eighth + 1)
    cut_three = jax.random.randint(key_three, (sequence_count, 1), 6 * eighth, 7 * eighth)
    cut_four = jax.random.randint(key_four, (sequence_count, 1), 7 * eighth, 8 * eighth)
    places = jnp.arange(SEQUENCE_LENGTH, dtype=jnp.int32)[None, :]
    cuts = (places == cut_one) | (places == cut_two) | (places == cut_three) | (places == cut_four)
    document_labels = jnp.cumsum(cuts.astype(jnp.int32), axis=1).astype(jnp.int32)
    return document_labels.reshape(TOKENS)


def draw_small_params(key, part):
    key = jax.random.fold_in(key, 21)
    key_gain, key_bias = jax.random.split(key, 2)
    growth = 3.0
    bias = 0.5 * jax.random.truncated_normal(key_bias, -3.0, 3.0, (QKV,), jnp.float32)
    factor = jnp.exp(jax.random.uniform(key_gain, (2, D), jnp.float32, -0.3, 0.3))
    gains = 0.75 * rising_rows(D, growth)[None, :] * factor
    return jnp.concatenate([gains.reshape(2 * D), bias])


def draw_small_first(key, part):
    key = jax.random.fold_in(key, 22)
    return first_moment(key, (2 * D + QKV,))


def draw_small_second(key, part):
    key = jax.random.fold_in(key, 23)
    return second_moment(key, (2 * D + QKV,))


def draw_qkv_first(key, part):
    key = jax.random.fold_in(key, 31)
    return first_moment(key, (D, QKV))


def draw_qkv_second(key, part):
    key = jax.random.fold_in(key, 32)
    return second_moment(key, (D, QKV))


def draw_out_weight(key, part):
    key = jax.random.fold_in(key, 41)
    row_count = QUERY_HEADS * HEAD_WIDTH
    growth = 3.0
    entries = jax.random.truncated_normal(key, -4.0, 4.0, (row_count, D), jnp.float32)
    return entries * (3.2 / math.sqrt(row_count)) * rising_rows(row_count, growth)[:, None]


def draw_out_first(key, part):
    key = jax.random.fold_in(key, 42)
    return first_moment(key, (QUERY_HEADS * HEAD_WIDTH, D))


def draw_out_second(key, part):
    key = jax.random.fold_in(key, 43)
    return second_moment(key, (QUERY_HEADS * HEAD_WIDTH, D))


def draw_gateup_first(key, part):
    key = jax.random.fold_in(key, 51)
    return first_moment(key, (2, D, FF))


def draw_gateup_second(key, part):
    key = jax.random.fold_in(key, 52)
    return second_moment(key, (2, D, FF))


def draw_down_weight(key, part):
    key = jax.random.fold_in(key, 61)
    growth = 3.0
    entries = jax.random.truncated_normal(key, -4.0, 4.0, (FF, D), jnp.float32)
    return entries * (0.8 / math.sqrt(FF)) * rising_rows(FF, growth)[:, None]


def draw_down_first(key, part):
    key = jax.random.fold_in(key, 62)
    return first_moment(key, (FF, D))


def draw_down_second(key, part):
    key = jax.random.fold_in(key, 63)
    return second_moment(key, (FF, D))


def levels(stream_key, extent, cuts, low, largest):
    def one(axis_at, blocks):
        steps = jax.random.uniform(jax.random.fold_in(jax.random.fold_in(stream_key, 6), axis_at), (blocks,), jnp.float32, low / len(cuts), largest / len(cuts))
        return jnp.repeat(jnp.exp(steps), extent[axis_at] // blocks).reshape((-1,) + (1,) * (len(extent) - axis_at - 1))

    gain = one(*cuts[0])
    for cut in cuts[1:]:
        gain = gain * one(*cut)
    return gain


def normal_values(own_key, dims, scale, reach, pieces=(), kind=jnp.bfloat16):
    drawn = scale * jax.random.normal(own_key, dims, jnp.float32)
    if pieces:
        drawn = drawn * levels(own_key, dims, pieces, -0.22, 0.18)
    return jnp.clip(drawn, -reach, reach).astype(kind)


def setup_inputs(seed: int = 0) -> dict:
    splits = jax.random.split(jax.random.key(seed), 19)
    return {
        "tokens": normal_values(splits[0], (TOKENS, D), 1.0, 6.0, ((0, 32),)),
        "cotangent": normal_values(splits[1], (TOKENS, D), 1.0, 6.0, ((0, 32),)),
        "segments": draw_segments(jax.random.fold_in(splits[18], 71), 0),
        "small_params": draw_small_params(jax.random.fold_in(splits[18], 71), 0),
        "small_first": draw_small_first(jax.random.fold_in(splits[18], 71), 0),
        "small_second": draw_small_second(jax.random.fold_in(splits[18], 71), 0),
        "qkv_weight": normal_values(splits[6], (D, QKV), D ** -0.5, 0.15625, ((0, 16), (1, 2)), jnp.float32),
        "qkv_first": draw_qkv_first(jax.random.fold_in(splits[18], 71), 0),
        "qkv_second": draw_qkv_second(jax.random.fold_in(splits[18], 71), 0),
        "out_weight": draw_out_weight(jax.random.fold_in(splits[18], 71), 0),
        "out_first": draw_out_first(jax.random.fold_in(splits[18], 71), 0),
        "out_second": draw_out_second(jax.random.fold_in(splits[18], 71), 0),
        "gateup_weight": normal_values(splits[12], (2, D, FF), D ** -0.5, 0.15625, ((1, 16), (2, 2)), jnp.float32),
        "gateup_first": draw_gateup_first(jax.random.fold_in(splits[18], 71), 0),
        "gateup_second": draw_gateup_second(jax.random.fold_in(splits[18], 71), 0),
        "down_weight": draw_down_weight(jax.random.fold_in(splits[18], 71), 0),
        "down_first": draw_down_first(jax.random.fold_in(splits[18], 71), 0),
        "down_second": draw_down_second(jax.random.fold_in(splits[18], 71), 0),
    }


EPSILON = 1e-06
ROPE_BASE = 1000000.0
BETA_ONE = 0.9
BETA_TWO = 0.999
ADAM_EPS = 1e-08
WEIGHT_DECAY = 0.1
MAX_NORM = 1.0
NEGATIVE = -1e+30
HIGHEST = lax.Precision.HIGHEST

@jax.custom_vjp
def low(v):
    return lax.optimization_barrier(v.astype(jnp.bfloat16)).astype(jnp.float32)

@jax.custom_vjp
def low_back(v):
    return v

def low_keep(v):
    return (low(v), None)

def low_pass(kept, grad):
    return (grad,)

def back_keep(v):
    return (v, None)

def back_low(kept, grad):
    return (low(grad),)
low.defvjp(low_keep, low_pass)
low_back.defvjp(back_keep, back_low)

def rms_norm(inputs):
    return inputs * lax.rsqrt(lax.optimization_barrier(jnp.mean(inputs * inputs, axis=-1, keepdims=True)) + EPSILON)

def rotate(features, cos_part, sin_part):
    half = features.shape[-1] // 2
    front_half = features[..., :half]
    back_half = features[..., half:]
    return jnp.concatenate([front_half * cos_part - back_half * sin_part, back_half * cos_part + front_half * sin_part], axis=-1)

def tables(document_labels):
    places = jnp.arange(document_labels.shape[0], dtype=jnp.int32)
    earlier = jnp.concatenate([document_labels[:1], document_labels[:-1]])
    begins = (places == 0) | (document_labels != earlier)
    starts = lax.cummax(jnp.where(begins, places, 0), axis=0)
    positions = (places - starts).astype(jnp.float32)
    frequency = 1.0 / ROPE_BASE ** (jnp.arange(0, HEAD_WIDTH, 2, dtype=jnp.float32) / HEAD_WIDTH)
    angles = positions[:, None] * frequency[None, :]
    return (jnp.cos(angles), jnp.sin(angles))

def attend(query_rows, key_matrix_rows, value_matrix_rows, document_labels):
    places = jnp.arange(document_labels.shape[0], dtype=jnp.int32)
    allowed = (document_labels[None, :] == document_labels[:, None]) & (places[None, :] <= places[:, None])
    scores = low_back(jnp.einsum('qgih,kgh->giqk', query_rows, key_matrix_rows, precision=HIGHEST) * (1.0 / math.sqrt(HEAD_WIDTH)))
    scores = jnp.where(allowed, scores, NEGATIVE)
    row_max = lax.optimization_barrier(jnp.max(scores, axis=-1, keepdims=True))
    weights_exp = jnp.exp(scores - row_max)
    prob_low = low(weights_exp / lax.optimization_barrier(jnp.sum(weights_exp, axis=-1, keepdims=True)))
    return jnp.einsum('giqk,kgh->qgih', prob_low, value_matrix_rows, precision=HIGHEST)

def attention_pieces(parts):
    return attend(parts[0], parts[1], parts[2], parts[3])

def block_forward(weights, inputs, cos_part, sin_part, document_labels):
    small, wqkv, wout, wgateup, wdown = weights
    total_token_count = inputs.shape[0]
    sequence_count = total_token_count // SEQUENCE_LENGTH
    queries_each_group = QUERY_HEADS // KEY_VALUE_HEADS
    normed_one = low(rms_norm(inputs) * small[:D])
    projected_output = low_back(jnp.dot(normed_one, low(wqkv), precision=HIGHEST) + small[2 * D:])
    reshaped_input = projected_output.reshape(total_token_count, KEY_VALUE_HEADS, queries_each_group + 2, HEAD_WIDTH)
    query_rows = low(rotate(reshaped_input[:, :, :queries_each_group], cos_part[:, None, None, :], sin_part[:, None, None, :]))
    key_matrix_rows = low(rotate(reshaped_input[:, :, queries_each_group], cos_part[:, None, :], sin_part[:, None, :]))
    value_matrix_rows = low(reshaped_input[:, :, queries_each_group + 1])
    attention_blended = lax.map(jax.checkpoint(attention_pieces), (query_rows.reshape(sequence_count, SEQUENCE_LENGTH, KEY_VALUE_HEADS, queries_each_group, HEAD_WIDTH), key_matrix_rows.reshape(sequence_count, SEQUENCE_LENGTH, KEY_VALUE_HEADS, HEAD_WIDTH), value_matrix_rows.reshape(sequence_count, SEQUENCE_LENGTH, KEY_VALUE_HEADS, HEAD_WIDTH), document_labels.reshape(sequence_count, SEQUENCE_LENGTH)))
    attn_rows = low_back(low(attention_blended.reshape(total_token_count, QUERY_HEADS * HEAD_WIDTH)))
    branch = low_back(jnp.dot(attn_rows, low(wout), precision=HIGHEST))
    residual = inputs + branch
    normed_two = low(rms_norm(residual) * small[D:2 * D])
    gate_pre = low_back(jnp.dot(normed_two, low(wgateup[0]), precision=HIGHEST))
    up_proj = low_back(jnp.dot(normed_two, low(wgateup[1]), precision=HIGHEST))
    hidden = low(gate_pre * jax.nn.sigmoid(gate_pre) * up_proj)
    return residual + jnp.dot(hidden, low(wdown), precision=HIGHEST)

def adam_update(weight, moment_one, moment_two, gradient, step_rate, decay_rate):
    first_new = BETA_ONE * moment_one + (1.0 - BETA_ONE) * gradient
    second_new = BETA_TWO * moment_two + (1.0 - BETA_TWO) * gradient * gradient
    corrected = first_new / (1.0 - BETA_ONE ** STEP)
    spread = jnp.sqrt(second_new / (1.0 - BETA_TWO ** STEP)) + ADAM_EPS
    return (weight * (1.0 - step_rate * decay_rate) - step_rate * corrected / spread, first_new, second_new)

def reference(tokens, cotangent, segments, small_params, small_first, small_second, qkv_weight, qkv_first, qkv_second, out_weight, out_first, out_second, gateup_weight, gateup_first, gateup_second, down_weight, down_first, down_second):
    weights = (small_params, qkv_weight, out_weight, gateup_weight, down_weight)
    seq_total = TOKENS // SEQUENCE_LENGTH
    per_step = max((divisor for divisor in range(1, seq_total + 1) if seq_total % divisor == 0 and divisor * SEQUENCE_LENGTH <= 4096))
    step_count = seq_total // per_step
    rows_all = tokens.astype(jnp.float32).reshape(step_count, per_step * SEQUENCE_LENGTH, D)
    cots_all = cotangent.astype(jnp.float32).reshape(step_count, per_step * SEQUENCE_LENGTH, D)
    ids_all = segments.reshape(step_count, per_step * SEQUENCE_LENGTH)

    def advance(totals, inputs):
        rows_part, cots_part, ids_part = inputs
        cos_part, sin_part = jax.vmap(tables)(ids_part.reshape(per_step, SEQUENCE_LENGTH))
        cos_part = cos_part.reshape(per_step * SEQUENCE_LENGTH, HEAD_WIDTH // 2)
        sin_part = sin_part.reshape(per_step * SEQUENCE_LENGTH, HEAD_WIDTH // 2)

        def apply(params, block_in):
            return block_forward(params, block_in, cos_part, sin_part, ids_part)
        result, pullback = jax.vjp(apply, weights, rows_part)
        param_grads, in_grad = pullback(cots_part)
        totals = jax.tree.map(jnp.add, totals, param_grads)
        return (totals, (result.astype(jnp.bfloat16), in_grad))
    zero_grads = jax.tree.map(jnp.zeros_like, weights)
    totals, (outs_all, in_grads) = lax.scan(advance, zero_grads, (rows_all, cots_all, ids_all))
    block_out = outs_all.reshape(TOKENS, D)
    input_grad = in_grads.reshape(TOKENS, D)
    squares = jnp.sum(totals[0] * totals[0])
    for gradient in totals[1:]:
        squares = squares + jnp.sum(gradient * gradient)
    grad_norm = jnp.sqrt(squares)
    clip_factor = jnp.minimum(1.0, MAX_NORM / (grad_norm + 1e-06))
    small_g, qkv_g, out_g, gateup_g, down_g = [clip_factor * gradient for gradient in totals]
    new_small, new_small_first, new_small_second = adam_update(small_params, small_first, small_second, small_g, 0.5, 0.0)
    new_qkv, new_qkv_first, new_qkv_second = adam_update(qkv_weight, qkv_first, qkv_second, qkv_g, 2.0 / math.sqrt(D), WEIGHT_DECAY)
    new_out, new_out_first, new_out_second = adam_update(out_weight, out_first, out_second, out_g, 8.0 / math.sqrt(QUERY_HEADS * HEAD_WIDTH), WEIGHT_DECAY)
    new_gateup, new_gateup_first, new_gateup_second = adam_update(gateup_weight, gateup_first, gateup_second, gateup_g, 2.0 / math.sqrt(D), WEIGHT_DECAY)
    new_down, new_down_first, new_down_second = adam_update(down_weight, down_first, down_second, down_g, 3.0 / math.sqrt(FF), WEIGHT_DECAY)
    return (block_out, input_grad, grad_norm, new_small, new_small_first, new_small_second, new_qkv, new_qkv_first, new_qkv_second, new_out, new_out_first, new_out_second, new_gateup, new_gateup_first, new_gateup_second, new_down, new_down_first, new_down_second)
```

```python
import functools
import math

import jax
import jax.numpy as jnp
from jax import lax
from jax.experimental import pallas as pl
from jax.experimental.pallas import tpu as pltpu
from jax.sharding import Mesh
from jax.sharding import PartitionSpec as P

D = 1536
FF = 8960
QUERY_HEADS = 12
KEY_VALUE_HEADS = 2
HEAD_WIDTH = 128
STEP = 10

EPSILON = 1e-06
ROPE_BASE = 1000000.0
BETA_ONE = 0.9
BETA_TWO = 0.999
ADAM_EPS = 1e-08
WEIGHT_DECAY = 0.1
MAX_NORM = 1.0
NEGATIVE = -1e30

BF = jnp.bfloat16
F32 = jnp.float32
HEADS = 3
Q_COLS = HEADS * HEAD_WIDTH
QKV_COLS = Q_COLS + 2 * HEAD_WIDTH
ATT_COLS = QKV_COLS + Q_COLS
FF_LOCAL = FF // 2
FF_PAD = 4608
FF_CORE = FF_PAD // 2
FF_OWN = FF_PAD // 4
TILE = 256
VMEM_LIMIT = 60 * 2**20
CHIP = ("hi", "lo", "yy")


def dot_ab(a, b):
    return lax.dot_general(a, b, (((1,), (0,)), ((), ())), preferred_element_type=F32)


def dot_abt(a, b):
    return lax.dot_general(a, b, (((1,), (1,)), ((), ())), preferred_element_type=F32)


def dot_atb(a, b):
    return lax.dot_general(a, b, (((0,), (0,)), ((), ())), preferred_element_type=F32)


def rms_scale(inputs):
    return lax.rsqrt(jnp.mean(inputs * inputs, axis=-1, keepdims=True) + EPSILON)


def norm_backward(inputs, inv_rms, gain_vec, upstream):
    normed = inputs * inv_rms
    normed_grad = upstream * gain_vec
    input_part = inv_rms * (
        normed_grad - normed * jnp.mean(normed_grad * normed, axis=-1, keepdims=True)
    )
    return (input_part, jnp.sum(upstream * normed, axis=0))


def adam_update(weight, moment_one, moment_two, gradient, step_rate, decay_rate):
    first_new = BETA_ONE * moment_one + (1.0 - BETA_ONE) * gradient
    second_new = BETA_TWO * moment_two + (1.0 - BETA_TWO) * gradient * gradient
    corrected = first_new / (1.0 - BETA_ONE**STEP)
    spread = jnp.sqrt(second_new / (1.0 - BETA_TWO**STEP)) + ADAM_EPS
    return (
        weight * (1.0 - step_rate * decay_rate) - step_rate * corrected / spread,
        first_new,
        second_new,
    )


def swap(value, axis):
    return lax.ppermute(value, axis, [(0, 1), (1, 0)])


class Order:
    def __init__(self):
        self.mark = None

    def after(self, value):
        if self.mark is None:
            return value
        return lax.optimization_barrier((value, self.mark))[0]

    def done(self, value):
        value = self.after(value)
        self.mark = value
        return value


def chip_at(step, other_lo, other_yy):
    count = lax.axis_size("hi")
    hi = (lax.axis_index("hi") + step) % count
    return (hi * 2 + (lax.axis_index("lo") ^ other_lo)) * 2 + (lax.axis_index("yy") ^ other_yy)


def turn(value, axis, steps):
    count = lax.axis_size(axis)
    return lax.ppermute(value, axis, [(i, (i + steps) % count) for i in range(count)])


def tree_order(sign):
    steps = [(0, 0), (0, 1)] + [(k, l) for k in range(1, lax.axis_size("hi")) for l in (0, 1)]
    return jnp.stack([chip_at(sign * k, l, y) for y in (0, 1) for k, l in steps]).astype(jnp.int32)


def sum_order():
    steps = range(1, lax.axis_size("hi"))
    chips = [chip_at(k, l, y) for l in (1, 0) for ks in (steps, (0,)) for k in ks for y in (1, 0)]
    return jnp.stack(chips).astype(jnp.int32)


class ChipSum:
    def __init__(self, lo_far, lo_near, far, near):
        self.far, self.near = far, near
        self.lo_far, self.lo_near = swap(lo_far, "lo"), swap(lo_near, "lo")

    def far_yy(self, order):
        self.far = self.far.astype(F32) + order.done(self.lo_far).astype(F32)
        theirs = self.far[0::2].astype(BF)
        self.yy_far = swap(theirs, "yy")
        order.mark = theirs

    def far_hi(self, order):
        far = (self.far[1::2] + order.done(self.yy_far).astype(F32)).astype(BF)
        self.hi = [turn(far[k - 1], "hi", k) for k in range(1, lax.axis_size("hi"))]
        order.mark = far

    def near_yy(self, order):
        self.near = self.near.astype(F32) + order.done(self.lo_near).astype(F32)
        theirs = self.near[0].astype(BF)
        self.yy_near = swap(theirs, "yy")
        order.mark = theirs

    def total(self, order):
        hi = order.done(self.hi)
        total = self.near[1] + order.done(self.yy_near).astype(F32)
        for part in hi:
            total = total + part.astype(F32)
        return total


def cost(flops, bytes_accessed, transcendentals):
    part = 4096
    return pl.CostEstimate(
        flops=flops // part,
        bytes_accessed=bytes_accessed // part,
        transcendentals=transcendentals // part,
    )


ANYWHERE = pl.BlockSpec(memory_space=pl.ANY)
WHOLE = pl.BlockSpec(memory_space=pltpu.VMEM)


def turn_halves(features, cos_both, sin_both):
    return features * cos_both + pltpu.roll(features, HEAD_WIDTH // 2, 1) * sin_both


def scores_t(keys, queries, key_place, place, start):
    scores = dot_abt(keys, queries) * (1.0 / math.sqrt(HEAD_WIDTH))
    return jnp.where((key_place <= place) & (key_place >= start), scores, NEGATIVE)


def attention_kernel(
    parts,
    rows,
    chips_ref,
    near_ref,
    far_ref,
    bias_ref,
    cos_ref,
    sin_ref,
    key_place_ref,
    place_ref,
    start_ref,
    *refs,
):
    shards, refs = refs[:parts], refs[parts:]
    qkv_ref, o_ref, lse_ref, *out_refs, weight_ref, weights, sems, out_sem = refs
    half = near_ref.shape[0]
    copies = [
        pltpu.make_async_copy(
            shards[i],
            weights.at[pl.ds(pl.multiple_of(chips_ref[i] * rows, rows), rows), :],
            sems.at[i],
        )
        for i in range(parts)
    ]
    for copy in copies:
        copy.start()
    for copy in copies:
        copy.wait()
    save = pltpu.make_async_copy(weights, weight_ref, out_sem)
    save.start()
    for side, ref in enumerate((near_ref, far_ref)):
        at = slice(side * half, (side + 1) * half)
        projected = dot_ab(ref[...], weights[:, :QKV_COLS]) + bias_ref[...]
        cos_both, sin_both = cos_ref[at, :], sin_ref[at, :]
        for j in range(HEADS + 1):
            cols = slice(j * HEAD_WIDTH, (j + 1) * HEAD_WIDTH)
            qkv_ref[at, cols] = turn_halves(projected[:, cols], cos_both, sin_both).astype(BF)
        cols = slice(Q_COLS + HEAD_WIDTH, QKV_COLS)
        qkv_ref[at, cols] = projected[:, cols].astype(BF)
    keys = qkv_ref[:, Q_COLS : Q_COLS + HEAD_WIDTH]
    values_t = qkv_ref[:, Q_COLS + HEAD_WIDTH : QKV_COLS].T
    lse_ref[...] = jnp.zeros_like(lse_ref)
    key_place = key_place_ref[...]
    for at in range(0, 2 * half, TILE):
        block = slice(at, at + TILE)
        place, start = place_ref[:, block], start_ref[:, block]
        for h in range(HEADS):
            cols = slice(h * HEAD_WIDTH, (h + 1) * HEAD_WIDTH)
            scores = scores_t(keys, qkv_ref[block, cols], key_place, place, start)
            top = jnp.max(scores, axis=0, keepdims=True)
            weights_exp = jnp.exp(scores - top)
            total = jnp.sum(weights_exp, axis=0, keepdims=True)
            lse_ref[h : h + 1, block] = top + jnp.log(total)
            prob = (weights_exp * (1.0 / total)).astype(BF)
            o_ref[block, cols] = dot_ab(values_t, prob).astype(BF).T
    for side in range(2):
        part = dot_abt(o_ref[side * half : (side + 1) * half, :], weights[:, QKV_COLS:])
        out_refs[2 * side][...] = part[: half // 2].astype(BF)
        out_refs[2 * side + 1][...] = part[half // 2 :].astype(BF)
    save.wait()


def attention(chips, rows_pair, bias, tables, shards):
    near, far = rows_pair
    half = near.shape[0]
    length = 2 * half
    parts = len(shards)
    rows = shards[0].shape[0]
    return pl.pallas_call(
        functools.partial(attention_kernel, parts, rows),
        grid_spec=pltpu.PrefetchScalarGridSpec(
            num_scalar_prefetch=1,
            grid=(),
            in_specs=[WHOLE] * 8 + [ANYWHERE] * parts,
            out_specs=[WHOLE] * 7 + [ANYWHERE],
            scratch_shapes=[
                pltpu.VMEM((D, ATT_COLS), BF),
                pltpu.SemaphoreType.DMA((parts,)),
                pltpu.SemaphoreType.DMA,
            ],
        ),
        out_shape=[
            jax.ShapeDtypeStruct((length, QKV_COLS), BF),
            jax.ShapeDtypeStruct((length, Q_COLS), BF),
            jax.ShapeDtypeStruct((8, length), F32),
            *[jax.ShapeDtypeStruct((half // 2, D), BF)] * 4,
            jax.ShapeDtypeStruct((D, ATT_COLS), BF),
        ],
        compiler_params=pltpu.CompilerParams(vmem_limit_bytes=VMEM_LIMIT),
        cost_estimate=cost(
            flops=2 * length * D * ATT_COLS + 4 * HEADS * length * length * HEAD_WIDTH,
            bytes_accessed=16 * 2**20,
            transcendentals=HEADS * length * length,
        ),
        name="attention",
    )(chips, near, far, bias, *tables, *shards)


def attention_back_kernel(
    count,
    rows,
    chips_ref,
    near_ref,
    far_ref,
    n1_near_ref,
    n1_far_ref,
    qkv_ref,
    o_ref,
    lse_ref,
    weight_ref,
    cos_ref,
    sin_ref,
    key_place_ref,
    place_ref,
    start_ref,
    dqkv_ref,
    bias_ref,
    *refs,
):
    *out_refs, mixed, grads = refs
    half = near_ref.shape[0]
    length = 2 * half
    scale = 1.0 / math.sqrt(HEAD_WIDTH)
    for side, ref in enumerate((near_ref, far_ref)):
        mixed[side * half : (side + 1) * half, :] = dot_ab(
            ref[...], weight_ref[:, QKV_COLS:]
        ).astype(BF)
    key_cols = slice(Q_COLS, Q_COLS + HEAD_WIDTH)
    value_cols = slice(Q_COLS + HEAD_WIDTH, QKV_COLS)
    keys, values = qkv_ref[:, key_cols], qkv_ref[:, value_cols]
    keys_t = keys.T
    key_place = key_place_ref[...]
    keys_grad = jnp.zeros((length, HEAD_WIDTH), F32)
    values_grad = jnp.zeros((length, HEAD_WIDTH), F32)
    for at in range(0, length, TILE):
        block = slice(at, at + TILE)
        place, start = place_ref[:, block], start_ref[:, block]
        for h in range(HEADS):
            cols = slice(h * HEAD_WIDTH, (h + 1) * HEAD_WIDTH)
            queries, up = qkv_ref[block, cols], mixed[block, cols]
            scores = scores_t(keys, queries, key_place, place, start)
            prob = jnp.exp(scores - lse_ref[h : h + 1, block])
            prob_grad = dot_abt(values, up)
            inner = jnp.sum(prob * prob_grad, axis=0, keepdims=True)
            score_grad = (prob * (prob_grad - inner)).astype(BF)
            values_grad += dot_ab(prob.astype(BF), up)
            keys_grad += dot_ab(score_grad, queries)
            query_grad = dot_ab(keys_t, score_grad).T * scale
            dqkv_ref[block, cols] = turn_halves(
                query_grad, cos_ref[block, :], -sin_ref[block, :]
            ).astype(BF)
    dqkv_ref[:, key_cols] = turn_halves(keys_grad * scale, cos_ref[...], -sin_ref[...]).astype(BF)
    dqkv_ref[:, value_cols] = values_grad.astype(BF)
    bias_ref[...] = jnp.sum(dqkv_ref[...].astype(F32), axis=0, keepdims=True)
    for cols, pair, right_ref in (
        (slice(0, QKV_COLS), (n1_near_ref, n1_far_ref), dqkv_ref),
        (slice(QKV_COLS, ATT_COLS), (near_ref, far_ref), o_ref),
    ):
        grads[:, :, cols] = (
            dot_ab(pair[0][...].T, right_ref[:half, :]) + dot_ab(pair[1][...].T, right_ref[half:, :])
        ).astype(BF).reshape(4 * count, rows, -1)
    at = 0
    for ref in out_refs:
        for k in range(ref.shape[0]):
            ref[k] = grads[chips_ref[at]]
            at += 1


def attention_back(chips, da_pair, n1_pair, qkv, o, lse, weight, tables):
    length = qkv.shape[0]
    count = chips.shape[0] // 4
    rows = D // (4 * count)
    blocks = [
        jax.ShapeDtypeStruct((2 * k, rows, ATT_COLS), BF) for k in (count - 1, 1, count - 1, 1)
    ]
    return pl.pallas_call(
        functools.partial(attention_back_kernel, count, rows),
        grid_spec=pltpu.PrefetchScalarGridSpec(
            num_scalar_prefetch=1,
            grid=(),
            in_specs=[WHOLE] * 13,
            out_specs=[WHOLE] * 6,
            scratch_shapes=[
                pltpu.VMEM((length, Q_COLS), BF),
                pltpu.VMEM((4 * count, rows, ATT_COLS), BF),
            ],
        ),
        out_shape=[
            jax.ShapeDtypeStruct((length, QKV_COLS), BF),
            jax.ShapeDtypeStruct((1, QKV_COLS), F32),
            *blocks,
        ],
        compiler_params=pltpu.CompilerParams(vmem_limit_bytes=VMEM_LIMIT),
        cost_estimate=cost(
            flops=2 * length * D * 2 * ATT_COLS + 10 * HEADS * length * length * HEAD_WIDTH,
            bytes_accessed=24 * 2**20,
            transcendentals=HEADS * length * length,
        ),
        name="attention_back",
    )(chips, *da_pair, *n1_pair, qkv, o, lse, weight, *tables)


def feed_forward_kernel(whole, split, rows, chips_ref, *refs):
    n2_refs, dy_refs, refs = refs[:2], refs[2:4], refs[4:]
    pieces, refs = refs[: whole + 2 * split], refs[whole + 2 * split :]
    keep_ref, send_ref, u_ref, dgate_ref, dup_ref, *refs = refs
    n2_t_ref, dy_t_ref, down_ref, gu_w, d_w, n2_s, dy_s, sems, out_sem = refs
    step = pl.program_id(0)
    steps = pl.num_programs(0)

    def copies():
        for i in range(whole + split):
            at = pl.ds(pl.multiple_of(chips_ref[i] * rows, rows), rows)
            for j in range(3):
                if i < whole:
                    here = pieces[i].at[j]
                elif j < 2:
                    here = pieces[i].at[j]
                else:
                    here = pieces[i + split]
                if j < 2:
                    there = gu_w.at[at, pl.ds(j * FF_OWN, FF_OWN)]
                else:
                    there = d_w.at[at, :]
                yield pltpu.make_async_copy(here, there, sems.at[i, j])

    save = pltpu.make_async_copy(d_w, down_ref, out_sem)

    @pl.when(step == 0)
    def _():
        for copy in copies():
            copy.start()
        for copy in copies():
            copy.wait()
        save.start()

    for j in range(2):

        @pl.when(step // 4 == j)
        def _(j=j):
            n2_s[...] = n2_refs[j][...]
            dy_s[...] = dy_refs[j][...]

    n2, dy = n2_s[...], dy_s[...]
    n2_t_ref[...] = n2.T
    dy_t_ref[...] = dy.T
    gate_up = dot_ab(n2, gu_w[...])
    du = dot_ab(dy, d_w[...])
    gate, up = gate_up[:, :FF_OWN], gate_up[:, FF_OWN:]
    sig = jax.nn.sigmoid(gate)
    silu = gate * sig
    u_ref[...] = (silu * up).astype(BF)
    dup = (du * silu).astype(BF)
    dgate = (du * up * sig * (1.0 + gate * (1.0 - sig))).astype(BF)
    dup_ref[...] = dup
    dgate_ref[...] = dgate
    dn2 = dot_abt(jnp.concatenate([dgate, dup], axis=1), gu_w[...]).astype(BF)

    @pl.when(step < steps // 2)
    def _():
        keep_ref[...] = dn2

    @pl.when(step >= steps // 2)
    def _():
        send_ref[...] = dn2

    @pl.when(step == steps - 1)
    def _():
        save.wait()


def feed_forward(chips, n2, dy, whole, split):
    rows = whole[0].shape[1]
    one = n2[0].shape[0] // 4
    length = 8 * one
    tile = lambda width: pl.BlockSpec((one, width), lambda i, c: (i, 0))
    turned = pl.BlockSpec((D, one), lambda i, c: (0, i))
    taken = [
        pl.BlockSpec((one, D), lambda i, c: (jnp.minimum(i, 3), 0)),
        pl.BlockSpec((one, D), lambda i, c: (jnp.maximum(i - 4, 0), 0)),
    ]
    parts = len(whole) + len(split)
    return pl.pallas_call(
        functools.partial(feed_forward_kernel, len(whole), len(split), rows),
        grid_spec=pltpu.PrefetchScalarGridSpec(
            num_scalar_prefetch=1,
            grid=(8,),
            in_specs=taken * 2 + [ANYWHERE] * (len(whole) + 2 * len(split)),
            out_specs=taken + [tile(FF_OWN)] * 3 + [turned, turned, ANYWHERE],
            scratch_shapes=[
                pltpu.VMEM((D, 2 * FF_OWN), BF),
                pltpu.VMEM((D, FF_OWN), BF),
                pltpu.VMEM((one, D), BF),
                pltpu.VMEM((one, D), BF),
                pltpu.SemaphoreType.DMA((parts, 3)),
                pltpu.SemaphoreType.DMA,
            ],
        ),
        out_shape=[jax.ShapeDtypeStruct((length // 2, D), BF)] * 2
        + [jax.ShapeDtypeStruct((length, FF_OWN), BF)] * 3
        + [jax.ShapeDtypeStruct((D, length), BF)] * 2
        + [jax.ShapeDtypeStruct((D, FF_OWN), BF)],
        compiler_params=pltpu.CompilerParams(vmem_limit_bytes=VMEM_LIMIT),
        cost_estimate=cost(
            flops=2 * 5 * length * D * FF_OWN,
            bytes_accessed=60 * 2**20,
            transcendentals=length * FF_OWN,
        ),
        name="feed_forward",
    )(chips, *n2, *dy, *whole, *[gu for gu, _ in split], *[d for _, d in split])


def weight_grad_kernel(rows, place_ref, left_ref, right_ref, *refs):
    out_refs, total = refs[:4], refs[4]
    width = right_ref.shape[1]
    for at in range(0, width, 256):
        to = min(at + 256, width)
        total[:, :, at:to] = dot_ab(left_ref[...], right_ref[:, at:to]).reshape(
            4, rows, to - at
        )
    lo, yy = place_ref[1], place_ref[2]
    for k in range(2):
        row = jnp.where(lo == 0, k, 1 - k) * 2
        out_refs[k][0] = total[row + yy].astype(BF)
        out_refs[2 + k][0] = total[row + 1 - yy].astype(BF)


def weight_grad(place, left, right):
    count = lax.axis_size("hi")
    length, width = right.shape
    rows = left.shape[0] // (4 * count)
    block = pl.BlockSpec((1, rows, width), lambda i, p: (i, 0, 0))
    out = jax.ShapeDtypeStruct((count, rows, width), BF)
    return pl.pallas_call(
        functools.partial(weight_grad_kernel, rows),
        grid_spec=pltpu.PrefetchScalarGridSpec(
            num_scalar_prefetch=1,
            grid=(count,),
            in_specs=[
                pl.BlockSpec((4 * rows, length), lambda i, p: (lax.rem(i + p[0], count), 0)),
                pl.BlockSpec((length, width), lambda i, p: (0, 0)),
            ],
            out_specs=[block] * 4,
            scratch_shapes=[pltpu.VMEM((4, rows, width), F32)],
        ),
        out_shape=[out] * 4,
        compiler_params=pltpu.CompilerParams(vmem_limit_bytes=VMEM_LIMIT),
        cost_estimate=cost(
            flops=2 * length * D * width, bytes_accessed=16 * 2**20, transcendentals=0
        ),
        name="weight_grad",
    )(place, left, right)


def down_kernel(left_ref, right_ref, keep_ref, send_ref):
    step = pl.program_id(0)
    product = dot_abt(left_ref[...], right_ref[...]).astype(BF)

    @pl.when(step < pl.num_programs(0) // 2)
    def _():
        keep_ref[...] = product

    @pl.when(step >= pl.num_programs(0) // 2)
    def _():
        send_ref[...] = product


def down(left, right):
    length, width = left.shape
    one = length // 8
    return pl.pallas_call(
        down_kernel,
        grid=(8,),
        in_specs=[
            pl.BlockSpec((one, width), lambda i: (i, 0)),
            pl.BlockSpec((D, width), lambda i: (0, 0)),
        ],
        out_specs=[
            pl.BlockSpec((one, D), lambda i: (jnp.minimum(i, 3), 0)),
            pl.BlockSpec((one, D), lambda i: (jnp.maximum(i - 4, 0), 0)),
        ],
        out_shape=[jax.ShapeDtypeStruct((length // 2, D), BF)] * 2,
        compiler_params=pltpu.CompilerParams(vmem_limit_bytes=VMEM_LIMIT),
        cost_estimate=cost(
            flops=2 * length * D * width, bytes_accessed=14 * 2**20, transcendentals=0
        ),
        name="down",
    )(left, right)


class EightSum:
    def __init__(self, keep, send):
        self.keep = keep
        self.one = keep.shape[0] // 4
        self.half = self.one // 2
        self.core = swap(send, "core")

    def part(self, begin, rows):
        at = slice(begin, begin + rows)
        return self.keep[at].astype(F32) + self.core[at].astype(F32)

    def second(self, order):
        self.core = order.done(self.core)
        one, half = self.one, self.half
        both_lo = self.part(3 * one, half).astype(BF)
        both_x = self.part(3 * one + half, half).astype(BF)
        self.to_lo, self.to_x = swap(both_lo, "tensor"), swap(both_x, "lo")

    def third(self, order):
        one, half = self.one, self.half
        to_lo, to_x = order.done((self.to_lo, self.to_x))
        by_x = [self.part(one, half), self.part(one + half, half) + to_x.astype(F32)]
        by_lo = [self.part(2 * one, half) + to_lo.astype(F32), self.part(2 * one + half, half)]
        self.by_x = swap(jnp.concatenate(by_x, axis=0).astype(BF), "tensor")
        self.by_lo = swap(jnp.concatenate(by_lo, axis=0).astype(BF), "lo")

    def total(self, order):
        by_x, by_lo = order.done((self.by_x, self.by_lo))
        return self.part(0, self.one) + by_x.astype(F32) + by_lo.astype(F32)


class FourSum:
    def __init__(self, own, by_x, core_own, core_by_x):
        self.own, self.by_x = own, by_x
        self.core_by_x, self.core_own = swap(core_by_x, "core"), swap(core_own, "core")

    def second(self, order):
        core_by_x = order.done(self.core_by_x)
        by_x = (self.by_x.astype(F32) + core_by_x.astype(F32)).astype(BF)
        self.x = swap(by_x, "tensor")
        order.mark = by_x
        self.core_own = order.done(self.core_own)

    def total(self, order):
        x = order.done(self.x)
        return self.own.astype(F32) + self.core_own.astype(F32) + x.astype(F32)


class GradSum:
    def __init__(self, keep, send):
        self.keep = keep
        self.other = swap(send, "yy")

    def across(self, order):
        self.other = order.done(self.other)
        self.far = [
            turn((self.keep[k].astype(F32) + self.other[k].astype(F32)).astype(BF), "hi", k)
            for k in range(1, lax.axis_size("hi"))
        ]

    def total(self, order):
        self.far = order.done(self.far)
        total = self.keep[0].astype(F32) + self.other[0].astype(F32)
        for far in self.far:
            total = total + far.astype(F32)
        return total


def body(
    tokens,
    cotangent,
    segments,
    small_params,
    small_first,
    small_second,
    qkv_weight,
    qkv_first,
    qkv_second,
    out_weight,
    out_first,
    out_second,
    gateup_weight,
    gateup_first,
    gateup_second,
    down_weight,
    down_first,
    down_second,
):
    hi_count = lax.axis_size("hi")
    hi, lo, yy = lax.axis_index("hi"), lax.axis_index("lo"), lax.axis_index("yy")
    core = lax.axis_index("core")
    place_x = lax.axis_index("tensor")
    own_rows = tokens.shape[0]
    shard_rows = qkv_weight.shape[0]
    gain_one = small_params[:D]
    gain_two = small_params[D : 2 * D]
    bias_all = small_params[2 * D :]
    q_at = place_x * (bias_all.shape[0] // 2) + core * Q_COLS
    kv_at = place_x * (bias_all.shape[0] // 2) + 2 * Q_COLS
    bias_local = jnp.concatenate(
        [
            lax.dynamic_slice_in_dim(bias_all, q_at, Q_COLS),
            lax.dynamic_slice_in_dim(bias_all, kv_at, 2 * HEAD_WIDTH),
        ]
    )

    order = Order()
    steps = range(1, hi_count)

    def both_cores(mine, other, axis):
        return jnp.where(
            core == 0,
            jnp.concatenate([mine, other], axis=axis),
            jnp.concatenate([other, mine], axis=axis),
        )

    other_ids = swap(segments, "core")
    qkv_low = qkv_weight.astype(BF)
    out_low = out_weight.astype(BF).T

    def attention_pack(which):
        return jnp.concatenate(
            [
                lax.dynamic_slice_in_dim(qkv_low, which * Q_COLS, Q_COLS, 1),
                qkv_low[:, 2 * Q_COLS :],
                lax.dynamic_slice_in_dim(out_low, which * Q_COLS, Q_COLS, 1),
            ],
            axis=1,
        )

    att_theirs = attention_pack(1 - core)
    att_core = swap(att_theirs, "core")
    order.mark = att_theirs
    rows_in = order.after(tokens).astype(F32)
    scale_one = rms_scale(rows_in)
    n1 = (rows_in * scale_one * gain_one).astype(BF)
    n1_x = swap(n1, "tensor")
    order.mark = n1
    att_shard = both_cores(attention_pack(core), order.done(att_core), 0)
    order.mark = att_shard
    other_ids = order.done(other_ids)
    att_hi = [turn(att_shard, "hi", k) for k in steps]
    att_yy = swap(att_shard, "yy")
    att_lo = swap(att_shard, "lo")

    gateup_in, down_in = order.after((gateup_weight, down_weight))
    ff_low = jnp.pad(
        jnp.concatenate([gateup_in.astype(BF), down_in.astype(BF).T[None]], axis=0),
        ((0, 0), (0, 0), (0, FF_PAD - FF_LOCAL)),
    )
    ff_mine = lax.dynamic_slice_in_dim(ff_low, core * FF_CORE, FF_CORE, 2)
    ff_theirs = lax.dynamic_slice_in_dim(ff_low, (1 - core) * FF_CORE, FF_CORE, 2)
    ff_core = swap(ff_theirs, "core")
    order.mark = ff_theirs
    ff_shard = both_cores(ff_mine, order.done(ff_core), 1)
    ff_own = lax.dynamic_slice_in_dim(ff_shard, lo * FF_OWN, FF_OWN, 2)
    ff_theirs = lax.dynamic_slice_in_dim(ff_shard, (1 - lo) * FF_OWN, FF_OWN, 2)
    order.mark = ff_theirs
    ff_hi = [turn(ff_own, "hi", k) for k in steps]
    ff_lo = swap(ff_theirs, "lo")
    att_lo = order.done(att_lo)
    att_lo_yy = swap(att_lo, "yy")

    ids = both_cores(segments, other_ids, 0)
    length = ids.shape[0]
    places = jnp.arange(length, dtype=jnp.int32)
    earlier = jnp.concatenate([ids[:1], ids[:-1]])
    starts = lax.cummax(jnp.where((places == 0) | (ids != earlier), places, 0), axis=0)

    def own_first(values):
        parts = values.reshape(4, own_rows)
        me = core * 2 + place_x
        return jnp.concatenate(
            [lax.dynamic_index_in_dim(parts, me ^ k, 0, keepdims=False) for k in range(4)]
        )

    starts = own_first(starts)
    places = own_first(places)
    positions = (places - starts).astype(F32)
    frequency = 1.0 / ROPE_BASE ** (jnp.arange(0, HEAD_WIDTH, 2, dtype=F32) / HEAD_WIDTH)
    angles = positions[:, None] * frequency[None, :]
    cos_part, sin_part = jnp.cos(angles), jnp.sin(angles)
    tables = (
        jnp.concatenate([cos_part, cos_part], axis=1),
        jnp.concatenate([-sin_part, sin_part], axis=1),
        places[:, None],
        places[None, :],
        starts[None, :],
    )
    tables = order.done(tables)

    att_yy = order.done(att_yy)
    att_hi = order.done(att_hi)
    att_hi_lo = [swap(part, "lo") for part in att_hi]
    att_hi_yy = [swap(part, "yy") for part in att_hi]
    n1_x = order.done(n1_x)
    n1_near = jnp.concatenate([n1, n1_x], axis=0)
    n1_far = swap(n1_near, "core")
    order.mark = n1_near
    cot_x = swap(order.after(cotangent), "tensor")
    att_lo_yy = order.done(att_lo_yy)
    ff_yy = swap(order.after(ff_own), "yy")
    att_hi_lo = order.done(att_hi_lo)
    att_hi_lo_yy = [swap(part, "yy") for part in att_hi_lo]
    n1_far = order.done(n1_far)
    att_hi_yy = order.done(att_hi_yy)
    cot_lo = swap(order.after(cotangent), "lo")
    att_hi_lo_yy = order.done(att_hi_lo_yy)

    near_parts = [att_shard, att_lo]
    yy_parts = [att_yy, att_lo_yy]
    for k in range(hi_count - 1):
        near_parts += [att_hi[k], att_hi_lo[k]]
        yy_parts += [att_hi_yy[k], att_hi_lo_yy[k]]
    att_parts = near_parts + yy_parts
    n1_pair = order.after((n1_near, n1_far))
    qkv, attn_rows, lse, *out_parts, att_weight = attention(
        tree_order(-1), n1_pair, bias_local[None], tables, att_parts
    )
    order.mark = lse

    out = FourSum(*out_parts)
    half = own_rows // 2
    ff_yy = order.done(ff_yy)
    ff_lo = order.done(ff_lo)
    ff_lo_yy = swap(ff_lo, "yy")
    ff_hi = order.done(ff_hi)
    ff_lo_hi_gu = [turn(order.after(ff_lo[:2]), "hi", k) for k in steps]
    out.second(order)
    cot_x, cot_lo = order.done((cot_x, cot_lo))
    cot_both = swap(cot_lo[:half], "tensor"), swap(cot_x[half:], "lo")
    ff_lo_yy = order.done(ff_lo_yy)
    ff_hi_yy = [swap(order.after(part), "yy") for part in ff_hi]
    residual = rows_in + out.total(order)
    scale_two = rms_scale(residual)
    n2 = (residual * scale_two * gain_two).astype(BF)
    n2_x, n2_lo = swap(n2, "tensor"), swap(n2, "lo")
    order.mark = n2
    cot_both = order.done(cot_both)
    cot_near = jnp.concatenate([cotangent, cot_x, cot_lo, *cot_both], axis=0)
    order.mark = cot_near
    ff_lo_hi_gu = order.done(ff_lo_hi_gu)
    ff_lo_hi_d = [turn(order.after(ff_lo[2]), "hi", k) for k in steps]
    n2_x, n2_lo = order.done((n2_x, n2_lo))
    n2_both = swap(n2_lo[:half], "tensor"), swap(n2_x[half:], "lo")
    ff_hi_yy = order.done(ff_hi_yy)
    ff_lo_hi_yy_gu = [swap(order.after(part), "yy") for part in ff_lo_hi_gu]
    cot_far = swap(order.after(cot_near), "core")
    n2_both = order.done(n2_both)
    n2_near = jnp.concatenate([n2, n2_x, n2_lo, *n2_both], axis=0)
    n2_far = swap(n2_near, "core")
    order.mark = n2_near
    ff_lo_hi_d = order.done(ff_lo_hi_d)
    ff_lo_hi_yy_d = [swap(part, "yy") for part in ff_lo_hi_d]
    cot_far = order.done(cot_far)
    n2_far = order.done(n2_far)
    ff_lo_hi_yy_gu = order.done(ff_lo_hi_yy_gu)
    ff_lo_hi_yy_d = order.done(ff_lo_hi_yy_d)

    whole = [ff_own, ff_lo, ff_yy, ff_lo_yy, *ff_hi, *ff_hi_yy]
    split = [*zip(ff_lo_hi_gu, ff_lo_hi_d), *zip(ff_lo_hi_yy_gu, ff_lo_hi_yy_d)]
    ff_chips = [chip_at(0, l, y) for y in (0, 1) for l in (0, 1)]
    ff_chips += [chip_at(-k, l, y) for l in (0, 1) for y in (0, 1) for k in steps]
    keep, send, hidden, gate_grad, up_grad, n2_t, cot_t, w_down = feed_forward(
        jnp.stack(ff_chips).astype(jnp.int32),
        order.after((n2_near, n2_far)),
        (cot_near, cot_far),
        whole,
        split,
    )
    order.mark = w_down

    place = jnp.stack([hi, lo, yy]).astype(jnp.int32)

    def grad_parts(left, right, send_now=True):
        keep_own, keep_lo, send_own, send_lo = weight_grad(place, order.after(left), right)
        order.mark = keep_own
        first = GradSum(keep_lo, send_lo) if send_now else (keep_lo, send_lo)
        return first, (keep_own, send_own)

    ff_squares = 0.0
    rows_of = lambda value, which, axis: lax.dynamic_slice_in_dim(
        value, which * shard_rows, shard_rows, axis
    )

    def this_side(lo_sum):
        nonlocal ff_squares
        total = lo_sum.total(order)
        ff_squares = ff_squares + jnp.sum(total * total)
        low = total.astype(BF)
        order.mark = low
        return low, swap(low, "lo")

    def own_rows_of(low, other):
        other = order.done(other)
        cols = jnp.where(
            lo == 0,
            jnp.concatenate([low, other], axis=1),
            jnp.concatenate([other, low], axis=1),
        )
        theirs = rows_of(cols, 1 - core, 0)
        order.mark = theirs
        return rows_of(cols, core, 0), swap(theirs, "core")

    def own_sum(own):
        nonlocal ff_squares
        total = own.total(order)
        ff_squares = ff_squares + jnp.sum(total * total)
        order.mark = total.astype(BF)
        return order.mark

    dn2 = EightSum(keep, send)
    d_lo, d_own = grad_parts(cot_t, hidden)
    d_own = GradSum(*d_own)
    dn2.second(order)
    g_lo, g_own = grad_parts(n2_t, gate_grad)
    dn2.third(order)
    u_lo, u_own = grad_parts(n2_t, up_grad, False)
    d_lo.across(order)
    norm_two_in, gain_two_grad = norm_backward(residual, scale_two, gain_two, dn2.total(order))
    residual_grad = cotangent.astype(F32) + norm_two_in
    da = residual_grad.astype(BF)
    da_x = swap(da, "tensor")
    order.mark = da
    keep, send = down(*order.after((hidden, w_down)))
    order.mark = keep
    da_x = order.done(da_x)
    da_near = jnp.concatenate([da, da_x], axis=0)
    da_far = swap(da_near, "core")
    order.mark = da_near
    d_own.across(order)
    g_own = GradSum(g_own[0], order.after(g_own[1]))
    g_lo.across(order)
    u_lo = GradSum(u_lo[0], order.after(u_lo[1]))
    d_way = this_side(d_lo)[1]
    da_far = order.done(da_far)

    projected_grad, bias_grad, *att_grads = attention_back(
        sum_order(), order.after((da_near, da_far)), n1_pair, qkv, attn_rows, lse, att_weight, tables
    )
    order.mark = bias_grad
    bias_grad = bias_grad[0]
    att = ChipSum(*att_grads)
    d_low = own_sum(d_own)
    g_own.across(order)
    g_way = this_side(g_lo)[1]
    u_lo.across(order)
    dn1_parts = [None] * 4
    for k in (3, 2, 1, 0):
        part = order.after(projected_grad)[k * own_rows : (k + 1) * own_rows]
        dn1_parts[k] = dot_abt(part, att_weight[:, :QKV_COLS]).astype(BF)
        order.mark = dn1_parts[k]
    dn1 = FourSum(*dn1_parts)
    dn1.second(order)
    att.far_yy(order)
    u_own = GradSum(u_own[0], order.after(u_own[1]))
    d_rows = own_rows_of(d_low, d_way)
    g_low = own_sum(g_own)
    att.far_hi(order)
    branch = EightSum(keep, order.after(send))
    norm_one_in, gain_one_grad = norm_backward(rows_in, scale_one, gain_one, dn1.total(order))
    input_grad = residual_grad + norm_one_in
    order.mark = gain_one_grad
    att.near_yy(order)
    u_way = this_side(u_lo)[1]
    branch.second(order)
    u_own.across(order)
    g_rows = own_rows_of(g_low, g_way)
    att_sum = att.total(order)
    att_low = att_sum.astype(BF)
    other_att = swap(rows_of(att_low, 1 - core, 0), "core")
    order.mark = att_low
    branch.third(order)
    u_low = own_sum(u_own)
    other_att = order.done(other_att)

    own_att = rows_of(att_low, core, 0)
    first_att = jnp.where(core == 0, own_att, other_att).astype(F32)
    second_att = jnp.where(core == 0, other_att, own_att).astype(F32)
    kv_sum = first_att[:, Q_COLS:QKV_COLS] + second_att[:, Q_COLS:QKV_COLS]
    qkv_owned = jnp.concatenate([first_att[:, :Q_COLS], second_att[:, :Q_COLS], kv_sum], axis=1)
    out_owned = jnp.concatenate([first_att[:, QKV_COLS:], second_att[:, QKV_COLS:]], axis=1).T
    owned_squares = (
        jnp.sum(qkv_owned * qkv_owned) + jnp.sum(out_owned * out_owned) + ff_squares
    )
    bias_slots = lax.dynamic_update_slice_in_dim(
        jnp.zeros_like(bias_all), bias_grad[:Q_COLS], q_at, 0
    )
    bias_slots = lax.dynamic_update_slice_in_dim(bias_slots, bias_grad[Q_COLS:], kv_at, 0)
    summed = jnp.concatenate(
        [gain_one_grad, gain_two_grad, bias_slots, jnp.full((128,), owned_squares)]
    )
    first = summed + order.done(swap(summed, "core"))
    order.mark = first
    u_rows = own_rows_of(u_low, u_way)
    summed = first + order.done(swap(first, "tensor"))
    summed = summed + order.done(swap(summed, "yy"))
    block_out = (residual + branch.total(order)).astype(BF)
    summed = summed + order.done(swap(summed, "lo"))
    step = 1
    while step < hi_count:
        moved = lax.ppermute(summed, "hi", [(i, i ^ step) for i in range(hi_count)])
        summed = summed + order.done(moved)
        step *= 2

    def owned(rows):
        mine, other = rows
        return both_cores(mine, other, 1)[:, :FF_LOCAL].astype(F32)

    gateup_owned = jnp.stack([owned(g_rows), owned(u_rows)])
    down_owned = owned(d_rows).T
    small_grad = summed[:-128]
    squares = summed[-1] + jnp.sum(small_grad * small_grad)
    grad_norm = jnp.sqrt(squares)
    clip_factor = jnp.minimum(1.0, MAX_NORM / (grad_norm + 1e-06))
    new_small, new_small_first, new_small_second = adam_update(
        small_params, small_first, small_second, clip_factor * small_grad, 0.5, 0.0
    )
    new_qkv, new_qkv_first, new_qkv_second = adam_update(
        qkv_weight, qkv_first, qkv_second, clip_factor * qkv_owned, 2.0 / math.sqrt(D), WEIGHT_DECAY
    )
    new_out, new_out_first, new_out_second = adam_update(
        out_weight,
        out_first,
        out_second,
        clip_factor * out_owned,
        8.0 / math.sqrt(QUERY_HEADS * HEAD_WIDTH),
        WEIGHT_DECAY,
    )
    new_gateup, new_gateup_first, new_gateup_second = adam_update(
        gateup_weight,
        gateup_first,
        gateup_second,
        clip_factor * gateup_owned,
        2.0 / math.sqrt(D),
        WEIGHT_DECAY,
    )
    new_down, new_down_first, new_down_second = adam_update(
        down_weight,
        down_first,
        down_second,
        clip_factor * down_owned,
        3.0 / math.sqrt(FF),
        WEIGHT_DECAY,
    )
    return (
        block_out,
        input_grad,
        grad_norm,
        new_small,
        new_small_first,
        new_small_second,
        new_qkv,
        new_qkv_first,
        new_qkv_second,
        new_out,
        new_out_first,
        new_out_second,
        new_gateup,
        new_gateup_first,
        new_gateup_second,
        new_down,
        new_down_first,
        new_down_second,
    )


def solution(mesh):
    count = mesh.shape["dp"]
    fine = Mesh(
        mesh.devices.reshape(count // 8, 2, 2, 2, mesh.shape["tensor"]),
        CHIP + ("core", "tensor"),
    )
    dp = CHIP + ("core",)
    rows = P(dp + ("tensor",), None)
    by_rows = P(dp, "tensor")
    by_cols = P("tensor", dp)
    stacked = P(None, dp, "tensor")
    weights = (by_rows,) * 3 + (by_cols,) * 3 + (stacked,) * 3 + (by_cols,) * 3
    return jax.shard_map(
        body,
        mesh=fine,
        in_specs=(rows, rows, P(dp), P(), P(), P()) + weights,
        out_specs=(rows, rows, P(), P(), P(), P()) + weights,
        check_vma=False,
    )
```

```python
import functools
import math

import jax
import jax.numpy as jnp
import numpy as np
from jax import lax
from jax.experimental import pallas as pl
from jax.experimental.pallas import tpu as pltpu
from jax.sharding import Mesh
from jax.sharding import PartitionSpec as P

D = 1536
FF = 8960
QUERY_HEADS = 12
KEY_VALUE_HEADS = 2
HEAD_WIDTH = 128
STEP = 10

EPSILON = 1e-06
ROPE_BASE = 1000000.0
BETA_ONE = 0.9
BETA_TWO = 0.999
ADAM_EPS = 1e-08
WEIGHT_DECAY = 0.1
MAX_NORM = 1.0
NEGATIVE = -1e30

BF = jnp.bfloat16
F32 = jnp.float32
HEADS = 3
Q_COLS = HEADS * HEAD_WIDTH
QKV_COLS = Q_COLS + 2 * HEAD_WIDTH
ATT_COLS = QKV_COLS + Q_COLS
FF_LOCAL = FF // 2
FF_PAD = 4608
FF_CORE = FF_PAD // 2
FF_OWN = FF_PAD // 4
TILE = 256
VMEM_LIMIT = 60 * 2**20
CHIP = ("hi", "lo", "yy")


def dot_ab(a, b):
    return lax.dot_general(a, b, (((1,), (0,)), ((), ())), preferred_element_type=F32)


def dot_abt(a, b):
    return lax.dot_general(a, b, (((1,), (1,)), ((), ())), preferred_element_type=F32)


def dot_atb(a, b):
    return lax.dot_general(a, b, (((0,), (0,)), ((), ())), preferred_element_type=F32)


def rms_scale(inputs):
    return lax.rsqrt(jnp.mean(inputs * inputs, axis=-1, keepdims=True) + EPSILON)


def norm_backward(inputs, inv_rms, gain_vec, upstream):
    normed = inputs * inv_rms
    normed_grad = upstream * gain_vec
    input_part = inv_rms * (
        normed_grad - normed * jnp.mean(normed_grad * normed, axis=-1, keepdims=True)
    )
    return (input_part, jnp.sum(upstream * normed, axis=0))


def adam_update(weight, moment_one, moment_two, gradient, step_rate, decay_rate):
    first_new = BETA_ONE * moment_one + (1.0 - BETA_ONE) * gradient
    second_new = BETA_TWO * moment_two + (1.0 - BETA_TWO) * gradient * gradient
    corrected = first_new / (1.0 - BETA_ONE**STEP)
    spread = jnp.sqrt(second_new / (1.0 - BETA_TWO**STEP)) + ADAM_EPS
    return (
        weight * (1.0 - step_rate * decay_rate) - step_rate * corrected / spread,
        first_new,
        second_new,
    )


def swap(value, axis):
    return lax.ppermute(value, axis, [(0, 1), (1, 0)])


class Order:
    def __init__(self):
        self.mark = None

    def after(self, value):
        if self.mark is None:
            return value
        return lax.optimization_barrier((value, self.mark))[0]

    def done(self, value):
        value = self.after(value)
        self.mark = value
        return value


def chip_at(step, other_lo, other_yy):
    count = lax.axis_size("hi")
    hi = (lax.axis_index("hi") + step) % count
    return (hi * 2 + (lax.axis_index("lo") ^ other_lo)) * 2 + (lax.axis_index("yy") ^ other_yy)


def turn(value, axis, steps):
    count = lax.axis_size(axis)
    return lax.ppermute(value, axis, [(i, (i + steps) % count) for i in range(count)])


def others_of(every):
    count = lax.axis_size("hi")
    hi = lax.axis_index("hi")
    return [
        lax.dynamic_index_in_dim(every, (hi - k) % count, 0, keepdims=False)
        for k in range(1, count)
    ]


def tree_order(sign):
    steps = [(0, 0), (0, 1)] + [(k, l) for k in range(1, lax.axis_size("hi")) for l in (0, 1)]
    return jnp.stack([chip_at(sign * k, l, y) for y in (0, 1) for k, l in steps]).astype(jnp.int32)


def sum_order():
    steps = range(1, lax.axis_size("hi"))
    chips = [chip_at(k, l, y) for l in (1, 0) for ks in (steps, (0,)) for k in ks for y in (1, 0)]
    return jnp.stack(chips).astype(jnp.int32)


class ChipSum:
    def __init__(self, lo_far, lo_near, far, near):
        self.far, self.near, self.lo_near = far, near, lo_near
        self.lo_far = swap(lo_far, "lo")

    def far_yy(self, order):
        self.far = self.far.astype(F32) + order.done(self.lo_far).astype(F32)
        theirs = self.far[0::2].astype(BF)
        self.yy_far = swap(theirs, "yy")
        order.mark = theirs
        self.lo_near = swap(order.after(self.lo_near), "lo")

    def far_hi(self, order):
        far = (self.far[1::2] + order.done(self.yy_far).astype(F32)).astype(BF)
        self.hi = [turn(far[k - 1], "hi", k) for k in range(1, lax.axis_size("hi"))]
        order.mark = far

    def near_yy(self, order):
        self.near = self.near.astype(F32) + order.done(self.lo_near).astype(F32)
        theirs = self.near[0].astype(BF)
        self.yy_near = swap(theirs, "yy")
        order.mark = theirs

    def total(self, order):
        hi = order.done(self.hi)
        total = self.near[1] + order.done(self.yy_near).astype(F32)
        for part in hi:
            total = total + part.astype(F32)
        return total


def cost(flops, bytes_accessed, transcendentals):
    part = 4096
    return pl.CostEstimate(
        flops=flops // part,
        bytes_accessed=bytes_accessed // part,
        transcendentals=transcendentals // part,
    )


ANYWHERE = pl.BlockSpec(memory_space=pl.ANY)
WHOLE = pl.BlockSpec(memory_space=pltpu.VMEM)


def turn_halves(features, cos_both, sin_both):
    return features * cos_both + pltpu.roll(features, HEAD_WIDTH // 2, 1) * sin_both


def scores_t(keys, queries, key_place, place, start):
    scores = dot_abt(keys, queries) * (1.0 / math.sqrt(HEAD_WIDTH))
    return jnp.where((key_place <= place) & (key_place >= start), scores, NEGATIVE)


def rows_from(refs):
    begin = 0
    for ref in refs:
        yield slice(begin, begin + ref.shape[0]), ref
        begin += ref.shape[0]


def attention_kernel(blocks, parts, rows, chips_ref, *refs):
    n1_refs, refs = refs[:blocks], refs[blocks:]
    bias_ref, cos_ref, sin_ref, key_place_ref, place_ref, start_ref, *refs = refs
    shards, refs = refs[:parts], refs[parts:]
    qkv_ref, o_ref, lse_ref, *out_refs, weight_ref, weights, sems, out_sem = refs
    length = qkv_ref.shape[0]
    copies = [
        pltpu.make_async_copy(
            shards[i],
            weights.at[pl.ds(pl.multiple_of(chips_ref[i] * rows, rows), rows), :],
            sems.at[i],
        )
        for i in range(parts)
    ]
    for copy in copies:
        copy.start()
    for copy in copies:
        copy.wait()
    save = pltpu.make_async_copy(weights, weight_ref, out_sem)
    save.start()
    for at, ref in rows_from(n1_refs):
        projected = dot_ab(ref[...], weights[:, :QKV_COLS]) + bias_ref[...]
        cos_both, sin_both = cos_ref[at, :], sin_ref[at, :]
        for j in range(HEADS + 1):
            cols = slice(j * HEAD_WIDTH, (j + 1) * HEAD_WIDTH)
            qkv_ref[at, cols] = turn_halves(projected[:, cols], cos_both, sin_both).astype(BF)
        cols = slice(Q_COLS + HEAD_WIDTH, QKV_COLS)
        qkv_ref[at, cols] = projected[:, cols].astype(BF)
    keys = qkv_ref[:, Q_COLS : Q_COLS + HEAD_WIDTH]
    values_t = qkv_ref[:, Q_COLS + HEAD_WIDTH : QKV_COLS].T
    lse_ref[...] = jnp.zeros_like(lse_ref)
    key_place = key_place_ref[...]
    for at in range(0, length, TILE):
        block = slice(at, at + TILE)
        place, start = place_ref[:, block], start_ref[:, block]
        for h in range(HEADS):
            cols = slice(h * HEAD_WIDTH, (h + 1) * HEAD_WIDTH)
            scores = scores_t(keys, qkv_ref[block, cols], key_place, place, start)
            top = jnp.max(scores, axis=0, keepdims=True)
            weights_exp = jnp.exp(scores - top)
            total = jnp.sum(weights_exp, axis=0, keepdims=True)
            lse_ref[h : h + 1, block] = top + jnp.log(total)
            prob = (weights_exp * (1.0 / total)).astype(BF)
            o_ref[block, cols] = dot_ab(values_t, prob).astype(BF).T
    for at, ref in rows_from(out_refs):
        ref[...] = dot_abt(o_ref[at, :], weights[:, QKV_COLS:]).astype(BF)
    save.wait()


def documents_kernel(where_ref, ids_ref, other_ref, frequency_ref, angle_ref, key_place_ref, place_ref, start_ref):
    core, place_x = where_ref[0], where_ref[1]
    one = ids_ref.shape[1]

    def in_order(ref):
        rows = [ref[k : k + 1, :] for k in range(2)]
        return [
            jnp.where(place_x == 0, rows[0], rows[1]),
            jnp.where(place_x == 0, rows[1], rows[0]),
        ]

    ids = jnp.concatenate(in_order(ids_ref) + in_order(other_ref), axis=1)
    index = lax.broadcasted_iota(jnp.int32, (1, 4 * one), 1)
    block = index // one
    mine = core * 2 + place_x
    place = jnp.bitwise_xor(mine, block) * one + index - block * one

    def column(row):
        return jnp.broadcast_to(row.astype(F32), (8, 4 * one)).T[:, :1]

    ids_col, place_col = column(ids), column(place)
    ids_row, place_row = ids.astype(F32), place.astype(F32)
    start_row = jnp.min(
        jnp.where(ids_col == ids_row, place_col, 4.0 * one), axis=0, keepdims=True
    )
    place_ref[...] = place
    start_ref[...] = start_row.astype(jnp.int32)
    key_place_ref[...] = place_col.astype(jnp.int32)
    angle_ref[...] = column(place_row - start_row) * frequency_ref[...]


def documents(core, place_x, ids, other_ids):
    one = ids.shape[0] // 2
    exponent = np.arange(0, HEAD_WIDTH, 2, dtype=np.float32) / np.float32(HEAD_WIDTH)
    frequency = np.float32(1.0) / np.float32(ROPE_BASE) ** exponent
    return pl.pallas_call(
        documents_kernel,
        grid_spec=pltpu.PrefetchScalarGridSpec(
            num_scalar_prefetch=1,
            grid=(),
            in_specs=[WHOLE] * 3,
            out_specs=[WHOLE] * 4,
        ),
        out_shape=[
            jax.ShapeDtypeStruct((4 * one, HEAD_WIDTH), F32),
            jax.ShapeDtypeStruct((4 * one, 1), jnp.int32),
            jax.ShapeDtypeStruct((1, 4 * one), jnp.int32),
            jax.ShapeDtypeStruct((1, 4 * one), jnp.int32),
        ],
        compiler_params=pltpu.CompilerParams(vmem_limit_bytes=VMEM_LIMIT),
        cost_estimate=cost(flops=2**20, bytes_accessed=2**20, transcendentals=0),
        name="documents",
    )(
        jnp.stack([core, place_x]).astype(jnp.int32),
        ids.reshape(2, one),
        other_ids.reshape(2, one),
        jnp.asarray(np.concatenate([frequency, frequency])[None]),
    )


def four_shapes(rows):
    return [jax.ShapeDtypeStruct((r, D), BF) for r in (rows, rows // 2, rows // 2) * 2]


def attention(chips, n1, bias, tables, shards):
    length = tables[0].shape[0]
    parts = len(shards)
    rows = shards[0].shape[0]
    return pl.pallas_call(
        functools.partial(attention_kernel, len(n1), parts, rows),
        grid_spec=pltpu.PrefetchScalarGridSpec(
            num_scalar_prefetch=1,
            grid=(),
            in_specs=[WHOLE] * (len(n1) + 6) + [ANYWHERE] * parts,
            out_specs=[WHOLE] * 9 + [ANYWHERE],
            scratch_shapes=[
                pltpu.VMEM((D, ATT_COLS), BF),
                pltpu.SemaphoreType.DMA((parts,)),
                pltpu.SemaphoreType.DMA,
            ],
        ),
        out_shape=[
            jax.ShapeDtypeStruct((length, QKV_COLS), BF),
            jax.ShapeDtypeStruct((length, Q_COLS), BF),
            jax.ShapeDtypeStruct((8, length), F32),
            *four_shapes(length // 4),
            jax.ShapeDtypeStruct((D, ATT_COLS), BF),
        ],
        compiler_params=pltpu.CompilerParams(vmem_limit_bytes=VMEM_LIMIT),
        cost_estimate=cost(
            flops=2 * length * D * ATT_COLS + 4 * HEADS * length * length * HEAD_WIDTH,
            bytes_accessed=16 * 2**20,
            transcendentals=HEADS * length * length,
        ),
        name="attention",
    )(chips, *n1, bias, *tables, *shards)


def attention_back_kernel(das, n1s, count, rows, chips_ref, *refs):
    da_refs, n1_refs, refs = refs[:das], refs[das : das + n1s], refs[das + n1s :]
    qkv_ref, o_ref, lse_ref, weight_ref, *refs = refs
    cos_ref, sin_ref, key_place_ref, place_ref, start_ref, *refs = refs
    dqkv_ref, bias_ref, *refs = refs
    dn1_refs, block_refs, (mixed, left_t, grads) = refs[:6], refs[6:10], refs[10:]
    length = qkv_ref.shape[0]
    scale = 1.0 / math.sqrt(HEAD_WIDTH)
    for at, ref in rows_from(da_refs):
        mixed[at, :] = dot_ab(ref[...], weight_ref[:, QKV_COLS:]).astype(BF)
    key_cols = slice(Q_COLS, Q_COLS + HEAD_WIDTH)
    value_cols = slice(Q_COLS + HEAD_WIDTH, QKV_COLS)
    keys, values = qkv_ref[:, key_cols], qkv_ref[:, value_cols]
    keys_t = keys.T
    key_place = key_place_ref[...]
    keys_grad = jnp.zeros((length, HEAD_WIDTH), F32)
    values_grad = jnp.zeros((length, HEAD_WIDTH), F32)
    for at in range(0, length, TILE):
        block = slice(at, at + TILE)
        place, start = place_ref[:, block], start_ref[:, block]
        for h in range(HEADS):
            cols = slice(h * HEAD_WIDTH, (h + 1) * HEAD_WIDTH)
            queries, up = qkv_ref[block, cols], mixed[block, cols]
            scores = scores_t(keys, queries, key_place, place, start)
            prob = jnp.exp(scores - lse_ref[h : h + 1, block])
            prob_grad = dot_abt(values, up)
            inner = jnp.sum(prob * prob_grad, axis=0, keepdims=True)
            score_grad = (prob * (prob_grad - inner)).astype(BF)
            values_grad += dot_ab(prob.astype(BF), up)
            keys_grad += dot_ab(score_grad, queries)
            query_grad = dot_ab(keys_t, score_grad).T * scale
            dqkv_ref[block, cols] = turn_halves(
                query_grad, cos_ref[block, :], -sin_ref[block, :]
            ).astype(BF)
    dqkv_ref[:, key_cols] = turn_halves(keys_grad * scale, cos_ref[...], -sin_ref[...]).astype(BF)
    dqkv_ref[:, value_cols] = values_grad.astype(BF)
    bias_ref[...] = jnp.sum(dqkv_ref[...].astype(F32), axis=0, keepdims=True)
    for cols, left_refs, right_ref in (
        (slice(0, QKV_COLS), n1_refs, dqkv_ref),
        (slice(QKV_COLS, ATT_COLS), da_refs, o_ref),
    ):
        for at, ref in rows_from(left_refs):
            left_t[:, at] = ref[...].T
        grads[:, :, cols] = (
            dot_ab(left_t[...], right_ref[...]).astype(BF).reshape(4 * count, rows, -1)
        )
    at = 0
    for ref in block_refs:
        for k in range(ref.shape[0]):
            ref[k] = grads[chips_ref[at]]
            at += 1
    for at, ref in rows_from(dn1_refs):
        ref[...] = dot_abt(dqkv_ref[at, :], weight_ref[:, :QKV_COLS]).astype(BF)


def attention_back(chips, da, n1, qkv, o, lse, weight, tables):
    length = qkv.shape[0]
    count = chips.shape[0] // 4
    rows = D // (4 * count)
    blocks = [
        jax.ShapeDtypeStruct((2 * k, rows, ATT_COLS), BF) for k in (count - 1, 1, count - 1, 1)
    ]
    return pl.pallas_call(
        functools.partial(attention_back_kernel, len(da), len(n1), count, rows),
        grid_spec=pltpu.PrefetchScalarGridSpec(
            num_scalar_prefetch=1,
            grid=(),
            in_specs=[WHOLE] * (len(da) + len(n1) + 9),
            out_specs=[WHOLE] * 12,
            scratch_shapes=[
                pltpu.VMEM((length, Q_COLS), BF),
                pltpu.VMEM((D, length), BF),
                pltpu.VMEM((4 * count, rows, ATT_COLS), BF),
            ],
        ),
        out_shape=[
            jax.ShapeDtypeStruct((length, QKV_COLS), BF),
            jax.ShapeDtypeStruct((1, QKV_COLS), F32),
            *four_shapes(length // 4),
            *blocks,
        ],
        compiler_params=pltpu.CompilerParams(vmem_limit_bytes=VMEM_LIMIT),
        cost_estimate=cost(
            flops=2 * length * D * 2 * ATT_COLS + 10 * HEADS * length * length * HEAD_WIDTH,
            bytes_accessed=24 * 2**20,
            transcendentals=HEADS * length * length,
        ),
        name="attention_back",
    )(chips, *da, *n1, qkv, o, lse, weight, *tables)


def feed_forward_kernel(whole, split, rows, chips_ref, *refs):
    n2_refs, dy_refs, refs = refs[:6], refs[6:12], refs[12:]
    pieces, refs = refs[: whole + 2 * split], refs[whole + 2 * split :]
    dn2_refs, refs = refs[:8], refs[8:]
    u_ref, dgate_ref, dup_ref, n2_t_ref, dy_t_ref, down_ref, *refs = refs
    gu_w, d_w, tiles, tile_sems, sems, out_sem = refs
    step = pl.program_id(0)
    steps = pl.num_programs(0)
    one = tiles.shape[2]

    def copies():
        for i in range(whole + split):
            at = pl.ds(pl.multiple_of(chips_ref[i] * rows, rows), rows)
            for j in range(3):
                if i < whole or j < 2:
                    here = pieces[i].at[j]
                else:
                    here = pieces[i + split]
                if j < 2:
                    there = gu_w.at[at, pl.ds(j * FF_OWN, FF_OWN)]
                else:
                    there = d_w.at[at, :]
                yield pltpu.make_async_copy(here, there, sems.at[i, j])

    def tile_copies(j):
        part, row = divmod(j, 4)
        ref, at = ((0, 0), (1, 0), (1, one), (2, 0))[row]
        for k, taken in enumerate((n2_refs, dy_refs)):
            yield pltpu.make_async_copy(
                taken[3 * part + ref].at[pl.ds(at, one), :],
                tiles.at[j % 2, k],
                tile_sems.at[j % 2, k],
            )

    save = pltpu.make_async_copy(d_w, down_ref, out_sem)

    @pl.when(step == 0)
    def _():
        for copy in copies():
            copy.start()
        for copy in tile_copies(0):
            copy.start()
        for copy in copies():
            copy.wait()
        save.start()

    for j in range(8):

        @pl.when(step == j)
        def _(j=j):
            if j < 7:
                for copy in tile_copies(j + 1):
                    copy.start()
            for copy in tile_copies(j):
                copy.wait()

    n2, dy = tiles[step % 2, 0], tiles[step % 2, 1]
    n2_t_ref[...] = n2.T
    dy_t_ref[...] = dy.T
    gate_up = dot_ab(n2, gu_w[...])
    du = dot_ab(dy, d_w[...])
    gate, up = gate_up[:, :FF_OWN], gate_up[:, FF_OWN:]
    sig = jax.nn.sigmoid(gate)
    silu = gate * sig
    u_ref[...] = (silu * up).astype(BF)
    dup = (du * silu).astype(BF)
    dgate = (du * up * sig * (1.0 + gate * (1.0 - sig))).astype(BF)
    dup_ref[...] = dup
    dgate_ref[...] = dgate
    dn2 = dot_abt(jnp.concatenate([dgate, dup], axis=1), gu_w[...]).astype(BF)
    for j in range(8):

        @pl.when(step == j)
        def _(j=j):
            dn2_refs[j][...] = dn2

    @pl.when(step == steps - 1)
    def _():
        save.wait()


def feed_forward(chips, n2, dy, whole, split):
    rows = whole[0].shape[1]
    one = n2[0].shape[0]
    length = 8 * one
    tile = lambda width: pl.BlockSpec((one, width), lambda i, c: (i, 0))
    turned = pl.BlockSpec((D, one), lambda i, c: (0, i))
    kept = pl.BlockSpec((one, D), lambda i, c: (0, 0))
    parts = len(whole) + len(split)
    return pl.pallas_call(
        functools.partial(feed_forward_kernel, len(whole), len(split), rows),
        grid_spec=pltpu.PrefetchScalarGridSpec(
            num_scalar_prefetch=1,
            grid=(8,),
            in_specs=[ANYWHERE] * (12 + len(whole) + 2 * len(split)),
            out_specs=[kept] * 8 + [tile(FF_OWN)] * 3 + [turned, turned, ANYWHERE],
            scratch_shapes=[
                pltpu.VMEM((D, 2 * FF_OWN), BF),
                pltpu.VMEM((D, FF_OWN), BF),
                pltpu.VMEM((2, 2, one, D), BF),
                pltpu.SemaphoreType.DMA((2, 2)),
                pltpu.SemaphoreType.DMA((parts, 3)),
                pltpu.SemaphoreType.DMA,
            ],
        ),
        out_shape=[jax.ShapeDtypeStruct((one, D), BF)] * 8
        + [jax.ShapeDtypeStruct((length, FF_OWN), BF)] * 3
        + [jax.ShapeDtypeStruct((D, length), BF)] * 2
        + [jax.ShapeDtypeStruct((D, FF_OWN), BF)],
        compiler_params=pltpu.CompilerParams(vmem_limit_bytes=VMEM_LIMIT),
        cost_estimate=cost(
            flops=2 * 5 * length * D * FF_OWN,
            bytes_accessed=60 * 2**20,
            transcendentals=length * FF_OWN,
        ),
        name="feed_forward",
    )(chips, *n2, *dy, *whole, *[gu for gu, _ in split], *[d for _, d in split])


def weight_grad_kernel(rows, place_ref, left_ref, right_ref, *refs):
    keep_ref, send_ref, total = refs
    width = right_ref.shape[1]
    for at in range(0, width, 256):
        to = min(at + 256, width)
        total[:, :, at:to] = dot_ab(left_ref[...], right_ref[:, at:to]).reshape(
            4, rows, to - at
        )
    lo, yy = place_ref[1], place_ref[2]
    for k in range(2):
        row = jnp.where(lo == 0, k, 1 - k) * 2
        keep_ref[0, k] = total[row + yy].astype(BF)
        send_ref[0, k] = total[row + 1 - yy].astype(BF)


def weight_grad(place, left, right):
    count = lax.axis_size("hi")
    length, width = right.shape
    rows = left.shape[0] // (4 * count)
    block = pl.BlockSpec((1, 2, rows, width), lambda i, p: (i, 0, 0, 0))
    out = jax.ShapeDtypeStruct((count, 2, rows, width), BF)
    return pl.pallas_call(
        functools.partial(weight_grad_kernel, rows),
        grid_spec=pltpu.PrefetchScalarGridSpec(
            num_scalar_prefetch=1,
            grid=(count,),
            in_specs=[
                pl.BlockSpec((4 * rows, length), lambda i, p: (lax.rem(i + p[0], count), 0)),
                pl.BlockSpec((length, width), lambda i, p: (0, 0)),
            ],
            out_specs=[block] * 2,
            scratch_shapes=[pltpu.VMEM((4, rows, width), F32)],
        ),
        out_shape=[out] * 2,
        compiler_params=pltpu.CompilerParams(vmem_limit_bytes=VMEM_LIMIT),
        cost_estimate=cost(
            flops=2 * length * D * width, bytes_accessed=16 * 2**20, transcendentals=0
        ),
        name="weight_grad",
    )(place, left, right)


def down_kernel(left_ref, right_ref, *out_refs):
    product = dot_abt(left_ref[...], right_ref[...]).astype(BF)
    for j in range(8):

        @pl.when(pl.program_id(0) == j)
        def _(j=j):
            out_refs[j][...] = product


def down(left, right):
    length, width = left.shape
    one = length // 8
    return pl.pallas_call(
        down_kernel,
        grid=(8,),
        in_specs=[
            pl.BlockSpec((one, width), lambda i: (i, 0)),
            pl.BlockSpec((D, width), lambda i: (0, 0)),
        ],
        out_specs=[pl.BlockSpec((one, D), lambda i: (0, 0))] * 8,
        out_shape=[jax.ShapeDtypeStruct((one, D), BF)] * 8,
        compiler_params=pltpu.CompilerParams(vmem_limit_bytes=VMEM_LIMIT),
        cost_estimate=cost(
            flops=2 * length * D * width, bytes_accessed=14 * 2**20, transcendentals=0
        ),
        name="down",
    )(left, right)


def total_of(*parts):
    return sum(part.astype(F32) for part in parts)


class EightSum:
    def __init__(self, parts):
        self.keep = parts[:4]
        self.core = [None] * 4
        for k in (3, 1, 2, 0):
            self.core[k] = swap(parts[4 + k], "core")
        self.half = parts[0].shape[0] // 2

    def second(self, order):
        self.core = order.done(self.core)
        half = self.half
        both, by_x, by_lo = [total_of(self.keep[k], self.core[k]) for k in (3, 1, 2)]
        self.to_lo = swap(both[:half].astype(BF), "tensor")
        self.to_x = swap(both[half:].astype(BF), "lo")
        self.x_first = swap(by_x[:half].astype(BF), "tensor")
        self.lo_second = swap(by_lo[half:].astype(BF), "lo")
        self.by_x, self.by_lo = by_x[half:], by_lo[:half]

    def third(self, order):
        to_lo, to_x, self.x_first, self.lo_second = order.done(
            (self.to_lo, self.to_x, self.x_first, self.lo_second)
        )
        self.x_second = swap(total_of(self.by_x, to_x).astype(BF), "tensor")
        self.lo_first = swap(total_of(self.by_lo, to_lo).astype(BF), "lo")

    def total(self, order):
        x_second, lo_first = order.done((self.x_second, self.lo_first))
        return (
            total_of(self.keep[0], self.core[0])
            + jnp.concatenate([self.x_first, x_second], axis=0).astype(F32)
            + jnp.concatenate([lo_first, self.lo_second], axis=0).astype(F32)
        )


class FourSum:
    def __init__(self, own, first, second, core_own, core_first, core_second):
        self.own, self.x = own, (first, second)
        self.core_x = swap(core_first, "core"), swap(core_second, "core")
        self.core_own = swap(core_own, "core")

    def second(self, order):
        core_x = order.done(self.core_x)
        by_x = [total_of(*pair).astype(BF) for pair in zip(self.x, core_x)]
        self.x = [swap(part, "tensor") for part in by_x]
        order.mark = by_x

    def total(self, order):
        self.core_own = order.done(self.core_own)
        x = order.done(self.x)
        return total_of(self.own, self.core_own, jnp.concatenate(x, axis=0))


class GradSum:
    def __init__(self, keep, send):
        self.keep = keep
        self.other = swap(send, "yy")

    def across(self, order, by_gather):
        self.other = order.done(self.other)
        count = lax.axis_size("hi")
        far = [total_of(self.keep[k], self.other[k]).astype(BF) for k in range(1, count)]
        if by_gather:
            self.every = [lax.all_gather(part, "hi") for part in far]
        else:
            self.every = None
            self.far = [turn(part, "hi", k + 1) for k, part in enumerate(far)]
        order.mark = far

    def arrived(self, order):
        if self.every is None:
            self.far = order.done(self.far)
        else:
            every = order.done(self.every)
            self.far = [others_of(part)[k] for k, part in enumerate(every)]

    def total(self):
        total = self.keep[0].astype(F32) + self.other[0].astype(F32)
        for far in self.far:
            total = total + far.astype(F32)
        return total


def body(
    tokens,
    cotangent,
    segments,
    small_params,
    small_first,
    small_second,
    qkv_weight,
    qkv_first,
    qkv_second,
    out_weight,
    out_first,
    out_second,
    gateup_weight,
    gateup_first,
    gateup_second,
    down_weight,
    down_first,
    down_second,
):
    hi_count = lax.axis_size("hi")
    hi, lo, yy = lax.axis_index("hi"), lax.axis_index("lo"), lax.axis_index("yy")
    core = lax.axis_index("core")
    place_x = lax.axis_index("tensor")
    own_rows = tokens.shape[0]
    shard_rows = qkv_weight.shape[0]
    gain_one = small_params[:D]
    gain_two = small_params[D : 2 * D]
    bias_all = small_params[2 * D :]
    q_at = place_x * (bias_all.shape[0] // 2) + core * Q_COLS
    kv_at = place_x * (bias_all.shape[0] // 2) + 2 * Q_COLS
    bias_local = jnp.concatenate(
        [
            lax.dynamic_slice_in_dim(bias_all, q_at, Q_COLS),
            lax.dynamic_slice_in_dim(bias_all, kv_at, 2 * HEAD_WIDTH),
        ]
    )

    order = Order()
    steps = range(1, hi_count)

    def both_cores(mine, other, axis):
        return jnp.where(
            core == 0,
            jnp.concatenate([mine, other], axis=axis),
            jnp.concatenate([other, mine], axis=axis),
        )

    other_ids = swap(segments, "core")
    qkv_low = qkv_weight.astype(BF)
    out_low = out_weight.astype(BF).T

    def attention_pack(which):
        return jnp.concatenate(
            [
                lax.dynamic_slice_in_dim(qkv_low, which * Q_COLS, Q_COLS, 1),
                qkv_low[:, 2 * Q_COLS :],
                lax.dynamic_slice_in_dim(out_low, which * Q_COLS, Q_COLS, 1),
            ],
            axis=1,
        )

    att_theirs = attention_pack(1 - core)
    att_core = swap(att_theirs, "core")
    order.mark = att_theirs
    rows_in = order.after(tokens).astype(F32)
    scale_one = rms_scale(rows_in)
    n1 = (rows_in * scale_one * gain_one).astype(BF)
    n1_x = swap(n1, "tensor")
    order.mark = n1
    att_shard = both_cores(attention_pack(core), order.done(att_core), 0)
    order.mark = att_shard
    att_hi = [turn(att_shard, "hi", k) for k in steps]
    att_yy = swap(att_shard, "yy")
    att_lo = swap(att_shard, "lo")

    gateup_in, down_in = order.after((gateup_weight, down_weight))
    ff_low = jnp.pad(
        jnp.concatenate([gateup_in.astype(BF), down_in.astype(BF).T[None]], axis=0),
        ((0, 0), (0, 0), (0, FF_PAD - FF_LOCAL)),
    )
    ff_mine = lax.dynamic_slice_in_dim(ff_low, core * FF_CORE, FF_CORE, 2)
    ff_theirs = lax.dynamic_slice_in_dim(ff_low, (1 - core) * FF_CORE, FF_CORE, 2)
    ff_core = swap(ff_theirs, "core")
    order.mark = ff_theirs

    ff_shard = both_cores(ff_mine, order.done(ff_core), 1)
    ff_own = lax.dynamic_slice_in_dim(ff_shard, lo * FF_OWN, FF_OWN, 2)
    ff_theirs = lax.dynamic_slice_in_dim(ff_shard, (1 - lo) * FF_OWN, FF_OWN, 2)
    order.mark = ff_theirs
    ff_hi = lax.all_gather(ff_own, "hi")
    att_lo = order.done(att_lo)
    att_lo_yy = swap(att_lo, "yy")
    att_yy = order.done(att_yy)
    att_hi = order.done(att_hi)
    att_hi_lo = [swap(part, "lo") for part in att_hi]
    att_hi_yy = [swap(part, "yy") for part in att_hi]
    n1_core = swap(order.after(n1), "core")
    att_lo_yy = order.done(att_lo_yy)
    att_hi_lo = order.done(att_hi_lo)
    att_hi_lo_yy = [swap(part, "yy") for part in att_hi_lo]
    ff_lo = swap(order.after(ff_theirs), "lo")
    n1_core = order.done(n1_core)
    n1_x = order.done(n1_x)
    n1_core_x = swap(n1_x, "core")
    other_ids = order.done(other_ids)
    angles, key_place, row_place, row_start = documents(core, place_x, segments, other_ids)
    sign = jnp.where(jnp.arange(HEAD_WIDTH) < HEAD_WIDTH // 2, -1.0, 1.0)
    tables = order.after((jnp.cos(angles), jnp.sin(angles) * sign, key_place, row_place, row_start))
    order.mark = tables[0]
    att_hi_yy = order.done(att_hi_yy)
    cot_x = swap(order.after(cotangent), "tensor")
    n1_core_x = order.done(n1_core_x)
    att_hi_lo_yy = order.done(att_hi_lo_yy)
    ff_yy = swap(order.after(ff_own), "yy")

    near_parts = [att_shard, att_lo]
    yy_parts = [att_yy, att_lo_yy]
    for k in range(hi_count - 1):
        near_parts += [att_hi[k], att_hi_lo[k]]
        yy_parts += [att_hi_yy[k], att_hi_lo_yy[k]]
    att_parts = near_parts + yy_parts
    n1_parts = order.after((n1, n1_x, n1_core, n1_core_x))
    qkv, attn_rows, lse, *out_parts, att_weight = attention(
        tree_order(-1), n1_parts, bias_local[None], tables, att_parts
    )
    order.mark = lse

    out = FourSum(*out_parts)
    half = own_rows // 2
    cot_x = order.done(cot_x)
    ff_lo = order.done(ff_lo)
    ff_lo_hi = [lax.all_gather(part, "hi") for part in (ff_lo[:2], ff_lo[2])]
    ff_yy = order.done(ff_yy)
    ff_lo_yy = swap(ff_lo, "yy")
    out.second(order)
    cot_lo = swap(order.after(cotangent), "lo")
    residual = rows_in + out.total(order)
    scale_two = rms_scale(residual)
    n2 = (residual * scale_two * gain_two).astype(BF)
    n2_x_second, n2_lo_first = swap(n2[half:], "tensor"), swap(n2[:half], "lo")
    n2_x_first, n2_lo_second = swap(n2[:half], "tensor"), swap(n2[half:], "lo")
    order.mark = n2
    ff_hi = others_of(order.done(ff_hi))
    order.mark = ff_hi
    n2_x_second, n2_lo_first = order.done((n2_x_second, n2_lo_first))
    n2_both = swap(n2_lo_first, "tensor"), swap(n2_x_second, "lo")
    ff_lo_yy, cot_lo = order.done((ff_lo_yy, cot_lo))
    ff_hi_yy = [swap(order.after(part), "yy") for part in ff_hi]
    n2_x_first, n2_lo_second = order.done((n2_x_first, n2_lo_second))
    n2_near = jnp.concatenate([n2_x_first, n2_x_second, n2_lo_first, n2_lo_second])
    n2_core_near = swap(n2_near, "core")
    order.mark = n2_near
    n2_both = jnp.concatenate(order.done(n2_both))
    n2_core_both, n2_core = swap(n2_both, "core"), swap(n2, "core")
    order.mark = n2_both
    cot_both = swap(order.after(cot_lo[:half]), "tensor"), swap(order.after(cot_x[half:]), "lo")
    n2_core_near, n2_core_both, n2_core = order.done((n2_core_near, n2_core_both, n2_core))
    cot_both = order.done(cot_both)
    cot_parts = [cotangent, jnp.concatenate([cot_x, cot_lo]), jnp.concatenate(cot_both)]
    cot_parts += [swap(part, "core") for part in cot_parts]
    order.mark = cot_parts[:3]
    ff_hi_yy = order.done(ff_hi_yy)
    ff_lo_hi_gu = others_of(order.done(ff_lo_hi[0]))
    ff_lo_hi_yy_gu = [swap(part, "yy") for part in ff_lo_hi_gu]
    order.mark = ff_lo_hi_gu
    ff_lo_hi_d = others_of(order.done(ff_lo_hi[1]))
    ff_lo_hi_yy_d = [swap(part, "yy") for part in ff_lo_hi_d]
    order.mark = ff_lo_hi_d
    cot_parts = order.done(cot_parts)
    ff_lo_hi_yy_gu = order.done(ff_lo_hi_yy_gu)
    ff_lo_hi_yy_d = order.done(ff_lo_hi_yy_d)
    n2_parts = [n2, n2_near, n2_both, n2_core, n2_core_near, n2_core_both]

    whole = [ff_own, ff_lo, ff_yy, ff_lo_yy, *ff_hi, *ff_hi_yy]
    split = [*zip(ff_lo_hi_gu, ff_lo_hi_d), *zip(ff_lo_hi_yy_gu, ff_lo_hi_yy_d)]
    ff_chips = [chip_at(0, l, y) for y in (0, 1) for l in (0, 1)]
    ff_chips += [chip_at(-k, l, y) for l in (0, 1) for y in (0, 1) for k in steps]
    *dn2_parts, hidden, gate_grad, up_grad, n2_t, cot_t, w_down = feed_forward(
        jnp.stack(ff_chips).astype(jnp.int32), order.after(n2_parts), cot_parts, whole, split
    )
    order.mark = w_down

    place = jnp.stack([hi, lo, yy]).astype(jnp.int32)

    def grad_of(left, right):
        keep, send = weight_grad(place, order.after(left), right)
        order.mark = keep
        return GradSum(keep, send)

    ff_squares = 0.0
    rows_of = lambda value, which, axis: lax.dynamic_slice_in_dim(
        value, which * shard_rows, shard_rows, axis
    )

    def summed_up(grad):
        nonlocal ff_squares
        total = order.after(grad.total())
        ff_squares = ff_squares + jnp.sum(total * total)
        low = total.astype(BF)
        order.mark = low
        return low[0], swap(low[1], "lo")

    def own_rows_of(low, other):
        other = order.done(other)
        cols = jnp.where(
            lo == 0,
            jnp.concatenate([low, other], axis=1),
            jnp.concatenate([other, low], axis=1),
        )
        theirs = rows_of(cols, 1 - core, 0)
        order.mark = theirs
        return rows_of(cols, core, 0), swap(theirs, "core")

    dn2 = EightSum(dn2_parts)
    d_sum = grad_of(cot_t, hidden)
    dn2.second(order)
    g_sum = grad_of(n2_t, gate_grad)
    dn2.third(order)
    u_sum = grad_of(n2_t, up_grad)
    d_sum.across(order, True)
    norm_two_in, gain_two_grad = norm_backward(residual, scale_two, gain_two, dn2.total(order))
    residual_grad = cotangent.astype(F32) + norm_two_in
    da = residual_grad.astype(BF)
    da_x = [swap(da[:half], "tensor"), swap(da[half:], "tensor")]
    da_core = swap(da, "core")
    order.mark = da
    branch_parts = down(*order.after((hidden, w_down)))
    order.mark = branch_parts[0]
    da_x = order.done(da_x)
    da_core_x = [swap(part, "core") for part in da_x]
    da_core, da_core_x = order.done((da_core, da_core_x))

    _, bias_grad, *parts = attention_back(
        sum_order(),
        order.after((da, *da_x, da_core, *da_core_x)),
        n1_parts,
        qkv,
        attn_rows,
        lse,
        att_weight,
        tables,
    )
    order.mark = bias_grad
    g_sum.across(order, True)
    dn1 = FourSum(*parts[:6])
    att = ChipSum(*parts[6:])
    dn1.second(order)
    d_sum.arrived(order)
    u_sum.across(order, False)
    att.far_yy(order)
    norm_one_in, gain_one_grad = norm_backward(rows_in, scale_one, gain_one, dn1.total(order))
    order.mark = gain_one_grad
    att.far_hi(order)
    d_low, d_way = summed_up(d_sum)
    input_grad = residual_grad + norm_one_in
    att.near_yy(order)
    branch = EightSum(order.after(branch_parts))
    g_sum.arrived(order)
    g_low, g_way = summed_up(g_sum)
    d_rows = own_rows_of(d_low, d_way)
    branch.second(order)
    u_sum.arrived(order)
    u_low, u_way = summed_up(u_sum)
    att_sum = att.total(order)
    att_low = att_sum.astype(BF)
    other_att = swap(rows_of(att_low, 1 - core, 0), "core")
    order.mark = att_low
    g_rows = own_rows_of(g_low, g_way)
    branch.third(order)
    other_att = order.done(other_att)

    own_att = rows_of(att_low, core, 0)
    first_att = jnp.where(core == 0, own_att, other_att).astype(F32)
    second_att = jnp.where(core == 0, other_att, own_att).astype(F32)
    kv_sum = first_att[:, Q_COLS:QKV_COLS] + second_att[:, Q_COLS:QKV_COLS]
    qkv_owned = jnp.concatenate([first_att[:, :Q_COLS], second_att[:, :Q_COLS], kv_sum], axis=1)
    out_owned = jnp.concatenate([first_att[:, QKV_COLS:], second_att[:, QKV_COLS:]], axis=1).T
    owned_squares = (
        jnp.sum(qkv_owned * qkv_owned) + jnp.sum(out_owned * out_owned) + ff_squares
    )
    bias_grad = order.after(bias_grad)[0]
    bias_slots = lax.dynamic_update_slice_in_dim(
        jnp.zeros_like(bias_all), bias_grad[:Q_COLS], q_at, 0
    )
    bias_slots = lax.dynamic_update_slice_in_dim(bias_slots, bias_grad[Q_COLS:], kv_at, 0)
    summed = jnp.concatenate(
        [gain_one_grad, gain_two_grad, bias_slots, jnp.full((128,), owned_squares)]
    )
    first = summed + order.done(swap(summed, "core"))
    order.mark = first
    u_rows = own_rows_of(u_low, u_way)
    summed = first + order.done(swap(first, "tensor"))
    summed = summed + order.done(swap(summed, "yy"))
    block_out = (residual + branch.total(order)).astype(BF)
    summed = summed + order.done(swap(summed, "lo"))
    step = 1
    while step < hi_count:
        moved = lax.ppermute(summed, "hi", [(i, i ^ step) for i in range(hi_count)])
        summed = summed + order.done(moved)
        step *= 2

    def owned(rows):
        mine, other = rows
        return both_cores(mine, other, 1)[:, :FF_LOCAL].astype(F32)

    gateup_owned = jnp.stack([owned(g_rows), owned(u_rows)])
    down_owned = owned(d_rows).T
    small_grad = summed[:-128]
    squares = summed[-1] + jnp.sum(small_grad * small_grad)
    grad_norm = jnp.sqrt(squares)
    clip_factor = jnp.minimum(1.0, MAX_NORM / (grad_norm + 1e-06))
    new_small, new_small_first, new_small_second = adam_update(
        small_params, small_first, small_second, clip_factor * small_grad, 0.5, 0.0
    )
    new_qkv, new_qkv_first, new_qkv_second = adam_update(
        qkv_weight, qkv_first, qkv_second, clip_factor * qkv_owned, 2.0 / math.sqrt(D), WEIGHT_DECAY
    )
    new_out, new_out_first, new_out_second = adam_update(
        out_weight,
        out_first,
        out_second,
        clip_factor * out_owned,
        8.0 / math.sqrt(QUERY_HEADS * HEAD_WIDTH),
        WEIGHT_DECAY,
    )
    new_gateup, new_gateup_first, new_gateup_second = adam_update(
        gateup_weight,
        gateup_first,
        gateup_second,
        clip_factor * gateup_owned,
        2.0 / math.sqrt(D),
        WEIGHT_DECAY,
    )
    new_down, new_down_first, new_down_second = adam_update(
        down_weight,
        down_first,
        down_second,
        clip_factor * down_owned,
        3.0 / math.sqrt(FF),
        WEIGHT_DECAY,
    )
    return (
        block_out,
        input_grad,
        grad_norm,
        new_small,
        new_small_first,
        new_small_second,
        new_qkv,
        new_qkv_first,
        new_qkv_second,
        new_out,
        new_out_first,
        new_out_second,
        new_gateup,
        new_gateup_first,
        new_gateup_second,
        new_down,
        new_down_first,
        new_down_second,
    )


def solution(mesh):
    count = mesh.shape["dp"]
    fine = Mesh(
        mesh.devices.reshape(count // 8, 2, 2, 2, mesh.shape["tensor"]),
        CHIP + ("core", "tensor"),
    )
    dp = CHIP + ("core",)
    rows = P(dp + ("tensor",), None)
    by_rows = P(dp, "tensor")
    by_cols = P("tensor", dp)
    stacked = P(None, dp, "tensor")
    weights = (by_rows,) * 3 + (by_cols,) * 3 + (stacked,) * 3 + (by_cols,) * 3
    return jax.shard_map(
        body,
        mesh=fine,
        in_specs=(rows, rows, P(dp), P(), P(), P()) + weights,
        out_specs=(rows, rows, P(), P(), P(), P()) + weights,
        check_vma=False,
    )
```

```python
import functools
import math

import jax
import jax.numpy as jnp
import numpy as np
from jax import lax
from jax.experimental import pallas as pl
from jax.experimental.pallas import tpu as pltpu
from jax.sharding import Mesh
from jax.sharding import PartitionSpec as P

D = 1536
FF = 8960
QUERY_HEADS = 12
KEY_VALUE_HEADS = 2
HEAD_WIDTH = 128
STEP = 10

EPSILON = 1e-06
ROPE_BASE = 1000000.0
BETA_ONE = 0.9
BETA_TWO = 0.999
ADAM_EPS = 1e-08
WEIGHT_DECAY = 0.1
MAX_NORM = 1.0
NEGATIVE = -1e30

BF = jnp.bfloat16
F32 = jnp.float32
HEADS = 3
Q_COLS = HEADS * HEAD_WIDTH
QKV_COLS = Q_COLS + 2 * HEAD_WIDTH
ATT_COLS = QKV_COLS + Q_COLS
FF_LOCAL = FF // 2
FF_PAD = 4608
FF_CORE = FF_PAD // 2
FF_OWN = FF_PAD // 4
TILE = 256
VMEM_LIMIT = 60 * 2**20
CHIP = ("hi", "lo", "yy")


def dot_ab(a, b):
    return lax.dot_general(a, b, (((1,), (0,)), ((), ())), preferred_element_type=F32)


def dot_abt(a, b):
    return lax.dot_general(a, b, (((1,), (1,)), ((), ())), preferred_element_type=F32)


def dot_atb(a, b):
    return lax.dot_general(a, b, (((0,), (0,)), ((), ())), preferred_element_type=F32)


def rms_scale(inputs):
    return lax.rsqrt(jnp.mean(inputs * inputs, axis=-1, keepdims=True) + EPSILON)


def norm_backward(inputs, inv_rms, gain_vec, upstream):
    normed = inputs * inv_rms
    normed_grad = upstream * gain_vec
    input_part = inv_rms * (
        normed_grad - normed * jnp.mean(normed_grad * normed, axis=-1, keepdims=True)
    )
    return (input_part, jnp.sum(upstream * normed, axis=0))


def adam_update(weight, moment_one, moment_two, gradient, step_rate, decay_rate):
    first_new = BETA_ONE * moment_one + (1.0 - BETA_ONE) * gradient
    second_new = BETA_TWO * moment_two + (1.0 - BETA_TWO) * gradient * gradient
    corrected = first_new / (1.0 - BETA_ONE**STEP)
    spread = jnp.sqrt(second_new / (1.0 - BETA_TWO**STEP)) + ADAM_EPS
    return (
        weight * (1.0 - step_rate * decay_rate) - step_rate * corrected / spread,
        first_new,
        second_new,
    )


def swap(value, axis):
    return lax.ppermute(value, axis, [(0, 1), (1, 0)])


class Order:
    def __init__(self):
        self.mark = None

    def after(self, value):
        if self.mark is None:
            return value
        return lax.optimization_barrier((value, self.mark))[0]

    def done(self, value):
        value = self.after(value)
        self.mark = value
        return value


def chip_at(step, other_lo, other_yy):
    count = lax.axis_size("hi")
    hi = (lax.axis_index("hi") + step) % count
    return (hi * 2 + (lax.axis_index("lo") ^ other_lo)) * 2 + (lax.axis_index("yy") ^ other_yy)


def turn(value, axis, steps):
    count = lax.axis_size(axis)
    return lax.ppermute(value, axis, [(i, (i + steps) % count) for i in range(count)])


def others_of(every):
    count = lax.axis_size("hi")
    hi = lax.axis_index("hi")
    return [
        lax.dynamic_index_in_dim(every, (hi - k) % count, 0, keepdims=False)
        for k in range(1, count)
    ]


def tree_order(sign):
    steps = [(0, 0), (0, 1)] + [(k, l) for k in range(1, lax.axis_size("hi")) for l in (0, 1)]
    return jnp.stack([chip_at(sign * k, l, y) for y in (0, 1) for k, l in steps]).astype(jnp.int32)


def sum_order():
    steps = range(1, lax.axis_size("hi"))
    chips = [chip_at(k, l, y) for l in (1, 0) for ks in (steps, (0,)) for k in ks for y in (1, 0)]
    return jnp.stack(chips).astype(jnp.int32)


class ChipSum:
    def __init__(self, lo_far, lo_near, far, near):
        self.far, self.near, self.lo_near = far, near, lo_near
        self.lo_far = swap(lo_far, "lo")

    def far_yy(self, order):
        self.far = self.far.astype(F32) + order.done(self.lo_far).astype(F32)
        theirs = self.far[0::2].astype(BF)
        self.yy_far = swap(theirs, "yy")
        order.mark = theirs
        self.lo_near = swap(order.after(self.lo_near), "lo")

    def far_hi(self, order):
        far = (self.far[1::2] + order.done(self.yy_far).astype(F32)).astype(BF)
        self.hi = [turn(far[k - 1], "hi", k) for k in range(1, lax.axis_size("hi"))]
        order.mark = far

    def near_yy(self, order):
        self.near = self.near.astype(F32) + order.done(self.lo_near).astype(F32)
        theirs = self.near[0].astype(BF)
        self.yy_near = swap(theirs, "yy")
        order.mark = theirs

    def total(self, order):
        hi = order.done(self.hi)
        total = self.near[1] + order.done(self.yy_near).astype(F32)
        for part in hi:
            total = total + part.astype(F32)
        return total


def cost(flops, bytes_accessed, transcendentals):
    part = 4096
    return pl.CostEstimate(
        flops=flops // part,
        bytes_accessed=bytes_accessed // part,
        transcendentals=transcendentals // part,
    )


ANYWHERE = pl.BlockSpec(memory_space=pl.ANY)
WHOLE = pl.BlockSpec(memory_space=pltpu.VMEM)


def turn_halves(features, cos_both, sin_both):
    return features * cos_both + pltpu.roll(features, HEAD_WIDTH // 2, 1) * sin_both


def scores_t(keys, queries, key_place, place, start):
    scores = dot_abt(keys, queries) * (1.0 / math.sqrt(HEAD_WIDTH))
    return jnp.where((key_place <= place) & (key_place >= start), scores, NEGATIVE)


def rows_from(refs):
    begin = 0
    for ref in refs:
        yield slice(begin, begin + ref.shape[0]), ref
        begin += ref.shape[0]


def attention_kernel(blocks, parts, rows, chips_ref, *refs):
    n1_refs, refs = refs[:blocks], refs[blocks:]
    bias_ref, cos_ref, sin_ref, key_place_ref, place_ref, start_ref, *refs = refs
    shards, refs = refs[:parts], refs[parts:]
    qkv_ref, o_ref, lse_ref, *out_refs, weight_ref, weights, sems, out_sem = refs
    length = qkv_ref.shape[0]
    copies = [
        pltpu.make_async_copy(
            shards[i],
            weights.at[pl.ds(pl.multiple_of(chips_ref[i] * rows, rows), rows), :],
            sems.at[i],
        )
        for i in range(parts)
    ]
    for copy in copies:
        copy.start()
    for copy in copies:
        copy.wait()
    save = pltpu.make_async_copy(weights, weight_ref, out_sem)
    save.start()
    for at, ref in rows_from(n1_refs):
        projected = dot_ab(ref[...], weights[:, :QKV_COLS]) + bias_ref[...]
        cos_both, sin_both = cos_ref[at, :], sin_ref[at, :]
        for j in range(HEADS + 1):
            cols = slice(j * HEAD_WIDTH, (j + 1) * HEAD_WIDTH)
            qkv_ref[at, cols] = turn_halves(projected[:, cols], cos_both, sin_both).astype(BF)
        cols = slice(Q_COLS + HEAD_WIDTH, QKV_COLS)
        qkv_ref[at, cols] = projected[:, cols].astype(BF)
    keys = qkv_ref[:, Q_COLS : Q_COLS + HEAD_WIDTH]
    values_t = qkv_ref[:, Q_COLS + HEAD_WIDTH : QKV_COLS].T
    lse_ref[...] = jnp.zeros_like(lse_ref)
    key_place = key_place_ref[...]
    for at in range(0, length, TILE):
        block = slice(at, at + TILE)
        place, start = place_ref[:, block], start_ref[:, block]
        for h in range(HEADS):
            cols = slice(h * HEAD_WIDTH, (h + 1) * HEAD_WIDTH)
            scores = scores_t(keys, qkv_ref[block, cols], key_place, place, start)
            top = jnp.max(scores, axis=0, keepdims=True)
            weights_exp = jnp.exp(scores - top)
            total = jnp.sum(weights_exp, axis=0, keepdims=True)
            lse_ref[h : h + 1, block] = top + jnp.log(total)
            prob = (weights_exp * (1.0 / total)).astype(BF)
            o_ref[block, cols] = dot_ab(values_t, prob).astype(BF).T
    for at, ref in rows_from(out_refs):
        ref[...] = dot_abt(o_ref[at, :], weights[:, QKV_COLS:]).astype(BF)
    save.wait()


def documents_kernel(where_ref, ids_ref, other_ref, frequency_ref, angle_ref, key_place_ref, place_ref, start_ref):
    core, place_x = where_ref[0], where_ref[1]
    one = ids_ref.shape[1]

    def in_order(ref):
        rows = [ref[k : k + 1, :] for k in range(2)]
        return [
            jnp.where(place_x == 0, rows[0], rows[1]),
            jnp.where(place_x == 0, rows[1], rows[0]),
        ]

    ids = jnp.concatenate(in_order(ids_ref) + in_order(other_ref), axis=1)
    index = lax.broadcasted_iota(jnp.int32, (1, 4 * one), 1)
    block = index // one
    mine = core * 2 + place_x
    place = jnp.bitwise_xor(mine, block) * one + index - block * one

    def column(row):
        return jnp.broadcast_to(row.astype(F32), (8, 4 * one)).T[:, :1]

    ids_col, place_col = column(ids), column(place)
    ids_row, place_row = ids.astype(F32), place.astype(F32)
    start_row = jnp.min(
        jnp.where(ids_col == ids_row, place_col, 4.0 * one), axis=0, keepdims=True
    )
    place_ref[...] = place
    start_ref[...] = start_row.astype(jnp.int32)
    key_place_ref[...] = place_col.astype(jnp.int32)
    angle_ref[...] = column(place_row - start_row) * frequency_ref[...]


def documents(core, place_x, ids, other_ids):
    one = ids.shape[0] // 2
    exponent = np.arange(0, HEAD_WIDTH, 2, dtype=np.float32) / np.float32(HEAD_WIDTH)
    frequency = np.float32(1.0) / np.float32(ROPE_BASE) ** exponent
    return pl.pallas_call(
        documents_kernel,
        grid_spec=pltpu.PrefetchScalarGridSpec(
            num_scalar_prefetch=1,
            grid=(),
            in_specs=[WHOLE] * 3,
            out_specs=[WHOLE] * 4,
        ),
        out_shape=[
            jax.ShapeDtypeStruct((4 * one, HEAD_WIDTH), F32),
            jax.ShapeDtypeStruct((4 * one, 1), jnp.int32),
            jax.ShapeDtypeStruct((1, 4 * one), jnp.int32),
            jax.ShapeDtypeStruct((1, 4 * one), jnp.int32),
        ],
        compiler_params=pltpu.CompilerParams(vmem_limit_bytes=VMEM_LIMIT),
        cost_estimate=cost(flops=2**20, bytes_accessed=2**20, transcendentals=0),
        name="documents",
    )(
        jnp.stack([core, place_x]).astype(jnp.int32),
        ids.reshape(2, one),
        other_ids.reshape(2, one),
        jnp.asarray(np.concatenate([frequency, frequency])[None]),
    )


def four_shapes(rows):
    return [jax.ShapeDtypeStruct((r, D), BF) for r in (rows, rows // 2, rows // 2) * 2]


def attention(chips, n1, bias, tables, shards):
    length = tables[0].shape[0]
    parts = len(shards)
    rows = shards[0].shape[0]
    return pl.pallas_call(
        functools.partial(attention_kernel, len(n1), parts, rows),
        grid_spec=pltpu.PrefetchScalarGridSpec(
            num_scalar_prefetch=1,
            grid=(),
            in_specs=[WHOLE] * (len(n1) + 6) + [ANYWHERE] * parts,
            out_specs=[WHOLE] * 9 + [ANYWHERE],
            scratch_shapes=[
                pltpu.VMEM((D, ATT_COLS), BF),
                pltpu.SemaphoreType.DMA((parts,)),
                pltpu.SemaphoreType.DMA,
            ],
        ),
        out_shape=[
            jax.ShapeDtypeStruct((length, QKV_COLS), BF),
            jax.ShapeDtypeStruct((length, Q_COLS), BF),
            jax.ShapeDtypeStruct((8, length), F32),
            *four_shapes(length // 4),
            jax.ShapeDtypeStruct((D, ATT_COLS), BF),
        ],
        compiler_params=pltpu.CompilerParams(vmem_limit_bytes=VMEM_LIMIT),
        cost_estimate=cost(
            flops=2 * length * D * ATT_COLS + 4 * HEADS * length * length * HEAD_WIDTH,
            bytes_accessed=16 * 2**20,
            transcendentals=HEADS * length * length,
        ),
        name="attention",
    )(chips, *n1, bias, *tables, *shards)


def attention_back_kernel(das, n1s, count, rows, chips_ref, *refs):
    da_refs, n1_refs, refs = refs[:das], refs[das : das + n1s], refs[das + n1s :]
    qkv_ref, o_ref, lse_ref, weight_ref, *refs = refs
    cos_ref, sin_ref, key_place_ref, place_ref, start_ref, *refs = refs
    dqkv_ref, bias_ref, *refs = refs
    dn1_refs, block_refs, (mixed, left_t, grads) = refs[:6], refs[6:10], refs[10:]
    length = qkv_ref.shape[0]
    scale = 1.0 / math.sqrt(HEAD_WIDTH)
    for at, ref in rows_from(da_refs):
        mixed[at, :] = dot_ab(ref[...], weight_ref[:, QKV_COLS:]).astype(BF)
    key_cols = slice(Q_COLS, Q_COLS + HEAD_WIDTH)
    value_cols = slice(Q_COLS + HEAD_WIDTH, QKV_COLS)
    keys, values = qkv_ref[:, key_cols], qkv_ref[:, value_cols]
    keys_t = keys.T
    key_place = key_place_ref[...]
    keys_grad = jnp.zeros((length, HEAD_WIDTH), F32)
    values_grad = jnp.zeros((length, HEAD_WIDTH), F32)
    for at in range(0, length, TILE):
        block = slice(at, at + TILE)
        place, start = place_ref[:, block], start_ref[:, block]
        for h in range(HEADS):
            cols = slice(h * HEAD_WIDTH, (h + 1) * HEAD_WIDTH)
            queries, up = qkv_ref[block, cols], mixed[block, cols]
            scores = scores_t(keys, queries, key_place, place, start)
            prob = jnp.exp(scores - lse_ref[h : h + 1, block])
            prob_grad = dot_abt(values, up)
            inner = jnp.sum(prob * prob_grad, axis=0, keepdims=True)
            score_grad = (prob * (prob_grad - inner)).astype(BF)
            values_grad += dot_ab(prob.astype(BF), up)
            keys_grad += dot_ab(score_grad, queries)
            query_grad = dot_ab(keys_t, score_grad).T * scale
            dqkv_ref[block, cols] = turn_halves(
                query_grad, cos_ref[block, :], -sin_ref[block, :]
            ).astype(BF)
    dqkv_ref[:, key_cols] = turn_halves(keys_grad * scale, cos_ref[...], -sin_ref[...]).astype(BF)
    dqkv_ref[:, value_cols] = values_grad.astype(BF)
    bias_ref[...] = jnp.sum(dqkv_ref[...].astype(F32), axis=0, keepdims=True)
    for cols, left_refs, right_ref in (
        (slice(0, QKV_COLS), n1_refs, dqkv_ref),
        (slice(QKV_COLS, ATT_COLS), da_refs, o_ref),
    ):
        for at, ref in rows_from(left_refs):
            left_t[:, at] = ref[...].T
        grads[:, :, cols] = (
            dot_ab(left_t[...], right_ref[...]).astype(BF).reshape(4 * count, rows, -1)
        )
    at = 0
    for ref in block_refs:
        for k in range(ref.shape[0]):
            ref[k] = grads[chips_ref[at]]
            at += 1
    for at, ref in rows_from(dn1_refs):
        ref[...] = dot_abt(dqkv_ref[at, :], weight_ref[:, :QKV_COLS]).astype(BF)


def attention_back(chips, da, n1, qkv, o, lse, weight, tables):
    length = qkv.shape[0]
    count = chips.shape[0] // 4
    rows = D // (4 * count)
    blocks = [
        jax.ShapeDtypeStruct((2 * k, rows, ATT_COLS), BF) for k in (count - 1, 1, count - 1, 1)
    ]
    return pl.pallas_call(
        functools.partial(attention_back_kernel, len(da), len(n1), count, rows),
        grid_spec=pltpu.PrefetchScalarGridSpec(
            num_scalar_prefetch=1,
            grid=(),
            in_specs=[WHOLE] * (len(da) + len(n1) + 9),
            out_specs=[WHOLE] * 12,
            scratch_shapes=[
                pltpu.VMEM((length, Q_COLS), BF),
                pltpu.VMEM((D, length), BF),
                pltpu.VMEM((4 * count, rows, ATT_COLS), BF),
            ],
        ),
        out_shape=[
            jax.ShapeDtypeStruct((length, QKV_COLS), BF),
            jax.ShapeDtypeStruct((1, QKV_COLS), F32),
            *four_shapes(length // 4),
            *blocks,
        ],
        compiler_params=pltpu.CompilerParams(vmem_limit_bytes=VMEM_LIMIT),
        cost_estimate=cost(
            flops=2 * length * D * 2 * ATT_COLS + 10 * HEADS * length * length * HEAD_WIDTH,
            bytes_accessed=24 * 2**20,
            transcendentals=HEADS * length * length,
        ),
        name="attention_back",
    )(chips, *da, *n1, qkv, o, lse, weight, *tables)


def feed_forward_kernel(whole, split, rows, chips_ref, *refs):
    n2_refs, dy_refs, refs = refs[:6], refs[6:12], refs[12:]
    pieces, refs = refs[: whole + 2 * split], refs[whole + 2 * split :]
    dn2_refs, refs = refs[:8], refs[8:]
    u_ref, dgate_ref, dup_ref, n2_t_ref, dy_t_ref, down_ref, *refs = refs
    gu_w, d_w, tiles, tile_sems, sems, out_sem = refs
    step = pl.program_id(0)
    steps = pl.num_programs(0)
    one = tiles.shape[2]

    def copies():
        for i in range(whole + split):
            at = pl.ds(pl.multiple_of(chips_ref[i] * rows, rows), rows)
            for j in range(3):
                if i < whole or j < 2:
                    here = pieces[i].at[j]
                else:
                    here = pieces[i + split]
                if j < 2:
                    there = gu_w.at[at, pl.ds(j * FF_OWN, FF_OWN)]
                else:
                    there = d_w.at[at, :]
                yield pltpu.make_async_copy(here, there, sems.at[i, j])

    def tile_copies(j):
        part, row = divmod(j, 4)
        ref, at = ((0, 0), (1, 0), (1, one), (2, 0))[row]
        for k, taken in enumerate((n2_refs, dy_refs)):
            yield pltpu.make_async_copy(
                taken[3 * part + ref].at[pl.ds(at, one), :],
                tiles.at[j % 2, k],
                tile_sems.at[j % 2, k],
            )

    save = pltpu.make_async_copy(d_w, down_ref, out_sem)

    @pl.when(step == 0)
    def _():
        for copy in copies():
            copy.start()
        for copy in tile_copies(0):
            copy.start()
        for copy in copies():
            copy.wait()
        save.start()

    for j in range(8):

        @pl.when(step == j)
        def _(j=j):
            if j < 7:
                for copy in tile_copies(j + 1):
                    copy.start()
            for copy in tile_copies(j):
                copy.wait()

    n2, dy = tiles[step % 2, 0], tiles[step % 2, 1]
    n2_t_ref[...] = n2.T
    dy_t_ref[...] = dy.T
    gate_up = dot_ab(n2, gu_w[...])
    du = dot_ab(dy, d_w[...])
    gate, up = gate_up[:, :FF_OWN], gate_up[:, FF_OWN:]
    sig = jax.nn.sigmoid(gate)
    silu = gate * sig
    u_ref[...] = (silu * up).astype(BF)
    dup = (du * silu).astype(BF)
    dgate = (du * up * sig * (1.0 + gate * (1.0 - sig))).astype(BF)
    dup_ref[...] = dup
    dgate_ref[...] = dgate
    dn2 = dot_abt(jnp.concatenate([dgate, dup], axis=1), gu_w[...]).astype(BF)
    for j in range(8):

        @pl.when(step == j)
        def _(j=j):
            dn2_refs[j][...] = dn2

    @pl.when(step == steps - 1)
    def _():
        save.wait()


def feed_forward(chips, n2, dy, whole, split):
    rows = whole[0].shape[1]
    one = n2[0].shape[0]
    length = 8 * one
    tile = lambda width: pl.BlockSpec((one, width), lambda i, c: (i, 0))
    turned = pl.BlockSpec((D, one), lambda i, c: (0, i))
    kept = pl.BlockSpec((one, D), lambda i, c: (0, 0))
    parts = len(whole) + len(split)
    return pl.pallas_call(
        functools.partial(feed_forward_kernel, len(whole), len(split), rows),
        grid_spec=pltpu.PrefetchScalarGridSpec(
            num_scalar_prefetch=1,
            grid=(8,),
            in_specs=[ANYWHERE] * (12 + len(whole) + 2 * len(split)),
            out_specs=[kept] * 8 + [tile(FF_OWN)] * 3 + [turned, turned, ANYWHERE],
            scratch_shapes=[
                pltpu.VMEM((D, 2 * FF_OWN), BF),
                pltpu.VMEM((D, FF_OWN), BF),
                pltpu.VMEM((2, 2, one, D), BF),
                pltpu.SemaphoreType.DMA((2, 2)),
                pltpu.SemaphoreType.DMA((parts, 3)),
                pltpu.SemaphoreType.DMA,
            ],
        ),
        out_shape=[jax.ShapeDtypeStruct((one, D), BF)] * 8
        + [jax.ShapeDtypeStruct((length, FF_OWN), BF)] * 3
        + [jax.ShapeDtypeStruct((D, length), BF)] * 2
        + [jax.ShapeDtypeStruct((D, FF_OWN), BF)],
        compiler_params=pltpu.CompilerParams(vmem_limit_bytes=VMEM_LIMIT),
        cost_estimate=cost(
            flops=2 * 5 * length * D * FF_OWN,
            bytes_accessed=60 * 2**20,
            transcendentals=length * FF_OWN,
        ),
        name="feed_forward",
    )(chips, *n2, *dy, *whole, *[gu for gu, _ in split], *[d for _, d in split])


def weight_grad_kernel(rows, place_ref, left_ref, right_ref, *refs):
    keep_ref, send_ref, total = refs
    width = right_ref.shape[1]
    for at in range(0, width, 256):
        to = min(at + 256, width)
        total[:, :, at:to] = dot_ab(left_ref[...], right_ref[:, at:to]).reshape(
            4, rows, to - at
        )
    lo, yy = place_ref[1], place_ref[2]
    for k in range(2):
        row = jnp.where(lo == 0, k, 1 - k) * 2
        keep_ref[0, k] = total[row + yy].astype(BF)
        send_ref[0, k] = total[row + 1 - yy].astype(BF)


def weight_grad(place, left, right):
    count = lax.axis_size("hi")
    length, width = right.shape
    rows = left.shape[0] // (4 * count)
    block = pl.BlockSpec((1, 2, rows, width), lambda i, p: (i, 0, 0, 0))
    out = jax.ShapeDtypeStruct((count, 2, rows, width), BF)
    return pl.pallas_call(
        functools.partial(weight_grad_kernel, rows),
        grid_spec=pltpu.PrefetchScalarGridSpec(
            num_scalar_prefetch=1,
            grid=(count,),
            in_specs=[
                pl.BlockSpec((4 * rows, length), lambda i, p: (lax.rem(i + p[0], count), 0)),
                pl.BlockSpec((length, width), lambda i, p: (0, 0)),
            ],
            out_specs=[block] * 2,
            scratch_shapes=[pltpu.VMEM((4, rows, width), F32)],
        ),
        out_shape=[out] * 2,
        compiler_params=pltpu.CompilerParams(vmem_limit_bytes=VMEM_LIMIT),
        cost_estimate=cost(
            flops=2 * length * D * width, bytes_accessed=16 * 2**20, transcendentals=0
        ),
        name="weight_grad",
    )(place, left, right)


def down_kernel(left_ref, right_ref, *out_refs):
    step = pl.program_id(0)
    product = dot_abt(left_ref[...], right_ref[...]).astype(BF)
    for k, ref in enumerate(out_refs):

        @pl.when((step % 2 == k % 2) & (step // 4 == k // 2))
        def _(ref=ref):
            ref[...] = product


def down(left, right):
    length, width = left.shape
    one = length // 8
    parts = [
        pl.BlockSpec((one, D), lambda i, j=j: (jnp.clip((i - j) // 2, 0, 1), 0)) for j in (0, 0, 4, 4)
    ]
    return pl.pallas_call(
        down_kernel,
        grid=(8,),
        in_specs=[
            pl.BlockSpec((one, width), lambda i: (i, 0)),
            pl.BlockSpec((D, width), lambda i: (0, 0)),
        ],
        out_specs=parts,
        out_shape=[jax.ShapeDtypeStruct((2 * one, D), BF)] * 4,
        compiler_params=pltpu.CompilerParams(vmem_limit_bytes=VMEM_LIMIT),
        cost_estimate=cost(
            flops=2 * length * D * width, bytes_accessed=14 * 2**20, transcendentals=0
        ),
        name="down",
    )(left, right)


def total_of(*parts):
    return sum(part.astype(F32) for part in parts)


class EightSum:
    def __init__(self, parts):
        self.keep = parts[:4]
        self.core = [None] * 4
        for k in (3, 1, 2, 0):
            self.core[k] = swap(parts[4 + k], "core")
        self.half = parts[0].shape[0] // 2

    def second(self, order):
        self.core = order.done(self.core)
        half = self.half
        both, by_x, by_lo = [total_of(self.keep[k], self.core[k]) for k in (3, 1, 2)]
        self.to_lo = swap(both[:half].astype(BF), "tensor")
        self.to_x = swap(both[half:].astype(BF), "lo")
        self.x_first = swap(by_x[:half].astype(BF), "tensor")
        self.lo_second = swap(by_lo[half:].astype(BF), "lo")
        self.by_x, self.by_lo = by_x[half:], by_lo[:half]

    def third(self, order):
        to_lo, to_x, self.x_first, self.lo_second = order.done(
            (self.to_lo, self.to_x, self.x_first, self.lo_second)
        )
        self.x_second = swap(total_of(self.by_x, to_x).astype(BF), "tensor")
        self.lo_first = swap(total_of(self.by_lo, to_lo).astype(BF), "lo")

    def total(self, order):
        x_second, lo_first = order.done((self.x_second, self.lo_first))
        return (
            total_of(self.keep[0], self.core[0])
            + jnp.concatenate([self.x_first, x_second], axis=0).astype(F32)
            + jnp.concatenate([lo_first, self.lo_second], axis=0).astype(F32)
        )


class BranchSum:
    def __init__(self, near, by_x, core_near, core_by_x):
        self.near, self.by_x = near, by_x
        self.core = swap(core_by_x, "core"), swap(core_near, "core")

    def along_x(self, order):
        by_x, near = order.done(self.core)
        self.near = total_of(self.near, near)
        self.x = swap(total_of(self.by_x, by_x).astype(BF), "tensor")

    def along_lo(self, order):
        total = self.near + order.done(self.x).astype(F32)
        half = total.shape[0] // 2
        self.own = total[:half]
        self.lo = swap(total[half:].astype(BF), "lo")

    def arrived(self, order):
        self.lo = order.done(self.lo)

    def total(self):
        return self.own + self.lo.astype(F32)


class FourSum:
    def __init__(self, own, first, second, core_own, core_first, core_second):
        self.own, self.x = own, (first, second)
        self.core_x = swap(core_first, "core"), swap(core_second, "core")
        self.core_own = swap(core_own, "core")

    def second(self, order):
        core_x = order.done(self.core_x)
        by_x = [total_of(*pair).astype(BF) for pair in zip(self.x, core_x)]
        self.x = [swap(part, "tensor") for part in by_x]
        order.mark = by_x

    def total(self, order):
        self.core_own = order.done(self.core_own)
        x = order.done(self.x)
        return total_of(self.own, self.core_own, jnp.concatenate(x, axis=0))


class GradSum:
    def __init__(self, keep, send):
        self.keep = keep
        self.other = swap(send, "yy")

    def across(self, order, by_gather):
        self.other = order.done(self.other)
        count = lax.axis_size("hi")
        far = [total_of(self.keep[k], self.other[k]).astype(BF) for k in range(1, count)]
        if by_gather:
            self.every = [lax.all_gather(part, "hi") for part in far]
        else:
            self.every = None
            self.far = [turn(part, "hi", k + 1) for k, part in enumerate(far)]

    def arrived(self, order):
        if self.every is None:
            self.far = order.done(self.far)
        else:
            every = order.done(self.every)
            self.far = [others_of(part)[k] for k, part in enumerate(every)]

    def total(self):
        total = self.keep[0].astype(F32) + self.other[0].astype(F32)
        for far in self.far:
            total = total + far.astype(F32)
        return total


def body(
    tokens,
    cotangent,
    segments,
    small_params,
    small_first,
    small_second,
    qkv_weight,
    qkv_first,
    qkv_second,
    out_weight,
    out_first,
    out_second,
    gateup_weight,
    gateup_first,
    gateup_second,
    down_weight,
    down_first,
    down_second,
):
    hi_count = lax.axis_size("hi")
    hi, lo, yy = lax.axis_index("hi"), lax.axis_index("lo"), lax.axis_index("yy")
    core = lax.axis_index("core")
    place_x = lax.axis_index("tensor")
    own_rows = tokens.shape[0]
    shard_rows = qkv_weight.shape[0]
    gain_one = small_params[:D]
    gain_two = small_params[D : 2 * D]
    bias_all = small_params[2 * D :]
    q_at = place_x * (bias_all.shape[0] // 2) + core * Q_COLS
    kv_at = place_x * (bias_all.shape[0] // 2) + 2 * Q_COLS
    bias_local = jnp.concatenate(
        [
            lax.dynamic_slice_in_dim(bias_all, q_at, Q_COLS),
            lax.dynamic_slice_in_dim(bias_all, kv_at, 2 * HEAD_WIDTH),
        ]
    )

    order = Order()
    steps = range(1, hi_count)

    def both_cores(mine, other, axis):
        return jnp.where(
            core == 0,
            jnp.concatenate([mine, other], axis=axis),
            jnp.concatenate([other, mine], axis=axis),
        )

    other_ids = swap(segments, "core")
    qkv_low = qkv_weight.astype(BF)
    out_low = out_weight.astype(BF).T

    def attention_pack(which):
        return jnp.concatenate(
            [
                lax.dynamic_slice_in_dim(qkv_low, which * Q_COLS, Q_COLS, 1),
                qkv_low[:, 2 * Q_COLS :],
                lax.dynamic_slice_in_dim(out_low, which * Q_COLS, Q_COLS, 1),
            ],
            axis=1,
        )

    att_theirs = attention_pack(1 - core)
    att_core = swap(att_theirs, "core")
    order.mark = att_theirs
    rows_in = order.after(tokens).astype(F32)
    scale_one = rms_scale(rows_in)
    n1 = (rows_in * scale_one * gain_one).astype(BF)
    n1_x = swap(n1, "tensor")
    order.mark = n1
    att_shard = both_cores(attention_pack(core), order.done(att_core), 0)
    order.mark = att_shard
    att_hi = [turn(att_shard, "hi", k) for k in steps]
    att_yy = swap(att_shard, "yy")
    att_lo = swap(att_shard, "lo")

    gateup_in, down_in = order.after((gateup_weight, down_weight))
    ff_low = jnp.pad(
        jnp.concatenate([gateup_in.astype(BF), down_in.astype(BF).T[None]], axis=0),
        ((0, 0), (0, 0), (0, FF_PAD - FF_LOCAL)),
    )
    ff_mine = lax.dynamic_slice_in_dim(ff_low, core * FF_CORE, FF_CORE, 2)
    ff_theirs = lax.dynamic_slice_in_dim(ff_low, (1 - core) * FF_CORE, FF_CORE, 2)
    ff_core = swap(ff_theirs, "core")
    order.mark = ff_theirs

    ff_shard = both_cores(ff_mine, order.done(ff_core), 1)
    ff_own = lax.dynamic_slice_in_dim(ff_shard, lo * FF_OWN, FF_OWN, 2)
    ff_theirs = lax.dynamic_slice_in_dim(ff_shard, (1 - lo) * FF_OWN, FF_OWN, 2)
    order.mark = ff_theirs
    att_lo = order.done(att_lo)
    att_lo_yy = swap(att_lo, "yy")
    att_yy = order.done(att_yy)
    att_hi = order.done(att_hi)
    att_hi_lo = [swap(part, "lo") for part in att_hi]
    att_hi_yy = [swap(part, "yy") for part in att_hi]
    n1_core = swap(order.after(n1), "core")
    att_lo_yy = order.done(att_lo_yy)
    att_hi_lo = order.done(att_hi_lo)
    att_hi_lo_yy = [swap(part, "yy") for part in att_hi_lo]
    ff_lo = swap(order.after(ff_theirs), "lo")
    ff_hi = lax.all_gather(order.after(ff_own), "hi")
    n1_core = order.done(n1_core)
    other_ids = order.done(other_ids)
    angles, key_place, row_place, row_start = documents(core, place_x, segments, other_ids)
    sign = jnp.where(jnp.arange(HEAD_WIDTH) < HEAD_WIDTH // 2, -1.0, 1.0)
    tables = order.after((jnp.cos(angles), jnp.sin(angles) * sign, key_place, row_place, row_start))
    order.mark = tables[0]
    att_hi_yy = order.done(att_hi_yy)
    n1_x = order.done(n1_x)
    n1_core_x = swap(n1_x, "core")
    cot_x = swap(order.after(cotangent), "tensor")
    n1_core_x = order.done(n1_core_x)
    att_hi_lo_yy = order.done(att_hi_lo_yy)
    ff_yy = swap(order.after(ff_own), "yy")

    near_parts = [att_shard, att_lo]
    yy_parts = [att_yy, att_lo_yy]
    for k in range(hi_count - 1):
        near_parts += [att_hi[k], att_hi_lo[k]]
        yy_parts += [att_hi_yy[k], att_hi_lo_yy[k]]
    att_parts = near_parts + yy_parts
    n1_parts = order.after((n1, n1_x, n1_core, n1_core_x))
    qkv, attn_rows, lse, *out_parts, att_weight = attention(
        tree_order(-1), n1_parts, bias_local[None], tables, att_parts
    )
    order.mark = lse

    out = FourSum(*out_parts)
    half = own_rows // 2
    cot_x = order.done(cot_x)
    ff_lo = order.done(ff_lo)
    ff_lo_hi_gu = lax.all_gather(ff_lo[:2], "hi")
    ff_yy = order.done(ff_yy)
    ff_lo_yy = swap(ff_lo, "yy")
    out.second(order)
    ff_hi = others_of(order.done(ff_hi))
    order.mark = ff_hi
    residual = rows_in + out.total(order)
    scale_two = rms_scale(residual)
    n2 = (residual * scale_two * gain_two).astype(BF)
    n2_x_second, n2_lo_first = swap(n2[half:], "tensor"), swap(n2[:half], "lo")
    n2_x_first, n2_lo_second = swap(n2[:half], "tensor"), swap(n2[half:], "lo")
    order.mark = n2
    ff_lo_yy = order.done(ff_lo_yy)
    ff_hi_yy = [swap(order.after(part), "yy") for part in ff_hi]
    n2_x_second, n2_lo_first = order.done((n2_x_second, n2_lo_first))
    n2_both = swap(n2_lo_first, "tensor"), swap(n2_x_second, "lo")
    n2_x_first, n2_lo_second = order.done((n2_x_first, n2_lo_second))
    n2_near = jnp.concatenate([n2_x_first, n2_x_second, n2_lo_first, n2_lo_second])
    n2_core_near, n2_core = swap(n2_near, "core"), swap(n2, "core")
    ff_lo_hi_gu = others_of(order.done(ff_lo_hi_gu))
    n2_both = jnp.concatenate(order.done(n2_both))
    n2_core_near, n2_core = order.done((n2_core_near, n2_core))
    n2_core_both = swap(n2_both, "core")
    cot_lo = swap(order.after(cotangent), "lo")
    ff_lo_hi_yy_gu = [swap(order.after(part), "yy") for part in ff_lo_hi_gu]
    ff_lo_hi_d = [turn(order.after(ff_lo[2]), "hi", k) for k in steps]
    ff_hi_yy = order.done(ff_hi_yy)
    cot_lo = order.done(cot_lo)
    cot_both = swap(cot_lo[:half], "tensor"), swap(cot_x[half:], "lo")
    ff_lo_hi_d = order.done(ff_lo_hi_d)
    ff_lo_hi_yy_d = [swap(part, "yy") for part in ff_lo_hi_d]
    n2_core_both = order.done(n2_core_both)
    cot_both = order.done(cot_both)
    cot_parts = [cotangent, jnp.concatenate([cot_x, cot_lo]), jnp.concatenate(cot_both)]
    cot_parts += [swap(part, "core") for part in cot_parts]
    ff_lo_hi_yy_gu = order.done(ff_lo_hi_yy_gu)
    cot_parts = order.done(cot_parts)
    ff_lo_hi_yy_d = order.done(ff_lo_hi_yy_d)
    n2_parts = [n2, n2_near, n2_both, n2_core, n2_core_near, n2_core_both]

    whole = [ff_own, ff_lo, ff_yy, ff_lo_yy, *ff_hi, *ff_hi_yy]
    split = [*zip(ff_lo_hi_gu, ff_lo_hi_d), *zip(ff_lo_hi_yy_gu, ff_lo_hi_yy_d)]
    ff_chips = [chip_at(0, l, y) for y in (0, 1) for l in (0, 1)]
    ff_chips += [chip_at(-k, l, y) for l in (0, 1) for y in (0, 1) for k in steps]
    *dn2_parts, hidden, gate_grad, up_grad, n2_t, cot_t, w_down = feed_forward(
        jnp.stack(ff_chips).astype(jnp.int32), order.after(n2_parts), cot_parts, whole, split
    )
    order.mark = w_down

    place = jnp.stack([hi, lo, yy]).astype(jnp.int32)

    def grad_of(left, right):
        keep, send = weight_grad(place, order.after(left), right)
        order.mark = keep
        return GradSum(keep, send)

    ff_squares = 0.0
    rows_of = lambda value, which, axis: lax.dynamic_slice_in_dim(
        value, which * shard_rows, shard_rows, axis
    )

    def summed_up(grad):
        nonlocal ff_squares
        total = order.after(grad.total())
        ff_squares = ff_squares + jnp.sum(total * total)
        low = total.astype(BF)
        order.mark = low
        return low[0], swap(low[1], "lo")

    def own_rows_of(low, other):
        other = order.done(other)
        cols = jnp.where(
            lo == 0,
            jnp.concatenate([low, other], axis=1),
            jnp.concatenate([other, low], axis=1),
        )
        theirs = rows_of(cols, 1 - core, 0)
        order.mark = theirs
        return rows_of(cols, core, 0), swap(theirs, "core")

    dn2 = EightSum(dn2_parts)
    d_sum = grad_of(cot_t, hidden)
    dn2.second(order)
    g_sum = grad_of(n2_t, gate_grad)
    dn2.third(order)
    u_sum = grad_of(n2_t, up_grad)
    d_sum.across(order, True)
    norm_two_in, gain_two_grad = norm_backward(residual, scale_two, gain_two, dn2.total(order))
    residual_grad = cotangent.astype(F32) + norm_two_in
    da = residual_grad.astype(BF)
    da_x = [swap(da[:half], "tensor"), swap(da[half:], "tensor")]
    da_core = swap(da, "core")
    order.mark = da
    branch_parts = down(*order.after((hidden, w_down)))
    order.mark = branch_parts[0]
    branch = BranchSum(*branch_parts)
    da_x = order.done(da_x)
    da_core_x = [swap(part, "core") for part in da_x]
    da_core, da_core_x = order.done((da_core, da_core_x))

    _, bias_grad, *parts = attention_back(
        sum_order(),
        order.after((da, *da_x, da_core, *da_core_x)),
        n1_parts,
        qkv,
        attn_rows,
        lse,
        att_weight,
        tables,
    )
    order.mark = bias_grad
    d_sum.arrived(order)
    g_sum.across(order, True)
    dn1 = FourSum(*parts[:6])
    att = ChipSum(*parts[6:])
    dn1.second(order)
    norm_one_in, gain_one_grad = norm_backward(rows_in, scale_one, gain_one, dn1.total(order))
    u_sum.across(order, False)
    att.far_yy(order)
    bias_grad = order.after(bias_grad)[0]
    bias_slots = lax.dynamic_update_slice_in_dim(
        jnp.zeros_like(bias_all), bias_grad[:Q_COLS], q_at, 0
    )
    bias_slots = lax.dynamic_update_slice_in_dim(bias_slots, bias_grad[Q_COLS:], kv_at, 0)
    att.far_hi(order)
    branch.along_x(order)
    d_low, d_way = summed_up(d_sum)
    g_sum.arrived(order)
    g_low, g_way = summed_up(g_sum)
    att.near_yy(order)
    input_grad = residual_grad + norm_one_in
    branch.along_lo(order)
    u_sum.arrived(order)
    att_sum = att.total(order)
    att_low = att_sum.astype(BF)
    other_att = swap(rows_of(att_low, 1 - core, 0), "core")
    u_low, u_way = summed_up(u_sum)
    other_att = order.done(other_att)
    d_rows = own_rows_of(d_low, d_way)
    g_rows = own_rows_of(g_low, g_way)
    branch.arrived(order)

    own_att = rows_of(att_low, core, 0)
    first_att = jnp.where(core == 0, own_att, other_att).astype(F32)
    second_att = jnp.where(core == 0, other_att, own_att).astype(F32)
    kv_sum = first_att[:, Q_COLS:QKV_COLS] + second_att[:, Q_COLS:QKV_COLS]
    qkv_owned = jnp.concatenate([first_att[:, :Q_COLS], second_att[:, :Q_COLS], kv_sum], axis=1)
    out_owned = jnp.concatenate([first_att[:, QKV_COLS:], second_att[:, QKV_COLS:]], axis=1).T
    owned_squares = (
        jnp.sum(qkv_owned * qkv_owned) + jnp.sum(out_owned * out_owned) + ff_squares
    )
    summed = jnp.concatenate(
        [gain_one_grad, gain_two_grad, bias_slots, jnp.full((128,), owned_squares)]
    )
    summed = summed + order.done(swap(summed, "core"))
    summed = summed + order.done(swap(summed, "tensor"))
    summed = summed + order.done(swap(summed, "yy"))
    summed = summed + order.done(swap(summed, "lo"))
    step = 1
    while step < hi_count:
        moved = lax.ppermute(summed, "hi", [(i, i ^ step) for i in range(hi_count)])
        summed = summed + order.done(moved)
        step *= 2
    order.mark = summed
    u_rows = own_rows_of(u_low, u_way)
    block_out = (residual + order.after(branch.total())).astype(BF)

    def owned(rows):
        mine, other = rows
        return both_cores(mine, other, 1)[:, :FF_LOCAL].astype(F32)

    gateup_owned = jnp.stack([owned(g_rows), owned(u_rows)])
    down_owned = owned(d_rows).T
    small_grad = summed[:-128]
    squares = summed[-1] + jnp.sum(small_grad * small_grad)
    grad_norm = jnp.sqrt(squares)
    clip_factor = jnp.minimum(1.0, MAX_NORM / (grad_norm + 1e-06))
    new_small, new_small_first, new_small_second = adam_update(
        small_params, small_first, small_second, clip_factor * small_grad, 0.5, 0.0
    )
    new_qkv, new_qkv_first, new_qkv_second = adam_update(
        qkv_weight, qkv_first, qkv_second, clip_factor * qkv_owned, 2.0 / math.sqrt(D), WEIGHT_DECAY
    )
    new_out, new_out_first, new_out_second = adam_update(
        out_weight,
        out_first,
        out_second,
        clip_factor * out_owned,
        8.0 / math.sqrt(QUERY_HEADS * HEAD_WIDTH),
        WEIGHT_DECAY,
    )
    new_gateup, new_gateup_first, new_gateup_second = adam_update(
        gateup_weight,
        gateup_first,
        gateup_second,
        clip_factor * gateup_owned,
        2.0 / math.sqrt(D),
        WEIGHT_DECAY,
    )
    new_down, new_down_first, new_down_second = adam_update(
        down_weight,
        down_first,
        down_second,
        clip_factor * down_owned,
        3.0 / math.sqrt(FF),
        WEIGHT_DECAY,
    )
    return (
        block_out,
        input_grad,
        grad_norm,
        new_small,
        new_small_first,
        new_small_second,
        new_qkv,
        new_qkv_first,
        new_qkv_second,
        new_out,
        new_out_first,
        new_out_second,
        new_gateup,
        new_gateup_first,
        new_gateup_second,
        new_down,
        new_down_first,
        new_down_second,
    )


def solution(mesh):
    count = mesh.shape["dp"]
    fine = Mesh(
        mesh.devices.reshape(count // 8, 2, 2, 2, mesh.shape["tensor"]),
        CHIP + ("core", "tensor"),
    )
    dp = CHIP + ("core",)
    rows = P(dp + ("tensor",), None)
    by_rows = P(dp, "tensor")
    by_cols = P("tensor", dp)
    stacked = P(None, dp, "tensor")
    weights = (by_rows,) * 3 + (by_cols,) * 3 + (stacked,) * 3 + (by_cols,) * 3
    return jax.shard_map(
        body,
        mesh=fine,
        in_specs=(rows, rows, P(dp), P(), P(), P()) + weights,
        out_specs=(rows, rows, P(), P(), P(), P()) + weights,
        check_vma=False,
    )
```

```python
import functools
import math

import jax
import jax.numpy as jnp
import numpy as np
from jax import lax
from jax.experimental import pallas as pl
from jax.experimental.pallas import tpu as pltpu
from jax.sharding import Mesh
from jax.sharding import PartitionSpec as P

D = 1536
FF = 8960
QUERY_HEADS = 12
KEY_VALUE_HEADS = 2
HEAD_WIDTH = 128
STEP = 10

EPSILON = 1e-06
ROPE_BASE = 1000000.0
BETA_ONE = 0.9
BETA_TWO = 0.999
ADAM_EPS = 1e-08
WEIGHT_DECAY = 0.1
MAX_NORM = 1.0
NEGATIVE = -1e30

BF = jnp.bfloat16
F32 = jnp.float32
HEADS = 3
Q_COLS = HEADS * HEAD_WIDTH
QKV_COLS = Q_COLS + 2 * HEAD_WIDTH
ATT_COLS = QKV_COLS + Q_COLS
FF_LOCAL = FF // 2
FF_PAD = 4608
FF_CORE = FF_PAD // 2
FF_OWN = FF_PAD // 4
TILE = 256
VMEM_LIMIT = 60 * 2**20
CHIP = ("hi", "lo", "yy")


def dot_ab(a, b):
    return lax.dot_general(a, b, (((1,), (0,)), ((), ())), preferred_element_type=F32)


def dot_abt(a, b):
    return lax.dot_general(a, b, (((1,), (1,)), ((), ())), preferred_element_type=F32)


def dot_atb(a, b):
    return lax.dot_general(a, b, (((0,), (0,)), ((), ())), preferred_element_type=F32)


def rms_scale(inputs):
    return lax.rsqrt(jnp.mean(inputs * inputs, axis=-1, keepdims=True) + EPSILON)


def norm_backward(inputs, inv_rms, gain_vec, upstream):
    normed = inputs * inv_rms
    normed_grad = upstream * gain_vec
    input_part = inv_rms * (
        normed_grad - normed * jnp.mean(normed_grad * normed, axis=-1, keepdims=True)
    )
    return (input_part, jnp.sum(upstream * normed, axis=0))


def adam_update(weight, moment_one, moment_two, gradient, step_rate, decay_rate):
    first_new = BETA_ONE * moment_one + (1.0 - BETA_ONE) * gradient
    second_new = BETA_TWO * moment_two + (1.0 - BETA_TWO) * gradient * gradient
    corrected = first_new / (1.0 - BETA_ONE**STEP)
    spread = jnp.sqrt(second_new / (1.0 - BETA_TWO**STEP)) + ADAM_EPS
    return (
        weight * (1.0 - step_rate * decay_rate) - step_rate * corrected / spread,
        first_new,
        second_new,
    )


def swap(value, axis):
    return lax.ppermute(value, axis, [(0, 1), (1, 0)])


class Order:
    def __init__(self):
        self.mark = None

    def after(self, value):
        if self.mark is None:
            return value
        return lax.optimization_barrier((value, self.mark))[0]

    def done(self, value):
        value = self.after(value)
        self.mark = value
        return value


def chip_at(step, other_lo, other_yy):
    count = lax.axis_size("hi")
    hi = (lax.axis_index("hi") + step) % count
    return (hi * 2 + (lax.axis_index("lo") ^ other_lo)) * 2 + (lax.axis_index("yy") ^ other_yy)


def turn(value, axis, steps):
    count = lax.axis_size(axis)
    return lax.ppermute(value, axis, [(i, (i + steps) % count) for i in range(count)])


def others_of(every):
    count = lax.axis_size("hi")
    hi = lax.axis_index("hi")
    return [
        lax.dynamic_index_in_dim(every, (hi - k) % count, 0, keepdims=False)
        for k in range(1, count)
    ]


def tree_order(sign):
    steps = [(0, 0), (0, 1)] + [(k, l) for k in range(1, lax.axis_size("hi")) for l in (0, 1)]
    return jnp.stack([chip_at(sign * k, l, y) for y in (0, 1) for k, l in steps]).astype(jnp.int32)


def sum_order():
    steps = range(1, lax.axis_size("hi"))
    chips = [chip_at(k, l, y) for l in (1, 0) for ks in (steps, (0,)) for k in ks for y in (1, 0)]
    return jnp.stack(chips).astype(jnp.int32)


class ChipSum:
    def __init__(self, lo_far, lo_near, far, near):
        self.far, self.near, self.lo_near = far, near, lo_near
        self.lo_far = swap(lo_far, "lo")

    def far_yy(self, order):
        self.far = self.far.astype(F32) + order.done(self.lo_far).astype(F32)
        theirs = self.far[0::2].astype(BF)
        self.yy_far = swap(theirs, "yy")
        order.mark = theirs
        self.lo_near = swap(order.after(self.lo_near), "lo")

    def far_hi(self, order):
        far = (self.far[1::2] + order.done(self.yy_far).astype(F32)).astype(BF)
        self.hi = [turn(far[k - 1], "hi", k) for k in range(1, lax.axis_size("hi"))]
        order.mark = far

    def near_yy(self, order):
        self.near = self.near.astype(F32) + order.done(self.lo_near).astype(F32)
        theirs = self.near[0].astype(BF)
        self.yy_near = swap(theirs, "yy")
        order.mark = theirs

    def total(self, order):
        hi = order.done(self.hi)
        total = self.near[1] + order.done(self.yy_near).astype(F32)
        for part in hi:
            total = total + part.astype(F32)
        return total


def cost(flops, bytes_accessed, transcendentals):
    part = 4096
    return pl.CostEstimate(
        flops=flops // part,
        bytes_accessed=bytes_accessed // part,
        transcendentals=transcendentals // part,
    )


ANYWHERE = pl.BlockSpec(memory_space=pl.ANY)
WHOLE = pl.BlockSpec(memory_space=pltpu.VMEM)


def turn_halves(features, cos_both, sin_both):
    return features * cos_both + pltpu.roll(features, HEAD_WIDTH // 2, 1) * sin_both


def scores_t(keys, queries, key_place, place, start):
    scores = dot_abt(keys, queries) * (1.0 / math.sqrt(HEAD_WIDTH))
    return jnp.where((key_place <= place) & (key_place >= start), scores, NEGATIVE)


def rows_from(refs):
    begin = 0
    for ref in refs:
        yield slice(begin, begin + ref.shape[0]), ref
        begin += ref.shape[0]


def attention_kernel(blocks, parts, rows, chips_ref, *refs):
    n1_refs, refs = refs[:blocks], refs[blocks:]
    bias_ref, cos_ref, sin_ref, key_place_ref, place_ref, start_ref, *refs = refs
    shards, refs = refs[:parts], refs[parts:]
    qkv_ref, o_ref, lse_ref, *out_refs, weight_ref, weights, sems, out_sem = refs
    length = qkv_ref.shape[0]
    copies = [
        pltpu.make_async_copy(
            shards[i],
            weights.at[pl.ds(pl.multiple_of(chips_ref[i] * rows, rows), rows), :],
            sems.at[i],
        )
        for i in range(parts)
    ]
    for copy in copies:
        copy.start()
    for copy in copies:
        copy.wait()
    save = pltpu.make_async_copy(weights, weight_ref, out_sem)
    save.start()
    for at, ref in rows_from(n1_refs):
        projected = dot_ab(ref[...], weights[:, :QKV_COLS]) + bias_ref[...]
        cos_both, sin_both = cos_ref[at, :], sin_ref[at, :]
        for j in range(HEADS + 1):
            cols = slice(j * HEAD_WIDTH, (j + 1) * HEAD_WIDTH)
            qkv_ref[at, cols] = turn_halves(projected[:, cols], cos_both, sin_both).astype(BF)
        cols = slice(Q_COLS + HEAD_WIDTH, QKV_COLS)
        qkv_ref[at, cols] = projected[:, cols].astype(BF)
    keys = qkv_ref[:, Q_COLS : Q_COLS + HEAD_WIDTH]
    values_t = qkv_ref[:, Q_COLS + HEAD_WIDTH : QKV_COLS].T
    lse_ref[...] = jnp.zeros_like(lse_ref)
    key_place = key_place_ref[...]
    for at in range(0, length, TILE):
        block = slice(at, at + TILE)
        place, start = place_ref[:, block], start_ref[:, block]
        for h in range(HEADS):
            cols = slice(h * HEAD_WIDTH, (h + 1) * HEAD_WIDTH)
            scores = scores_t(keys, qkv_ref[block, cols], key_place, place, start)
            top = jnp.max(scores, axis=0, keepdims=True)
            weights_exp = jnp.exp(scores - top)
            total = jnp.sum(weights_exp, axis=0, keepdims=True)
            lse_ref[h : h + 1, block] = top + jnp.log(total)
            prob = (weights_exp * (1.0 / total)).astype(BF)
            o_ref[block, cols] = dot_ab(values_t, prob).astype(BF).T
    for at, ref in rows_from(out_refs):
        ref[...] = dot_abt(o_ref[at, :], weights[:, QKV_COLS:]).astype(BF)
    save.wait()


def documents_kernel(where_ref, ids_ref, other_ref, frequency_ref, angle_ref, key_place_ref, place_ref, start_ref):
    core, place_x = where_ref[0], where_ref[1]
    one = ids_ref.shape[1]

    def in_order(ref):
        rows = [ref[k : k + 1, :] for k in range(2)]
        return [
            jnp.where(place_x == 0, rows[0], rows[1]),
            jnp.where(place_x == 0, rows[1], rows[0]),
        ]

    ids = jnp.concatenate(in_order(ids_ref) + in_order(other_ref), axis=1)
    index = lax.broadcasted_iota(jnp.int32, (1, 4 * one), 1)
    block = index // one
    mine = core * 2 + place_x
    place = jnp.bitwise_xor(mine, block) * one + index - block * one

    def column(row):
        return jnp.broadcast_to(row.astype(F32), (8, 4 * one)).T[:, :1]

    ids_col, place_col = column(ids), column(place)
    ids_row, place_row = ids.astype(F32), place.astype(F32)
    start_row = jnp.min(
        jnp.where(ids_col == ids_row, place_col, 4.0 * one), axis=0, keepdims=True
    )
    place_ref[...] = place
    start_ref[...] = start_row.astype(jnp.int32)
    key_place_ref[...] = place_col.astype(jnp.int32)
    angle_ref[...] = column(place_row - start_row) * frequency_ref[...]


def documents(core, place_x, ids, other_ids):
    one = ids.shape[0] // 2
    exponent = np.arange(0, HEAD_WIDTH, 2, dtype=np.float32) / np.float32(HEAD_WIDTH)
    frequency = np.float32(1.0) / np.float32(ROPE_BASE) ** exponent
    return pl.pallas_call(
        documents_kernel,
        grid_spec=pltpu.PrefetchScalarGridSpec(
            num_scalar_prefetch=1,
            grid=(),
            in_specs=[WHOLE] * 3,
            out_specs=[WHOLE] * 4,
        ),
        out_shape=[
            jax.ShapeDtypeStruct((4 * one, HEAD_WIDTH), F32),
            jax.ShapeDtypeStruct((4 * one, 1), jnp.int32),
            jax.ShapeDtypeStruct((1, 4 * one), jnp.int32),
            jax.ShapeDtypeStruct((1, 4 * one), jnp.int32),
        ],
        compiler_params=pltpu.CompilerParams(vmem_limit_bytes=VMEM_LIMIT),
        cost_estimate=cost(flops=2**20, bytes_accessed=2**20, transcendentals=0),
        name="documents",
    )(
        jnp.stack([core, place_x]).astype(jnp.int32),
        ids.reshape(2, one),
        other_ids.reshape(2, one),
        jnp.asarray(np.concatenate([frequency, frequency])[None]),
    )


def four_shapes(rows):
    return [jax.ShapeDtypeStruct((r, D), BF) for r in (rows, rows // 2, rows // 2) * 2]


def attention(chips, n1, bias, tables, shards):
    length = tables[0].shape[0]
    parts = len(shards)
    rows = shards[0].shape[0]
    return pl.pallas_call(
        functools.partial(attention_kernel, len(n1), parts, rows),
        grid_spec=pltpu.PrefetchScalarGridSpec(
            num_scalar_prefetch=1,
            grid=(),
            in_specs=[WHOLE] * (len(n1) + 6) + [ANYWHERE] * parts,
            out_specs=[WHOLE] * 9 + [ANYWHERE],
            scratch_shapes=[
                pltpu.VMEM((D, ATT_COLS), BF),
                pltpu.SemaphoreType.DMA((parts,)),
                pltpu.SemaphoreType.DMA,
            ],
        ),
        out_shape=[
            jax.ShapeDtypeStruct((length, QKV_COLS), BF),
            jax.ShapeDtypeStruct((length, Q_COLS), BF),
            jax.ShapeDtypeStruct((8, length), F32),
            *four_shapes(length // 4),
            jax.ShapeDtypeStruct((D, ATT_COLS), BF),
        ],
        compiler_params=pltpu.CompilerParams(vmem_limit_bytes=VMEM_LIMIT),
        cost_estimate=cost(
            flops=2 * length * D * ATT_COLS + 4 * HEADS * length * length * HEAD_WIDTH,
            bytes_accessed=16 * 2**20,
            transcendentals=HEADS * length * length,
        ),
        name="attention",
    )(chips, *n1, bias, *tables, *shards)


def attention_back_kernel(das, n1s, count, rows, chips_ref, *refs):
    da_refs, n1_refs, refs = refs[:das], refs[das : das + n1s], refs[das + n1s :]
    qkv_ref, o_ref, lse_ref, weight_ref, *refs = refs
    cos_ref, sin_ref, key_place_ref, place_ref, start_ref, *refs = refs
    dqkv_ref, bias_ref, *refs = refs
    dn1_refs, block_refs, (mixed, left_t, grads) = refs[:6], refs[6:10], refs[10:]
    length = qkv_ref.shape[0]
    scale = 1.0 / math.sqrt(HEAD_WIDTH)
    for at, ref in rows_from(da_refs):
        mixed[at, :] = dot_ab(ref[...], weight_ref[:, QKV_COLS:]).astype(BF)
    key_cols = slice(Q_COLS, Q_COLS + HEAD_WIDTH)
    value_cols = slice(Q_COLS + HEAD_WIDTH, QKV_COLS)
    keys, values = qkv_ref[:, key_cols], qkv_ref[:, value_cols]
    keys_t = keys.T
    key_place = key_place_ref[...]
    keys_grad = jnp.zeros((length, HEAD_WIDTH), F32)
    values_grad = jnp.zeros((length, HEAD_WIDTH), F32)
    for at in range(0, length, TILE):
        block = slice(at, at + TILE)
        place, start = place_ref[:, block], start_ref[:, block]
        for h in range(HEADS):
            cols = slice(h * HEAD_WIDTH, (h + 1) * HEAD_WIDTH)
            queries, up = qkv_ref[block, cols], mixed[block, cols]
            scores = scores_t(keys, queries, key_place, place, start)
            prob = jnp.exp(scores - lse_ref[h : h + 1, block])
            prob_grad = dot_abt(values, up)
            inner = jnp.sum(prob * prob_grad, axis=0, keepdims=True)
            score_grad = (prob * (prob_grad - inner)).astype(BF)
            values_grad += dot_ab(prob.astype(BF), up)
            keys_grad += dot_ab(score_grad, queries)
            query_grad = dot_ab(keys_t, score_grad).T * scale
            dqkv_ref[block, cols] = turn_halves(
                query_grad, cos_ref[block, :], -sin_ref[block, :]
            ).astype(BF)
    dqkv_ref[:, key_cols] = turn_halves(keys_grad * scale, cos_ref[...], -sin_ref[...]).astype(BF)
    dqkv_ref[:, value_cols] = values_grad.astype(BF)
    bias_ref[...] = jnp.sum(dqkv_ref[...].astype(F32), axis=0, keepdims=True)
    for cols, left_refs, right_ref in (
        (slice(0, QKV_COLS), n1_refs, dqkv_ref),
        (slice(QKV_COLS, ATT_COLS), da_refs, o_ref),
    ):
        for at, ref in rows_from(left_refs):
            left_t[:, at] = ref[...].T
        grads[:, :, cols] = (
            dot_ab(left_t[...], right_ref[...]).astype(BF).reshape(4 * count, rows, -1)
        )
    at = 0
    for ref in block_refs:
        for k in range(ref.shape[0]):
            ref[k] = grads[chips_ref[at]]
            at += 1
    for at, ref in rows_from(dn1_refs):
        ref[...] = dot_abt(dqkv_ref[at, :], weight_ref[:, :QKV_COLS]).astype(BF)


def attention_back(chips, da, n1, qkv, o, lse, weight, tables):
    length = qkv.shape[0]
    count = chips.shape[0] // 4
    rows = D // (4 * count)
    blocks = [
        jax.ShapeDtypeStruct((2 * k, rows, ATT_COLS), BF) for k in (count - 1, 1, count - 1, 1)
    ]
    return pl.pallas_call(
        functools.partial(attention_back_kernel, len(da), len(n1), count, rows),
        grid_spec=pltpu.PrefetchScalarGridSpec(
            num_scalar_prefetch=1,
            grid=(),
            in_specs=[WHOLE] * (len(da) + len(n1) + 9),
            out_specs=[WHOLE] * 12,
            scratch_shapes=[
                pltpu.VMEM((length, Q_COLS), BF),
                pltpu.VMEM((D, length), BF),
                pltpu.VMEM((4 * count, rows, ATT_COLS), BF),
            ],
        ),
        out_shape=[
            jax.ShapeDtypeStruct((length, QKV_COLS), BF),
            jax.ShapeDtypeStruct((1, QKV_COLS), F32),
            *four_shapes(length // 4),
            *blocks,
        ],
        compiler_params=pltpu.CompilerParams(vmem_limit_bytes=VMEM_LIMIT),
        cost_estimate=cost(
            flops=2 * length * D * 2 * ATT_COLS + 10 * HEADS * length * length * HEAD_WIDTH,
            bytes_accessed=24 * 2**20,
            transcendentals=HEADS * length * length,
        ),
        name="attention_back",
    )(chips, *da, *n1, qkv, o, lse, weight, *tables)


def tile_copies(j, taken, tiles, sems, one):
    part, row = divmod(j, 4)
    ref, at = ((0, 0), (1, 0), (1, one), (2, 0))[row]
    return pltpu.make_async_copy(
        taken[3 * part + ref].at[pl.ds(at, one), :], tiles.at[j % 2], sems.at[j % 2]
    )


def take_tile(step, taken, tiles, sems, one):
    for j in range(8):

        @pl.when(step == j)
        def _(j=j):
            if j < 7:
                tile_copies(j + 1, taken, tiles, sems, one).start()
            tile_copies(j, taken, tiles, sems, one).wait()


def weight_copies(pieces, chips_ref, rows, wide, there, sems):
    for i, piece in enumerate(pieces):
        at = pl.ds(pl.multiple_of(chips_ref[i] * rows, rows), rows)
        for j in range(wide):
            here = piece if piece.ndim == 2 else piece.at[j if wide > 1 else 2]
            yield pltpu.make_async_copy(
                here, there.at[at, pl.ds(j * FF_OWN, FF_OWN)], sems.at[i, j]
            )


def gate_up_kernel(count, rows, chips_ref, *refs):
    n2_refs, pieces, refs = refs[:6], refs[6 : 6 + count], refs[6 + count :]
    gate_up_ref, n2_t_ref, weights, tiles, tile_sems, sems = refs
    step = pl.program_id(0)
    one = tiles.shape[1]
    copies = list(weight_copies(pieces, chips_ref, rows, 2, weights, sems))

    @pl.when(step == 0)
    def _():
        for copy in copies:
            copy.start()
        tile_copies(0, n2_refs, tiles, tile_sems, one).start()
        for copy in copies:
            copy.wait()

    take_tile(step, n2_refs, tiles, tile_sems, one)
    n2 = tiles[step % 2]
    n2_t_ref[...] = n2.T
    gate_up_ref[...] = dot_ab(n2, weights[...]).astype(BF)


def gate_up(chips, n2, pieces):
    rows = pieces[0].shape[1]
    one = n2[0].shape[0]
    length = 8 * one
    return pl.pallas_call(
        functools.partial(gate_up_kernel, len(pieces), rows),
        grid_spec=pltpu.PrefetchScalarGridSpec(
            num_scalar_prefetch=1,
            grid=(8,),
            in_specs=[ANYWHERE] * (6 + len(pieces)),
            out_specs=[
                pl.BlockSpec((one, 2 * FF_OWN), lambda i, c: (i, 0)),
                pl.BlockSpec((D, one), lambda i, c: (0, i)),
            ],
            scratch_shapes=[
                pltpu.VMEM((D, 2 * FF_OWN), BF),
                pltpu.VMEM((2, one, D), BF),
                pltpu.SemaphoreType.DMA((2,)),
                pltpu.SemaphoreType.DMA((len(pieces), 2)),
            ],
        ),
        out_shape=[
            jax.ShapeDtypeStruct((length, 2 * FF_OWN), BF),
            jax.ShapeDtypeStruct((D, length), BF),
        ],
        compiler_params=pltpu.CompilerParams(vmem_limit_bytes=VMEM_LIMIT),
        cost_estimate=cost(
            flops=4 * length * D * FF_OWN, bytes_accessed=30 * 2**20, transcendentals=0
        ),
        name="gate_up",
    )(chips, *n2, *pieces)


def feed_forward_kernel(count, rows, chips_ref, gate_up_ref, *refs):
    dy_refs, refs = refs[:6], refs[6:]
    gu_pieces, d_pieces, refs = refs[:count], refs[count : 2 * count], refs[2 * count :]
    dn2_refs, refs = refs[:8], refs[8:]
    u_ref, dgate_ref, dup_ref, dy_t_ref, down_ref, *refs = refs
    gu_w, d_w, tiles, tile_sems, gu_sems, d_sems, out_sem = refs
    step = pl.program_id(0)
    one = tiles.shape[1]
    gu_copies = list(weight_copies(gu_pieces, chips_ref, rows, 2, gu_w, gu_sems))
    d_copies = list(weight_copies(d_pieces, chips_ref, rows, 1, d_w, d_sems))
    save = pltpu.make_async_copy(d_w, down_ref, out_sem)

    @pl.when(step == 0)
    def _():
        for copy in d_copies:
            copy.start()
        tile_copies(0, dy_refs, tiles, tile_sems, one).start()
        for copy in gu_copies:
            copy.start()
        for copy in d_copies:
            copy.wait()
        save.start()

    take_tile(step, dy_refs, tiles, tile_sems, one)
    dy = tiles[step % 2]
    dy_t_ref[...] = dy.T
    du = dot_ab(dy, d_w[...])
    gate = gate_up_ref[:, :FF_OWN].astype(F32)
    up = gate_up_ref[:, FF_OWN:].astype(F32)
    sig = jax.nn.sigmoid(gate)
    silu = gate * sig
    u_ref[...] = (silu * up).astype(BF)
    dup = (du * silu).astype(BF)
    dgate = (du * up * sig * (1.0 + gate * (1.0 - sig))).astype(BF)
    dup_ref[...] = dup
    dgate_ref[...] = dgate

    @pl.when(step == 0)
    def _():
        for copy in gu_copies:
            copy.wait()

    dn2 = dot_abt(jnp.concatenate([dgate, dup], axis=1), gu_w[...]).astype(BF)
    for j in range(8):

        @pl.when(step == j)
        def _(j=j):
            dn2_refs[j][...] = dn2

    @pl.when(step == pl.num_programs(0) - 1)
    def _():
        save.wait()


def feed_forward(chips, gates, dy, gu_pieces, d_pieces):
    count = len(d_pieces)
    rows = d_pieces[0].shape[-2]
    one = dy[0].shape[0]
    length = 8 * one
    tile = lambda width: pl.BlockSpec((one, width), lambda i, c: (i, 0))
    kept = pl.BlockSpec((one, D), lambda i, c: (0, 0))
    return pl.pallas_call(
        functools.partial(feed_forward_kernel, count, rows),
        grid_spec=pltpu.PrefetchScalarGridSpec(
            num_scalar_prefetch=1,
            grid=(8,),
            in_specs=[tile(2 * FF_OWN)] + [ANYWHERE] * (6 + 2 * count),
            out_specs=[kept] * 8
            + [tile(FF_OWN)] * 3
            + [pl.BlockSpec((D, one), lambda i, c: (0, i)), ANYWHERE],
            scratch_shapes=[
                pltpu.VMEM((D, 2 * FF_OWN), BF),
                pltpu.VMEM((D, FF_OWN), BF),
                pltpu.VMEM((2, one, D), BF),
                pltpu.SemaphoreType.DMA((2,)),
                pltpu.SemaphoreType.DMA((count, 2)),
                pltpu.SemaphoreType.DMA((count, 1)),
                pltpu.SemaphoreType.DMA,
            ],
        ),
        out_shape=[jax.ShapeDtypeStruct((one, D), BF)] * 8
        + [jax.ShapeDtypeStruct((length, FF_OWN), BF)] * 3
        + [jax.ShapeDtypeStruct((D, length), BF), jax.ShapeDtypeStruct((D, FF_OWN), BF)],
        compiler_params=pltpu.CompilerParams(vmem_limit_bytes=VMEM_LIMIT),
        cost_estimate=cost(
            flops=6 * length * D * FF_OWN,
            bytes_accessed=50 * 2**20,
            transcendentals=length * FF_OWN,
        ),
        name="feed_forward",
    )(chips, gates, *dy, *gu_pieces, *d_pieces)


def weight_grad_kernel(rows, place_ref, left_ref, right_ref, *refs):
    keep_ref, send_ref, total = refs
    width = right_ref.shape[1]
    for at in range(0, width, 256):
        to = min(at + 256, width)
        total[:, :, at:to] = dot_ab(left_ref[...], right_ref[:, at:to]).reshape(
            4, rows, to - at
        )
    lo, yy = place_ref[1], place_ref[2]
    for k in range(2):
        row = jnp.where(lo == 0, k, 1 - k) * 2
        keep_ref[0, k] = total[row + yy].astype(BF)
        send_ref[0, k] = total[row + 1 - yy].astype(BF)


def weight_grad(place, left, right):
    count = lax.axis_size("hi")
    length, width = right.shape
    rows = left.shape[0] // (4 * count)
    block = pl.BlockSpec((1, 2, rows, width), lambda i, p: (i, 0, 0, 0))
    out = jax.ShapeDtypeStruct((count, 2, rows, width), BF)
    return pl.pallas_call(
        functools.partial(weight_grad_kernel, rows),
        grid_spec=pltpu.PrefetchScalarGridSpec(
            num_scalar_prefetch=1,
            grid=(count,),
            in_specs=[
                pl.BlockSpec((4 * rows, length), lambda i, p: (lax.rem(i + p[0], count), 0)),
                pl.BlockSpec((length, width), lambda i, p: (0, 0)),
            ],
            out_specs=[block] * 2,
            scratch_shapes=[pltpu.VMEM((4, rows, width), F32)],
        ),
        out_shape=[out] * 2,
        compiler_params=pltpu.CompilerParams(vmem_limit_bytes=VMEM_LIMIT),
        cost_estimate=cost(
            flops=2 * length * D * width, bytes_accessed=16 * 2**20, transcendentals=0
        ),
        name="weight_grad",
    )(place, left, right)


def down_kernel(left_ref, right_ref, *out_refs):
    step = pl.program_id(0)
    product = dot_abt(left_ref[...], right_ref[...]).astype(BF)
    for k, ref in enumerate(out_refs):

        @pl.when((step % 2 == k % 2) & (step // 4 == k // 2))
        def _(ref=ref):
            ref[...] = product


def down(left, right):
    length, width = left.shape
    one = length // 8
    parts = [
        pl.BlockSpec((one, D), lambda i, j=j: (jnp.clip((i - j) // 2, 0, 1), 0)) for j in (0, 0, 4, 4)
    ]
    return pl.pallas_call(
        down_kernel,
        grid=(8,),
        in_specs=[
            pl.BlockSpec((one, width), lambda i: (i, 0)),
            pl.BlockSpec((D, width), lambda i: (0, 0)),
        ],
        out_specs=parts,
        out_shape=[jax.ShapeDtypeStruct((2 * one, D), BF)] * 4,
        compiler_params=pltpu.CompilerParams(vmem_limit_bytes=VMEM_LIMIT),
        cost_estimate=cost(
            flops=2 * length * D * width, bytes_accessed=14 * 2**20, transcendentals=0
        ),
        name="down",
    )(left, right)


def total_of(*parts):
    return sum(part.astype(F32) for part in parts)


class EightSum:
    def __init__(self, parts):
        self.keep = parts[:4]
        self.core = [None] * 4
        for k in (3, 1, 2, 0):
            self.core[k] = swap(parts[4 + k], "core")
        self.half = parts[0].shape[0] // 2

    def second(self, order):
        self.core = order.done(self.core)
        half = self.half
        both, by_x, by_lo = [total_of(self.keep[k], self.core[k]) for k in (3, 1, 2)]
        self.to_lo = swap(both[:half].astype(BF), "tensor")
        self.to_x = swap(both[half:].astype(BF), "lo")
        self.x_first = swap(by_x[:half].astype(BF), "tensor")
        self.lo_second = swap(by_lo[half:].astype(BF), "lo")
        self.by_x, self.by_lo = by_x[half:], by_lo[:half]

    def third(self, order):
        to_lo, to_x, self.x_first, self.lo_second = order.done(
            (self.to_lo, self.to_x, self.x_first, self.lo_second)
        )
        self.x_second = swap(total_of(self.by_x, to_x).astype(BF), "tensor")
        self.lo_first = swap(total_of(self.by_lo, to_lo).astype(BF), "lo")

    def total(self, order):
        x_second, lo_first = order.done((self.x_second, self.lo_first))
        return (
            total_of(self.keep[0], self.core[0])
            + jnp.concatenate([self.x_first, x_second], axis=0).astype(F32)
            + jnp.concatenate([lo_first, self.lo_second], axis=0).astype(F32)
        )


class BranchSum:
    def __init__(self, near, by_x, core_near, core_by_x):
        self.near, self.by_x = near, by_x
        self.core = swap(core_by_x, "core"), swap(core_near, "core")

    def along_x(self, order):
        by_x, near = order.done(self.core)
        self.near = total_of(self.near, near)
        self.x = swap(total_of(self.by_x, by_x).astype(BF), "tensor")

    def along_lo(self, order):
        total = self.near + order.done(self.x).astype(F32)
        half = total.shape[0] // 2
        self.own = total[:half]
        self.lo = swap(total[half:].astype(BF), "lo")

    def arrived(self, order):
        self.lo = order.done(self.lo)

    def total(self):
        return self.own + self.lo.astype(F32)


class FourSum:
    def __init__(self, own, first, second, core_own, core_first, core_second):
        self.own, self.x = own, (first, second)
        self.core_x = swap(core_first, "core"), swap(core_second, "core")
        self.core_own = swap(core_own, "core")

    def second(self, order):
        core_x = order.done(self.core_x)
        by_x = [total_of(*pair).astype(BF) for pair in zip(self.x, core_x)]
        self.x = [swap(part, "tensor") for part in by_x]

    def total(self, order):
        self.core_own = order.done(self.core_own)
        x = order.done(self.x)
        return total_of(self.own, self.core_own, jnp.concatenate(x, axis=0))


class GradSum:
    def __init__(self, keep, send):
        self.keep = keep
        self.other = swap(send, "yy")

    def across(self, order, by_gather):
        self.other = order.done(self.other)
        count = lax.axis_size("hi")
        far = [total_of(self.keep[k], self.other[k]).astype(BF) for k in range(1, count)]
        if by_gather:
            self.every = [lax.all_gather(part, "hi") for part in far]
        else:
            self.every = None
            self.far = [turn(part, "hi", k + 1) for k, part in enumerate(far)]

    def arrived(self, order):
        if self.every is None:
            self.far = order.done(self.far)
        else:
            every = order.done(self.every)
            self.far = [others_of(part)[k] for k, part in enumerate(every)]

    def total(self):
        total = self.keep[0].astype(F32) + self.other[0].astype(F32)
        for far in self.far:
            total = total + far.astype(F32)
        return total


def body(
    tokens,
    cotangent,
    segments,
    small_params,
    small_first,
    small_second,
    qkv_weight,
    qkv_first,
    qkv_second,
    out_weight,
    out_first,
    out_second,
    gateup_weight,
    gateup_first,
    gateup_second,
    down_weight,
    down_first,
    down_second,
):
    hi_count = lax.axis_size("hi")
    hi, lo, yy = lax.axis_index("hi"), lax.axis_index("lo"), lax.axis_index("yy")
    core = lax.axis_index("core")
    place_x = lax.axis_index("tensor")
    own_rows = tokens.shape[0]
    shard_rows = qkv_weight.shape[0]
    gain_one = small_params[:D]
    gain_two = small_params[D : 2 * D]
    bias_all = small_params[2 * D :]
    q_at = place_x * (bias_all.shape[0] // 2) + core * Q_COLS
    kv_at = place_x * (bias_all.shape[0] // 2) + 2 * Q_COLS
    bias_local = jnp.concatenate(
        [
            lax.dynamic_slice_in_dim(bias_all, q_at, Q_COLS),
            lax.dynamic_slice_in_dim(bias_all, kv_at, 2 * HEAD_WIDTH),
        ]
    )

    order = Order()
    steps = range(1, hi_count)

    def both_cores(mine, other, axis):
        return jnp.where(
            core == 0,
            jnp.concatenate([mine, other], axis=axis),
            jnp.concatenate([other, mine], axis=axis),
        )

    other_ids = swap(segments, "core")
    qkv_low = qkv_weight.astype(BF)
    out_low = out_weight.astype(BF).T

    def attention_pack(which):
        return jnp.concatenate(
            [
                lax.dynamic_slice_in_dim(qkv_low, which * Q_COLS, Q_COLS, 1),
                qkv_low[:, 2 * Q_COLS :],
                lax.dynamic_slice_in_dim(out_low, which * Q_COLS, Q_COLS, 1),
            ],
            axis=1,
        )

    att_theirs = attention_pack(1 - core)
    att_core = swap(att_theirs, "core")
    order.mark = att_theirs
    rows_in = order.after(tokens).astype(F32)
    scale_one = rms_scale(rows_in)
    n1 = (rows_in * scale_one * gain_one).astype(BF)
    n1_x = swap(n1, "tensor")
    order.mark = n1
    att_shard = both_cores(attention_pack(core), order.done(att_core), 0)
    order.mark = att_shard
    att_hi = [turn(att_shard, "hi", k) for k in steps]
    att_yy = swap(att_shard, "yy")
    att_lo = swap(att_shard, "lo")

    gateup_in, down_in = order.after((gateup_weight, down_weight))
    ff_low = jnp.pad(
        jnp.concatenate([gateup_in.astype(BF), down_in.astype(BF).T[None]], axis=0),
        ((0, 0), (0, 0), (0, FF_PAD - FF_LOCAL)),
    )
    ff_mine = lax.dynamic_slice_in_dim(ff_low, core * FF_CORE, FF_CORE, 2)
    ff_theirs = lax.dynamic_slice_in_dim(ff_low, (1 - core) * FF_CORE, FF_CORE, 2)
    ff_core = swap(ff_theirs, "core")
    order.mark = ff_theirs

    ff_shard = both_cores(ff_mine, order.done(ff_core), 1)
    ff_own = lax.dynamic_slice_in_dim(ff_shard, lo * FF_OWN, FF_OWN, 2)
    ff_theirs = lax.dynamic_slice_in_dim(ff_shard, (1 - lo) * FF_OWN, FF_OWN, 2)
    order.mark = ff_theirs
    att_lo = order.done(att_lo)
    att_lo_yy = swap(att_lo, "yy")
    att_yy = order.done(att_yy)
    att_hi = order.done(att_hi)
    att_hi_lo = [swap(part, "lo") for part in att_hi]
    att_hi_yy = [swap(part, "yy") for part in att_hi]
    n1_core = swap(order.after(n1), "core")
    att_lo_yy = order.done(att_lo_yy)
    att_hi_lo = order.done(att_hi_lo)
    att_hi_lo_yy = [swap(part, "yy") for part in att_hi_lo]
    ff_lo = swap(order.after(ff_theirs), "lo")
    ff_hi = lax.all_gather(order.after(ff_own), "hi")
    n1_core = order.done(n1_core)
    other_ids = order.done(other_ids)
    angles, key_place, row_place, row_start = documents(core, place_x, segments, other_ids)
    sign = jnp.where(jnp.arange(HEAD_WIDTH) < HEAD_WIDTH // 2, -1.0, 1.0)
    tables = order.after((jnp.cos(angles), jnp.sin(angles) * sign, key_place, row_place, row_start))
    order.mark = tables[0]
    att_hi_yy = order.done(att_hi_yy)
    n1_x = order.done(n1_x)
    n1_core_x = swap(n1_x, "core")
    cot_x = swap(order.after(cotangent), "tensor")
    n1_core_x = order.done(n1_core_x)
    att_hi_lo_yy = order.done(att_hi_lo_yy)
    ff_yy = swap(order.after(ff_own), "yy")

    near_parts = [att_shard, att_lo]
    yy_parts = [att_yy, att_lo_yy]
    for k in range(hi_count - 1):
        near_parts += [att_hi[k], att_hi_lo[k]]
        yy_parts += [att_hi_yy[k], att_hi_lo_yy[k]]
    att_parts = near_parts + yy_parts
    n1_parts = order.after((n1, n1_x, n1_core, n1_core_x))
    qkv, attn_rows, lse, *out_parts, att_weight = attention(
        tree_order(-1), n1_parts, bias_local[None], tables, att_parts
    )
    order.mark = lse

    out = FourSum(*out_parts)
    half = own_rows // 2
    cot_x = order.done(cot_x)
    ff_lo = order.done(ff_lo)
    ff_lo_hi_gu = lax.all_gather(ff_lo[:2], "hi")
    ff_yy = order.done(ff_yy)
    ff_lo_yy = swap(ff_lo, "yy")
    out.second(order)
    ff_hi = others_of(order.done(ff_hi))
    order.mark = ff_hi
    residual = rows_in + out.total(order)
    scale_two = rms_scale(residual)
    n2 = (residual * scale_two * gain_two).astype(BF)
    n2_x_second, n2_lo_first = swap(n2[half:], "tensor"), swap(n2[:half], "lo")
    n2_x_first, n2_lo_second = swap(n2[:half], "tensor"), swap(n2[half:], "lo")
    order.mark = n2
    ff_lo_yy = order.done(ff_lo_yy)
    ff_hi_yy = [swap(order.after(part), "yy") for part in ff_hi]
    n2_x_second, n2_lo_first = order.done((n2_x_second, n2_lo_first))
    n2_both = swap(n2_lo_first, "tensor"), swap(n2_x_second, "lo")
    n2_x_first, n2_lo_second = order.done((n2_x_first, n2_lo_second))
    n2_near = jnp.concatenate([n2_x_first, n2_x_second, n2_lo_first, n2_lo_second])
    n2_core_near, n2_core = swap(n2_near, "core"), swap(n2, "core")
    ff_lo_hi_gu = others_of(order.done(ff_lo_hi_gu))
    n2_both = jnp.concatenate(order.done(n2_both))
    n2_core_near, n2_core = order.done((n2_core_near, n2_core))
    n2_core_both = swap(n2_both, "core")
    cot_lo = swap(order.after(cotangent), "lo")
    ff_lo_hi_yy_gu = [swap(order.after(part), "yy") for part in ff_lo_hi_gu]
    ff_lo_hi_d = [turn(order.after(ff_lo[2]), "hi", k) for k in steps]
    ff_hi_yy = order.done(ff_hi_yy)
    cot_lo = order.done(cot_lo)
    cot_both = swap(cot_lo[:half], "tensor"), swap(cot_x[half:], "lo")
    cot_near = jnp.concatenate([cot_x, cot_lo])
    cot_core, cot_core_near = swap(order.after(cotangent), "core"), swap(cot_near, "core")
    n2_core_both = order.done(n2_core_both)
    ff_lo_hi_d = order.done(ff_lo_hi_d)
    ff_lo_hi_yy_d = [swap(part, "yy") for part in ff_lo_hi_d]
    ff_lo_hi_yy_gu = order.done(ff_lo_hi_yy_gu)
    n2_parts = [n2, n2_near, n2_both, n2_core, n2_core_near, n2_core_both]

    whole = [ff_own, ff_lo, ff_yy, ff_lo_yy, *ff_hi, *ff_hi_yy]
    gu_pieces = [*whole, *ff_lo_hi_gu, *ff_lo_hi_yy_gu]
    ff_chips = [chip_at(0, l, y) for y in (0, 1) for l in (0, 1)]
    ff_chips += [chip_at(-k, l, y) for l in (0, 1) for y in (0, 1) for k in steps]
    ff_chips = jnp.stack(ff_chips).astype(jnp.int32)
    gates, n2_t = gate_up(ff_chips, order.after(n2_parts), gu_pieces)
    order.mark = gates
    cot_both = jnp.concatenate(order.done(cot_both))
    cot_core_both = swap(cot_both, "core")
    cot_core, cot_core_near = order.done((cot_core, cot_core_near))
    ff_lo_hi_yy_d = order.done(ff_lo_hi_yy_d)
    cot_core_both = order.done(cot_core_both)
    cot_parts = [cotangent, cot_near, cot_both, cot_core, cot_core_near, cot_core_both]
    d_pieces = [*whole, *ff_lo_hi_d, *ff_lo_hi_yy_d]
    *dn2_parts, hidden, gate_grad, up_grad, cot_t, w_down = feed_forward(
        ff_chips, gates, order.after(cot_parts), gu_pieces, d_pieces
    )
    order.mark = w_down

    place = jnp.stack([hi, lo, yy]).astype(jnp.int32)

    def grad_of(left, right):
        keep, send = weight_grad(place, order.after(left), right)
        order.mark = keep
        return GradSum(keep, send)

    ff_squares = 0.0
    rows_of = lambda value, which, axis: lax.dynamic_slice_in_dim(
        value, which * shard_rows, shard_rows, axis
    )

    def summed_up(grad):
        nonlocal ff_squares
        total = order.after(grad.total())
        ff_squares = ff_squares + jnp.sum(total * total)
        low = total.astype(BF)
        order.mark = low
        return low[0], swap(low[1], "lo")

    def own_rows_of(low, other):
        other = order.done(other)
        cols = jnp.where(
            lo == 0,
            jnp.concatenate([low, other], axis=1),
            jnp.concatenate([other, low], axis=1),
        )
        theirs = rows_of(cols, 1 - core, 0)
        order.mark = theirs
        return rows_of(cols, core, 0), swap(theirs, "core")

    dn2 = EightSum(dn2_parts)
    d_sum = grad_of(cot_t, hidden)
    dn2.second(order)
    g_sum = grad_of(n2_t, gate_grad)
    dn2.third(order)
    u_sum = grad_of(n2_t, up_grad)
    d_sum.across(order, True)
    norm_two_in, gain_two_grad = norm_backward(residual, scale_two, gain_two, dn2.total(order))
    residual_grad = cotangent.astype(F32) + norm_two_in
    da = residual_grad.astype(BF)
    da_x = [swap(da[:half], "tensor"), swap(da[half:], "tensor")]
    da_core = swap(da, "core")
    order.mark = da
    branch_parts = down(*order.after((hidden, w_down)))
    order.mark = branch_parts[0]
    branch = BranchSum(*branch_parts)
    da_x = order.done(da_x)
    da_core_x = [swap(part, "core") for part in da_x]
    da_core, da_core_x = order.done((da_core, da_core_x))
    g_sum.across(order, False)

    _, bias_grad, *parts = attention_back(
        sum_order(),
        order.after((da, *da_x, da_core, *da_core_x)),
        n1_parts,
        qkv,
        attn_rows,
        lse,
        att_weight,
        tables,
    )
    order.mark = bias_grad
    d_sum.arrived(order)
    dn1 = FourSum(*parts[:6])
    att = ChipSum(*parts[6:])
    dn1.second(order)
    g_sum.arrived(order)
    norm_one_in, gain_one_grad = norm_backward(rows_in, scale_one, gain_one, dn1.total(order))
    u_sum.across(order, False)
    att.far_yy(order)
    bias_grad = order.after(bias_grad)[0]
    bias_slots = lax.dynamic_update_slice_in_dim(
        jnp.zeros_like(bias_all), bias_grad[:Q_COLS], q_at, 0
    )
    bias_slots = lax.dynamic_update_slice_in_dim(bias_slots, bias_grad[Q_COLS:], kv_at, 0)
    att.far_hi(order)
    branch.along_x(order)
    d_low, d_way = summed_up(d_sum)
    g_low, g_way = summed_up(g_sum)
    att.near_yy(order)
    input_grad = residual_grad + norm_one_in
    branch.along_lo(order)
    u_sum.arrived(order)
    att_sum = att.total(order)
    att_low = att_sum.astype(BF)
    other_att = swap(rows_of(att_low, 1 - core, 0), "core")
    u_low, u_way = summed_up(u_sum)
    other_att = order.done(other_att)
    d_rows = own_rows_of(d_low, d_way)
    g_rows = own_rows_of(g_low, g_way)
    branch.arrived(order)

    own_att = rows_of(att_low, core, 0)
    first_att = jnp.where(core == 0, own_att, other_att).astype(F32)
    second_att = jnp.where(core == 0, other_att, own_att).astype(F32)
    kv_sum = first_att[:, Q_COLS:QKV_COLS] + second_att[:, Q_COLS:QKV_COLS]
    qkv_owned = jnp.concatenate([first_att[:, :Q_COLS], second_att[:, :Q_COLS], kv_sum], axis=1)
    out_owned = jnp.concatenate([first_att[:, QKV_COLS:], second_att[:, QKV_COLS:]], axis=1).T
    owned_squares = (
        jnp.sum(qkv_owned * qkv_owned) + jnp.sum(out_owned * out_owned) + ff_squares
    )
    summed = jnp.concatenate(
        [gain_one_grad, gain_two_grad, bias_slots, jnp.full((128,), owned_squares)]
    )
    summed = summed + order.done(swap(summed, "core"))
    summed = summed + order.done(swap(summed, "tensor"))
    summed = summed + order.done(swap(summed, "yy"))
    summed = summed + order.done(swap(summed, "lo"))
    step = 1
    while step < hi_count:
        moved = lax.ppermute(summed, "hi", [(i, i ^ step) for i in range(hi_count)])
        summed = summed + order.done(moved)
        step *= 2
    order.mark = summed
    u_rows = own_rows_of(u_low, u_way)
    block_out = (residual + order.after(branch.total())).astype(BF)

    def owned(rows):
        mine, other = rows
        return both_cores(mine, other, 1)[:, :FF_LOCAL].astype(F32)

    gateup_owned = jnp.stack([owned(g_rows), owned(u_rows)])
    down_owned = owned(d_rows).T
    small_grad = summed[:-128]
    squares = summed[-1] + jnp.sum(small_grad * small_grad)
    grad_norm = jnp.sqrt(squares)
    clip_factor = jnp.minimum(1.0, MAX_NORM / (grad_norm + 1e-06))
    new_small, new_small_first, new_small_second = adam_update(
        small_params, small_first, small_second, clip_factor * small_grad, 0.5, 0.0
    )
    new_qkv, new_qkv_first, new_qkv_second = adam_update(
        qkv_weight, qkv_first, qkv_second, clip_factor * qkv_owned, 2.0 / math.sqrt(D), WEIGHT_DECAY
    )
    new_out, new_out_first, new_out_second = adam_update(
        out_weight,
        out_first,
        out_second,
        clip_factor * out_owned,
        8.0 / math.sqrt(QUERY_HEADS * HEAD_WIDTH),
        WEIGHT_DECAY,
    )
    new_gateup, new_gateup_first, new_gateup_second = adam_update(
        gateup_weight,
        gateup_first,
        gateup_second,
        clip_factor * gateup_owned,
        2.0 / math.sqrt(D),
        WEIGHT_DECAY,
    )
    new_down, new_down_first, new_down_second = adam_update(
        down_weight,
        down_first,
        down_second,
        clip_factor * down_owned,
        3.0 / math.sqrt(FF),
        WEIGHT_DECAY,
    )
    return (
        block_out,
        input_grad,
        grad_norm,
        new_small,
        new_small_first,
        new_small_second,
        new_qkv,
        new_qkv_first,
        new_qkv_second,
        new_out,
        new_out_first,
        new_out_second,
        new_gateup,
        new_gateup_first,
        new_gateup_second,
        new_down,
        new_down_first,
        new_down_second,
    )


def solution(mesh):
    count = mesh.shape["dp"]
    fine = Mesh(
        mesh.devices.reshape(count // 8, 2, 2, 2, mesh.shape["tensor"]),
        CHIP + ("core", "tensor"),
    )
    dp = CHIP + ("core",)
    rows = P(dp + ("tensor",), None)
    by_rows = P(dp, "tensor")
    by_cols = P("tensor", dp)
    stacked = P(None, dp, "tensor")
    weights = (by_rows,) * 3 + (by_cols,) * 3 + (stacked,) * 3 + (by_cols,) * 3
    return jax.shard_map(
        body,
        mesh=fine,
        in_specs=(rows, rows, P(dp), P(), P(), P()) + weights,
        out_specs=(rows, rows, P(), P(), P(), P()) + weights,
        check_vma=False,
    )
```

```python
import functools
import math

import jax
import jax.numpy as jnp
import numpy as np
from jax import lax
from jax.experimental import pallas as pl
from jax.experimental.pallas import tpu as pltpu
from jax.sharding import Mesh
from jax.sharding import PartitionSpec as P

D = 1536
FF = 8960
QUERY_HEADS = 12
KEY_VALUE_HEADS = 2
HEAD_WIDTH = 128
STEP = 10

EPSILON = 1e-06
ROPE_BASE = 1000000.0
BETA_ONE = 0.9
BETA_TWO = 0.999
ADAM_EPS = 1e-08
WEIGHT_DECAY = 0.1
MAX_NORM = 1.0
NEGATIVE = -1e30

BF = jnp.bfloat16
F32 = jnp.float32
HEADS = 3
Q_COLS = HEADS * HEAD_WIDTH
QKV_COLS = Q_COLS + 2 * HEAD_WIDTH
ATT_COLS = QKV_COLS + Q_COLS
FF_LOCAL = FF // 2
FF_PAD = 4608
FF_CORE = FF_PAD // 2
FF_OWN = FF_PAD // 4
TILE = 256
VMEM_LIMIT = 60 * 2**20
CHIP = ("hi", "lo", "yy")


def dot_ab(a, b):
    return lax.dot_general(a, b, (((1,), (0,)), ((), ())), preferred_element_type=F32)


def dot_abt(a, b):
    return lax.dot_general(a, b, (((1,), (1,)), ((), ())), preferred_element_type=F32)


def dot_atb(a, b):
    return lax.dot_general(a, b, (((0,), (0,)), ((), ())), preferred_element_type=F32)


def rms_scale(inputs):
    return lax.rsqrt(jnp.mean(inputs * inputs, axis=-1, keepdims=True) + EPSILON)


def norm_backward(inputs, inv_rms, gain_vec, upstream):
    normed = inputs * inv_rms
    normed_grad = upstream * gain_vec
    input_part = inv_rms * (
        normed_grad - normed * jnp.mean(normed_grad * normed, axis=-1, keepdims=True)
    )
    return (input_part, jnp.sum(upstream * normed, axis=0))


def adam_update(weight, moment_one, moment_two, gradient, step_rate, decay_rate):
    first_new = BETA_ONE * moment_one + (1.0 - BETA_ONE) * gradient
    second_new = BETA_TWO * moment_two + (1.0 - BETA_TWO) * gradient * gradient
    corrected = first_new / (1.0 - BETA_ONE**STEP)
    spread = jnp.sqrt(second_new / (1.0 - BETA_TWO**STEP)) + ADAM_EPS
    return (
        weight * (1.0 - step_rate * decay_rate) - step_rate * corrected / spread,
        first_new,
        second_new,
    )


def swap(value, axis):
    return lax.ppermute(value, axis, [(0, 1), (1, 0)])


class Order:
    def __init__(self):
        self.mark = None

    def after(self, value):
        if self.mark is None:
            return value
        return lax.optimization_barrier((value, self.mark))[0]

    def done(self, value):
        value = self.after(value)
        self.mark = value
        return value


def chip_at(step, other_lo, other_yy):
    count = lax.axis_size("hi")
    hi = (lax.axis_index("hi") + step) % count
    return (hi * 2 + (lax.axis_index("lo") ^ other_lo)) * 2 + (lax.axis_index("yy") ^ other_yy)


def turn(value, axis, steps):
    count = lax.axis_size(axis)
    return lax.ppermute(value, axis, [(i, (i + steps) % count) for i in range(count)])


def others_of(every):
    count = lax.axis_size("hi")
    hi = lax.axis_index("hi")
    return [
        lax.dynamic_index_in_dim(every, (hi - k) % count, 0, keepdims=False)
        for k in range(1, count)
    ]


def tree_order(sign):
    steps = [(0, 0), (0, 1)] + [(k, l) for k in range(1, lax.axis_size("hi")) for l in (0, 1)]
    return jnp.stack([chip_at(sign * k, l, y) for y in (0, 1) for k, l in steps]).astype(jnp.int32)


def sum_order():
    steps = range(1, lax.axis_size("hi"))
    chips = [chip_at(k, l, y) for l in (1, 0) for ks in (steps, (0,)) for k in ks for y in (1, 0)]
    return jnp.stack(chips).astype(jnp.int32)


class ChipSum:
    def __init__(self, lo_far, lo_near, far, near):
        self.far, self.near, self.lo_near = far, near, lo_near
        self.lo_far = swap(lo_far, "lo")

    def far_yy(self, order):
        self.far = self.far.astype(F32) + order.done(self.lo_far).astype(F32)
        theirs = self.far[0::2].astype(BF)
        self.yy_far = swap(theirs, "yy")
        order.mark = theirs
        self.lo_near = swap(order.after(self.lo_near), "lo")

    def far_hi(self, order):
        far = (self.far[1::2] + order.done(self.yy_far).astype(F32)).astype(BF)
        self.hi = [turn(far[k - 1], "hi", k) for k in range(1, lax.axis_size("hi"))]
        order.mark = far

    def near_yy(self, order):
        self.near = self.near.astype(F32) + order.done(self.lo_near).astype(F32)
        theirs = self.near[0].astype(BF)
        self.yy_near = swap(theirs, "yy")
        order.mark = theirs

    def total(self, order):
        hi = order.done(self.hi)
        total = self.near[1] + order.done(self.yy_near).astype(F32)
        for part in hi:
            total = total + part.astype(F32)
        return total


def cost(flops, bytes_accessed, transcendentals):
    part = 4096
    return pl.CostEstimate(
        flops=flops // part,
        bytes_accessed=bytes_accessed // part,
        transcendentals=transcendentals // part,
    )


ANYWHERE = pl.BlockSpec(memory_space=pl.ANY)
WHOLE = pl.BlockSpec(memory_space=pltpu.VMEM)


def turn_halves(features, cos_both, sin_both):
    return features * cos_both + pltpu.roll(features, HEAD_WIDTH // 2, 1) * sin_both


def scores_t(keys, queries, key_place, place, start):
    scores = dot_abt(keys, queries) * (1.0 / math.sqrt(HEAD_WIDTH))
    return jnp.where((key_place <= place) & (key_place >= start), scores, NEGATIVE)


def rows_from(refs):
    begin = 0
    for ref in refs:
        yield slice(begin, begin + ref.shape[0]), ref
        begin += ref.shape[0]


def attention_kernel(blocks, parts, rows, chips_ref, *refs):
    n1_refs, refs = refs[:blocks], refs[blocks:]
    bias_ref, cos_ref, sin_ref, key_place_ref, place_ref, start_ref, *refs = refs
    shards, refs = refs[:parts], refs[parts:]
    qkv_ref, o_ref, lse_ref, *out_refs, weight_ref, weights, sems, out_sem = refs
    length = qkv_ref.shape[0]
    copies = [
        pltpu.make_async_copy(
            shards[i],
            weights.at[pl.ds(pl.multiple_of(chips_ref[i] * rows, rows), rows), :],
            sems.at[i],
        )
        for i in range(parts)
    ]
    for copy in copies:
        copy.start()
    for copy in copies:
        copy.wait()
    save = pltpu.make_async_copy(weights, weight_ref, out_sem)
    save.start()
    for at, ref in rows_from(n1_refs):
        projected = dot_ab(ref[...], weights[:, :QKV_COLS]) + bias_ref[...]
        cos_both, sin_both = cos_ref[at, :], sin_ref[at, :]
        for j in range(HEADS + 1):
            cols = slice(j * HEAD_WIDTH, (j + 1) * HEAD_WIDTH)
            qkv_ref[at, cols] = turn_halves(projected[:, cols], cos_both, sin_both).astype(BF)
        cols = slice(Q_COLS + HEAD_WIDTH, QKV_COLS)
        qkv_ref[at, cols] = projected[:, cols].astype(BF)
    keys = qkv_ref[:, Q_COLS : Q_COLS + HEAD_WIDTH]
    values_t = qkv_ref[:, Q_COLS + HEAD_WIDTH : QKV_COLS].T
    lse_ref[...] = jnp.zeros_like(lse_ref)
    key_place = key_place_ref[...]
    for at in range(0, length, TILE):
        block = slice(at, at + TILE)
        place, start = place_ref[:, block], start_ref[:, block]
        for h in range(HEADS):
            cols = slice(h * HEAD_WIDTH, (h + 1) * HEAD_WIDTH)
            scores = scores_t(keys, qkv_ref[block, cols], key_place, place, start)
            top = jnp.max(scores, axis=0, keepdims=True)
            weights_exp = jnp.exp(scores - top)
            total = jnp.sum(weights_exp, axis=0, keepdims=True)
            lse_ref[h : h + 1, block] = top + jnp.log(total)
            prob = (weights_exp * (1.0 / total)).astype(BF)
            o_ref[block, cols] = dot_ab(values_t, prob).astype(BF).T
    for at, ref in rows_from(out_refs):
        ref[...] = dot_abt(o_ref[at, :], weights[:, QKV_COLS:]).astype(BF)
    save.wait()


def documents_kernel(where_ref, ids_ref, other_ref, frequency_ref, angle_ref, key_place_ref, place_ref, start_ref):
    core, place_x = where_ref[0], where_ref[1]
    one = ids_ref.shape[1]

    def in_order(ref):
        rows = [ref[k : k + 1, :] for k in range(2)]
        return [
            jnp.where(place_x == 0, rows[0], rows[1]),
            jnp.where(place_x == 0, rows[1], rows[0]),
        ]

    ids = jnp.concatenate(in_order(ids_ref) + in_order(other_ref), axis=1)
    index = lax.broadcasted_iota(jnp.int32, (1, 4 * one), 1)
    block = index // one
    mine = core * 2 + place_x
    place = jnp.bitwise_xor(mine, block) * one + index - block * one

    def column(row):
        return jnp.broadcast_to(row.astype(F32), (8, 4 * one)).T[:, :1]

    ids_col, place_col = column(ids), column(place)
    ids_row, place_row = ids.astype(F32), place.astype(F32)
    start_row = jnp.min(
        jnp.where(ids_col == ids_row, place_col, 4.0 * one), axis=0, keepdims=True
    )
    place_ref[...] = place
    start_ref[...] = start_row.astype(jnp.int32)
    key_place_ref[...] = place_col.astype(jnp.int32)
    angle_ref[...] = column(place_row - start_row) * frequency_ref[...]


def documents(core, place_x, ids, other_ids):
    one = ids.shape[0] // 2
    exponent = np.arange(0, HEAD_WIDTH, 2, dtype=np.float32) / np.float32(HEAD_WIDTH)
    frequency = np.float32(1.0) / np.float32(ROPE_BASE) ** exponent
    return pl.pallas_call(
        documents_kernel,
        grid_spec=pltpu.PrefetchScalarGridSpec(
            num_scalar_prefetch=1,
            grid=(),
            in_specs=[WHOLE] * 3,
            out_specs=[WHOLE] * 4,
        ),
        out_shape=[
            jax.ShapeDtypeStruct((4 * one, HEAD_WIDTH), F32),
            jax.ShapeDtypeStruct((4 * one, 1), jnp.int32),
            jax.ShapeDtypeStruct((1, 4 * one), jnp.int32),
            jax.ShapeDtypeStruct((1, 4 * one), jnp.int32),
        ],
        compiler_params=pltpu.CompilerParams(vmem_limit_bytes=VMEM_LIMIT),
        cost_estimate=cost(flops=2**20, bytes_accessed=2**20, transcendentals=0),
        name="documents",
    )(
        jnp.stack([core, place_x]).astype(jnp.int32),
        ids.reshape(2, one),
        other_ids.reshape(2, one),
        jnp.asarray(np.concatenate([frequency, frequency])[None]),
    )


def four_shapes(rows):
    return [jax.ShapeDtypeStruct((r, D), BF) for r in (rows, rows // 2, rows // 2) * 2]


def attention(chips, n1, bias, tables, shards):
    length = tables[0].shape[0]
    parts = len(shards)
    rows = shards[0].shape[0]
    return pl.pallas_call(
        functools.partial(attention_kernel, len(n1), parts, rows),
        grid_spec=pltpu.PrefetchScalarGridSpec(
            num_scalar_prefetch=1,
            grid=(),
            in_specs=[WHOLE] * (len(n1) + 6) + [ANYWHERE] * parts,
            out_specs=[WHOLE] * 9 + [ANYWHERE],
            scratch_shapes=[
                pltpu.VMEM((D, ATT_COLS), BF),
                pltpu.SemaphoreType.DMA((parts,)),
                pltpu.SemaphoreType.DMA,
            ],
        ),
        out_shape=[
            jax.ShapeDtypeStruct((length, QKV_COLS), BF),
            jax.ShapeDtypeStruct((length, Q_COLS), BF),
            jax.ShapeDtypeStruct((8, length), F32),
            *four_shapes(length // 4),
            jax.ShapeDtypeStruct((D, ATT_COLS), BF),
        ],
        compiler_params=pltpu.CompilerParams(vmem_limit_bytes=VMEM_LIMIT),
        cost_estimate=cost(
            flops=2 * length * D * ATT_COLS + 4 * HEADS * length * length * HEAD_WIDTH,
            bytes_accessed=16 * 2**20,
            transcendentals=HEADS * length * length,
        ),
        name="attention",
    )(chips, *n1, bias, *tables, *shards)


def attention_back_kernel(das, n1s, count, rows, chips_ref, *refs):
    da_refs, n1_refs, refs = refs[:das], refs[das : das + n1s], refs[das + n1s :]
    qkv_ref, o_ref, lse_ref, weight_ref, *refs = refs
    cos_ref, sin_ref, key_place_ref, place_ref, start_ref, *refs = refs
    dqkv_ref, bias_ref, *refs = refs
    dn1_refs, block_refs, (mixed, left_t, grads) = refs[:6], refs[6:10], refs[10:]
    length = qkv_ref.shape[0]
    scale = 1.0 / math.sqrt(HEAD_WIDTH)
    for at, ref in rows_from(da_refs):
        mixed[at, :] = dot_ab(ref[...], weight_ref[:, QKV_COLS:]).astype(BF)
    key_cols = slice(Q_COLS, Q_COLS + HEAD_WIDTH)
    value_cols = slice(Q_COLS + HEAD_WIDTH, QKV_COLS)
    keys, values = qkv_ref[:, key_cols], qkv_ref[:, value_cols]
    keys_t = keys.T
    key_place = key_place_ref[...]
    keys_grad = jnp.zeros((length, HEAD_WIDTH), F32)
    values_grad = jnp.zeros((length, HEAD_WIDTH), F32)
    for at in range(0, length, TILE):
        block = slice(at, at + TILE)
        place, start = place_ref[:, block], start_ref[:, block]
        for h in range(HEADS):
            cols = slice(h * HEAD_WIDTH, (h + 1) * HEAD_WIDTH)
            queries, up = qkv_ref[block, cols], mixed[block, cols]
            scores = scores_t(keys, queries, key_place, place, start)
            prob = jnp.exp(scores - lse_ref[h : h + 1, block])
            prob_grad = dot_abt(values, up)
            inner = jnp.sum(prob * prob_grad, axis=0, keepdims=True)
            score_grad = (prob * (prob_grad - inner)).astype(BF)
            values_grad += dot_ab(prob.astype(BF), up)
            keys_grad += dot_ab(score_grad, queries)
            query_grad = dot_ab(keys_t, score_grad).T * scale
            dqkv_ref[block, cols] = turn_halves(
                query_grad, cos_ref[block, :], -sin_ref[block, :]
            ).astype(BF)
    dqkv_ref[:, key_cols] = turn_halves(keys_grad * scale, cos_ref[...], -sin_ref[...]).astype(BF)
    dqkv_ref[:, value_cols] = values_grad.astype(BF)
    bias_ref[...] = jnp.sum(dqkv_ref[...].astype(F32), axis=0, keepdims=True)
    for cols, left_refs, right_ref in (
        (slice(0, QKV_COLS), n1_refs, dqkv_ref),
        (slice(QKV_COLS, ATT_COLS), da_refs, o_ref),
    ):
        for at, ref in rows_from(left_refs):
            left_t[:, at] = ref[...].T
        grads[:, :, cols] = (
            dot_ab(left_t[...], right_ref[...]).astype(BF).reshape(4 * count, rows, -1)
        )
    at = 0
    for ref in block_refs:
        for k in range(ref.shape[0]):
            ref[k] = grads[chips_ref[at]]
            at += 1
    for at, ref in rows_from(dn1_refs):
        ref[...] = dot_abt(dqkv_ref[at, :], weight_ref[:, :QKV_COLS]).astype(BF)


def attention_back(chips, da, n1, qkv, o, lse, weight, tables):
    length = qkv.shape[0]
    count = chips.shape[0] // 4
    rows = D // (4 * count)
    blocks = [
        jax.ShapeDtypeStruct((2 * k, rows, ATT_COLS), BF) for k in (count - 1, 1, count - 1, 1)
    ]
    return pl.pallas_call(
        functools.partial(attention_back_kernel, len(da), len(n1), count, rows),
        grid_spec=pltpu.PrefetchScalarGridSpec(
            num_scalar_prefetch=1,
            grid=(),
            in_specs=[WHOLE] * (len(da) + len(n1) + 9),
            out_specs=[WHOLE] * 12,
            scratch_shapes=[
                pltpu.VMEM((length, Q_COLS), BF),
                pltpu.VMEM((D, length), BF),
                pltpu.VMEM((4 * count, rows, ATT_COLS), BF),
            ],
        ),
        out_shape=[
            jax.ShapeDtypeStruct((length, QKV_COLS), BF),
            jax.ShapeDtypeStruct((1, QKV_COLS), F32),
            *four_shapes(length // 4),
            *blocks,
        ],
        compiler_params=pltpu.CompilerParams(vmem_limit_bytes=VMEM_LIMIT),
        cost_estimate=cost(
            flops=2 * length * D * 2 * ATT_COLS + 10 * HEADS * length * length * HEAD_WIDTH,
            bytes_accessed=24 * 2**20,
            transcendentals=HEADS * length * length,
        ),
        name="attention_back",
    )(chips, *da, *n1, qkv, o, lse, weight, *tables)


def tile_copies(j, taken, tiles, sems, one):
    part, row = divmod(j, 4)
    ref, at = ((0, 0), (1, 0), (1, one), (2, 0))[row]
    return pltpu.make_async_copy(
        taken[3 * part + ref].at[pl.ds(at, one), :], tiles.at[j % 2], sems.at[j % 2]
    )


def take_tile(step, taken, tiles, sems, one):
    for j in range(8):

        @pl.when(step == j)
        def _(j=j):
            if j < 7:
                tile_copies(j + 1, taken, tiles, sems, one).start()
            tile_copies(j, taken, tiles, sems, one).wait()


def weight_copies(pieces, chips_ref, rows, wide, there, sems):
    for i, piece in enumerate(pieces):
        at = pl.ds(pl.multiple_of(chips_ref[i] * rows, rows), rows)
        for j in range(wide):
            here = piece if piece.ndim == 2 else piece.at[j if wide > 1 else 2]
            yield pltpu.make_async_copy(
                here, there.at[at, pl.ds(j * FF_OWN, FF_OWN)], sems.at[i, j]
            )


def gate_up_kernel(count, rows, chips_ref, *refs):
    n2_refs, pieces, refs = refs[:6], refs[6 : 6 + count], refs[6 + count :]
    gate_up_ref, n2_t_ref, weights, tiles, tile_sems, sems = refs
    step = pl.program_id(0)
    one = tiles.shape[1]
    copies = list(weight_copies(pieces, chips_ref, rows, 2, weights, sems))

    @pl.when(step == 0)
    def _():
        for copy in copies:
            copy.start()
        tile_copies(0, n2_refs, tiles, tile_sems, one).start()
        for copy in copies:
            copy.wait()

    take_tile(step, n2_refs, tiles, tile_sems, one)
    n2 = tiles[step % 2]
    n2_t_ref[...] = n2.T
    gate_up_ref[...] = dot_ab(n2, weights[...]).astype(BF)


def gate_up(chips, n2, pieces):
    rows = pieces[0].shape[1]
    one = n2[0].shape[0]
    length = 8 * one
    return pl.pallas_call(
        functools.partial(gate_up_kernel, len(pieces), rows),
        grid_spec=pltpu.PrefetchScalarGridSpec(
            num_scalar_prefetch=1,
            grid=(8,),
            in_specs=[ANYWHERE] * (6 + len(pieces)),
            out_specs=[
                pl.BlockSpec((one, 2 * FF_OWN), lambda i, c: (i, 0)),
                pl.BlockSpec((D, one), lambda i, c: (0, i)),
            ],
            scratch_shapes=[
                pltpu.VMEM((D, 2 * FF_OWN), BF),
                pltpu.VMEM((2, one, D), BF),
                pltpu.SemaphoreType.DMA((2,)),
                pltpu.SemaphoreType.DMA((len(pieces), 2)),
            ],
        ),
        out_shape=[
            jax.ShapeDtypeStruct((length, 2 * FF_OWN), BF),
            jax.ShapeDtypeStruct((D, length), BF),
        ],
        compiler_params=pltpu.CompilerParams(vmem_limit_bytes=VMEM_LIMIT),
        cost_estimate=cost(
            flops=4 * length * D * FF_OWN, bytes_accessed=30 * 2**20, transcendentals=0
        ),
        name="gate_up",
    )(chips, *n2, *pieces)


def feed_forward_kernel(count, rows, chips_ref, gate_up_ref, *refs):
    dy_refs, refs = refs[:6], refs[6:]
    gu_pieces, d_pieces, refs = refs[:count], refs[count : 2 * count], refs[2 * count :]
    dn2_refs, refs = refs[:8], refs[8:]
    u_ref, dgate_ref, dup_ref, dy_t_ref, down_ref, *refs = refs
    gu_w, d_w, tiles, tile_sems, gu_sems, d_sems, out_sem = refs
    step = pl.program_id(0)
    one = tiles.shape[1]
    gu_copies = list(weight_copies(gu_pieces, chips_ref, rows, 2, gu_w, gu_sems))
    d_copies = list(weight_copies(d_pieces, chips_ref, rows, 1, d_w, d_sems))
    save = pltpu.make_async_copy(d_w, down_ref, out_sem)

    @pl.when(step == 0)
    def _():
        for copy in d_copies:
            copy.start()
        tile_copies(0, dy_refs, tiles, tile_sems, one).start()
        for copy in gu_copies:
            copy.start()
        for copy in d_copies:
            copy.wait()
        save.start()

    take_tile(step, dy_refs, tiles, tile_sems, one)
    dy = tiles[step % 2]
    dy_t_ref[...] = dy.T
    du = dot_ab(dy, d_w[...])
    gate = gate_up_ref[:, :FF_OWN].astype(F32)
    up = gate_up_ref[:, FF_OWN:].astype(F32)
    sig = jax.nn.sigmoid(gate)
    silu = gate * sig
    u_ref[...] = (silu * up).astype(BF)
    dup = (du * silu).astype(BF)
    dgate = (du * up * sig * (1.0 + gate * (1.0 - sig))).astype(BF)
    dup_ref[...] = dup
    dgate_ref[...] = dgate

    @pl.when(step == 0)
    def _():
        for copy in gu_copies:
            copy.wait()

    dn2 = dot_abt(jnp.concatenate([dgate, dup], axis=1), gu_w[...]).astype(BF)
    for j in range(8):

        @pl.when(step == j)
        def _(j=j):
            dn2_refs[j][...] = dn2

    @pl.when(step == pl.num_programs(0) - 1)
    def _():
        save.wait()


def feed_forward(chips, gates, dy, gu_pieces, d_pieces):
    count = len(d_pieces)
    rows = d_pieces[0].shape[-2]
    one = dy[0].shape[0]
    length = 8 * one
    tile = lambda width: pl.BlockSpec((one, width), lambda i, c: (i, 0))
    kept = pl.BlockSpec((one, D), lambda i, c: (0, 0))
    return pl.pallas_call(
        functools.partial(feed_forward_kernel, count, rows),
        grid_spec=pltpu.PrefetchScalarGridSpec(
            num_scalar_prefetch=1,
            grid=(8,),
            in_specs=[tile(2 * FF_OWN)] + [ANYWHERE] * (6 + 2 * count),
            out_specs=[kept] * 8
            + [tile(FF_OWN)] * 3
            + [pl.BlockSpec((D, one), lambda i, c: (0, i)), ANYWHERE],
            scratch_shapes=[
                pltpu.VMEM((D, 2 * FF_OWN), BF),
                pltpu.VMEM((D, FF_OWN), BF),
                pltpu.VMEM((2, one, D), BF),
                pltpu.SemaphoreType.DMA((2,)),
                pltpu.SemaphoreType.DMA((count, 2)),
                pltpu.SemaphoreType.DMA((count, 1)),
                pltpu.SemaphoreType.DMA,
            ],
        ),
        out_shape=[jax.ShapeDtypeStruct((one, D), BF)] * 8
        + [jax.ShapeDtypeStruct((length, FF_OWN), BF)] * 3
        + [jax.ShapeDtypeStruct((D, length), BF), jax.ShapeDtypeStruct((D, FF_OWN), BF)],
        compiler_params=pltpu.CompilerParams(vmem_limit_bytes=VMEM_LIMIT),
        cost_estimate=cost(
            flops=6 * length * D * FF_OWN,
            bytes_accessed=50 * 2**20,
            transcendentals=length * FF_OWN,
        ),
        name="feed_forward",
    )(chips, gates, *dy, *gu_pieces, *d_pieces)


def weight_grad_kernel(rows, place_ref, left_ref, right_ref, *refs):
    keep_ref, send_ref, total = refs
    width = right_ref.shape[1]
    for at in range(0, width, 256):
        to = min(at + 256, width)
        total[:, :, at:to] = dot_ab(left_ref[...], right_ref[:, at:to]).reshape(
            4, rows, to - at
        )
    lo, yy = place_ref[1], place_ref[2]
    for k in range(2):
        row = jnp.where(lo == 0, k, 1 - k) * 2
        keep_ref[0, k] = total[row + yy].astype(BF)
        send_ref[0, k] = total[row + 1 - yy].astype(BF)


def weight_grad(place, left, right):
    count = lax.axis_size("hi")
    length, width = right.shape
    rows = left.shape[0] // (4 * count)
    block = pl.BlockSpec((1, 2, rows, width), lambda i, p: (i, 0, 0, 0))
    out = jax.ShapeDtypeStruct((count, 2, rows, width), BF)
    return pl.pallas_call(
        functools.partial(weight_grad_kernel, rows),
        grid_spec=pltpu.PrefetchScalarGridSpec(
            num_scalar_prefetch=1,
            grid=(count,),
            in_specs=[
                pl.BlockSpec((4 * rows, length), lambda i, p: (lax.rem(i + p[0], count), 0)),
                pl.BlockSpec((length, width), lambda i, p: (0, 0)),
            ],
            out_specs=[block] * 2,
            scratch_shapes=[pltpu.VMEM((4, rows, width), F32)],
        ),
        out_shape=[out] * 2,
        compiler_params=pltpu.CompilerParams(vmem_limit_bytes=VMEM_LIMIT),
        cost_estimate=cost(
            flops=2 * length * D * width, bytes_accessed=16 * 2**20, transcendentals=0
        ),
        name="weight_grad",
    )(place, left, right)


def down_kernel(left_ref, right_ref, *out_refs):
    step = pl.program_id(0)
    product = dot_abt(left_ref[...], right_ref[...]).astype(BF)
    for k, ref in enumerate(out_refs):

        @pl.when((step % 2 == k % 2) & (step // 4 == k // 2))
        def _(ref=ref):
            ref[...] = product


def down(left, right):
    length, width = left.shape
    one = length // 8
    parts = [
        pl.BlockSpec((one, D), lambda i, j=j: (jnp.clip((i - j) // 2, 0, 1), 0)) for j in (0, 0, 4, 4)
    ]
    return pl.pallas_call(
        down_kernel,
        grid=(8,),
        in_specs=[
            pl.BlockSpec((one, width), lambda i: (i, 0)),
            pl.BlockSpec((D, width), lambda i: (0, 0)),
        ],
        out_specs=parts,
        out_shape=[jax.ShapeDtypeStruct((2 * one, D), BF)] * 4,
        compiler_params=pltpu.CompilerParams(vmem_limit_bytes=VMEM_LIMIT),
        cost_estimate=cost(
            flops=2 * length * D * width, bytes_accessed=14 * 2**20, transcendentals=0
        ),
        name="down",
    )(left, right)


def total_of(*parts):
    return sum(part.astype(F32) for part in parts)


class EightSum:
    def __init__(self, parts):
        self.keep = parts[:4]
        self.core = [None] * 4
        for k in (3, 1, 2, 0):
            self.core[k] = swap(parts[4 + k], "core")
        self.half = parts[0].shape[0] // 2

    def second(self, order):
        self.core = order.done(self.core)
        half = self.half
        both, by_x, by_lo = [total_of(self.keep[k], self.core[k]) for k in (3, 1, 2)]
        self.to_lo = swap(both[:half].astype(BF), "tensor")
        self.to_x = swap(both[half:].astype(BF), "lo")
        self.x_first = swap(by_x[:half].astype(BF), "tensor")
        self.lo_second = swap(by_lo[half:].astype(BF), "lo")
        self.by_x, self.by_lo = by_x[half:], by_lo[:half]

    def third(self, order):
        to_lo, to_x, self.x_first, self.lo_second = order.done(
            (self.to_lo, self.to_x, self.x_first, self.lo_second)
        )
        self.x_second = swap(total_of(self.by_x, to_x).astype(BF), "tensor")
        self.lo_first = swap(total_of(self.by_lo, to_lo).astype(BF), "lo")

    def total(self, order):
        x_second, lo_first = order.done((self.x_second, self.lo_first))
        return (
            total_of(self.keep[0], self.core[0])
            + jnp.concatenate([self.x_first, x_second], axis=0).astype(F32)
            + jnp.concatenate([lo_first, self.lo_second], axis=0).astype(F32)
        )


class BranchSum:
    def __init__(self, near, by_x, core_near, core_by_x):
        self.near, self.by_x = near, by_x
        self.core = swap(core_by_x, "core"), swap(core_near, "core")

    def along_x(self, order):
        by_x, near = order.done(self.core)
        self.near = total_of(self.near, near)
        self.x = swap(total_of(self.by_x, by_x).astype(BF), "tensor")

    def along_lo(self, order):
        total = self.near + order.done(self.x).astype(F32)
        half = total.shape[0] // 2
        self.own = total[:half]
        self.lo = swap(total[half:].astype(BF), "lo")

    def arrived(self, order):
        self.lo = order.done(self.lo)

    def total(self):
        return self.own + self.lo.astype(F32)


class FourSum:
    def __init__(self, own, first, second, core_own, core_first, core_second):
        self.own, self.x = own, (first, second)
        self.core_x = swap(core_first, "core"), swap(core_second, "core")
        self.core_own = swap(core_own, "core")

    def second(self, order):
        core_x = order.done(self.core_x)
        by_x = [total_of(*pair).astype(BF) for pair in zip(self.x, core_x)]
        self.x = [swap(part, "tensor") for part in by_x]

    def total(self, order):
        self.core_own = order.done(self.core_own)
        x = order.done(self.x)
        return total_of(self.own, self.core_own, jnp.concatenate(x, axis=0))


class GradSum:
    def __init__(self, keep, send):
        self.keep = keep
        self.other = swap(send, "yy")

    def across(self, order, by_gather):
        self.other = order.done(self.other)
        count = lax.axis_size("hi")
        far = [total_of(self.keep[k], self.other[k]).astype(BF) for k in range(1, count)]
        if by_gather:
            self.every = [lax.all_gather(part, "hi") for part in far]
        else:
            self.every = None
            self.far = [turn(part, "hi", k + 1) for k, part in enumerate(far)]

    def arrived(self, order):
        if self.every is None:
            self.far = order.done(self.far)
        else:
            every = order.done(self.every)
            self.far = [others_of(part)[k] for k, part in enumerate(every)]

    def total(self):
        total = self.keep[0].astype(F32) + self.other[0].astype(F32)
        for far in self.far:
            total = total + far.astype(F32)
        return total


def body(
    tokens,
    cotangent,
    segments,
    small_params,
    small_first,
    small_second,
    qkv_weight,
    qkv_first,
    qkv_second,
    out_weight,
    out_first,
    out_second,
    gateup_weight,
    gateup_first,
    gateup_second,
    down_weight,
    down_first,
    down_second,
):
    hi_count = lax.axis_size("hi")
    hi, lo, yy = lax.axis_index("hi"), lax.axis_index("lo"), lax.axis_index("yy")
    core = lax.axis_index("core")
    place_x = lax.axis_index("tensor")
    own_rows = tokens.shape[0]
    shard_rows = qkv_weight.shape[0]
    gain_one = small_params[:D]
    gain_two = small_params[D : 2 * D]
    bias_all = small_params[2 * D :]
    q_at = place_x * (bias_all.shape[0] // 2) + core * Q_COLS
    kv_at = place_x * (bias_all.shape[0] // 2) + 2 * Q_COLS
    bias_local = jnp.concatenate(
        [
            lax.dynamic_slice_in_dim(bias_all, q_at, Q_COLS),
            lax.dynamic_slice_in_dim(bias_all, kv_at, 2 * HEAD_WIDTH),
        ]
    )

    order = Order()
    steps = range(1, hi_count)

    def both_cores(mine, other, axis):
        return jnp.where(
            core == 0,
            jnp.concatenate([mine, other], axis=axis),
            jnp.concatenate([other, mine], axis=axis),
        )

    other_ids = swap(segments, "core")
    qkv_low = qkv_weight.astype(BF)
    out_low = out_weight.astype(BF).T

    def attention_pack(which):
        return jnp.concatenate(
            [
                lax.dynamic_slice_in_dim(qkv_low, which * Q_COLS, Q_COLS, 1),
                qkv_low[:, 2 * Q_COLS :],
                lax.dynamic_slice_in_dim(out_low, which * Q_COLS, Q_COLS, 1),
            ],
            axis=1,
        )

    att_theirs = attention_pack(1 - core)
    att_core = swap(att_theirs, "core")
    order.mark = att_theirs
    rows_in = order.after(tokens).astype(F32)
    scale_one = rms_scale(rows_in)
    n1 = (rows_in * scale_one * gain_one).astype(BF)
    n1_x = swap(n1, "tensor")
    order.mark = n1
    att_shard = both_cores(attention_pack(core), order.done(att_core), 0)
    order.mark = att_shard
    att_hi = [turn(att_shard, "hi", k) for k in steps]
    att_yy = swap(att_shard, "yy")
    att_lo = swap(att_shard, "lo")

    gateup_in, down_in = order.after((gateup_weight, down_weight))
    ff_low = jnp.pad(
        jnp.concatenate([gateup_in.astype(BF), down_in.astype(BF).T[None]], axis=0),
        ((0, 0), (0, 0), (0, FF_PAD - FF_LOCAL)),
    )
    ff_mine = lax.dynamic_slice_in_dim(ff_low, core * FF_CORE, FF_CORE, 2)
    ff_theirs = lax.dynamic_slice_in_dim(ff_low, (1 - core) * FF_CORE, FF_CORE, 2)
    ff_core = swap(ff_theirs, "core")
    order.mark = ff_theirs

    ff_shard = both_cores(ff_mine, order.done(ff_core), 1)
    ff_own = lax.dynamic_slice_in_dim(ff_shard, lo * FF_OWN, FF_OWN, 2)
    ff_theirs = lax.dynamic_slice_in_dim(ff_shard, (1 - lo) * FF_OWN, FF_OWN, 2)
    order.mark = ff_theirs
    att_lo = order.done(att_lo)
    att_lo_yy = swap(att_lo, "yy")
    att_yy = order.done(att_yy)
    att_hi = order.done(att_hi)
    att_hi_lo = [swap(part, "lo") for part in att_hi]
    att_hi_yy = [swap(part, "yy") for part in att_hi]
    n1_core = swap(order.after(n1), "core")
    att_lo_yy = order.done(att_lo_yy)
    att_hi_lo = order.done(att_hi_lo)
    att_hi_lo_yy = [swap(part, "yy") for part in att_hi_lo]
    ff_lo = swap(order.after(ff_theirs), "lo")
    ff_hi = lax.all_gather(order.after(ff_own), "hi")
    n1_core = order.done(n1_core)
    other_ids = order.done(other_ids)
    angles, key_place, row_place, row_start = documents(core, place_x, segments, other_ids)
    sign = jnp.where(jnp.arange(HEAD_WIDTH) < HEAD_WIDTH // 2, -1.0, 1.0)
    tables = order.after((jnp.cos(angles), jnp.sin(angles) * sign, key_place, row_place, row_start))
    order.mark = tables[0]
    att_hi_yy = order.done(att_hi_yy)
    n1_x = order.done(n1_x)
    n1_core_x = swap(n1_x, "core")
    cot_x = swap(order.after(cotangent), "tensor")
    n1_core_x = order.done(n1_core_x)
    att_hi_lo_yy = order.done(att_hi_lo_yy)
    ff_yy = swap(order.after(ff_own), "yy")

    near_parts = [att_shard, att_lo]
    yy_parts = [att_yy, att_lo_yy]
    for k in range(hi_count - 1):
        near_parts += [att_hi[k], att_hi_lo[k]]
        yy_parts += [att_hi_yy[k], att_hi_lo_yy[k]]
    att_parts = near_parts + yy_parts
    n1_parts = order.after((n1, n1_x, n1_core, n1_core_x))
    qkv, attn_rows, lse, *out_parts, att_weight = attention(
        tree_order(-1), n1_parts, bias_local[None], tables, att_parts
    )
    order.mark = lse

    out = FourSum(*out_parts)
    half = own_rows // 2
    cot_x = order.done(cot_x)
    ff_lo = order.done(ff_lo)
    ff_lo_hi_gu = lax.all_gather(ff_lo[:2], "hi")
    ff_yy = order.done(ff_yy)
    ff_lo_yy = swap(ff_lo, "yy")
    out.second(order)
    ff_hi = others_of(order.done(ff_hi))
    order.mark = ff_hi
    residual = rows_in + out.total(order)
    scale_two = rms_scale(residual)
    n2 = (residual * scale_two * gain_two).astype(BF)
    n2_x_second, n2_lo_first = swap(n2[half:], "tensor"), swap(n2[:half], "lo")
    n2_x_first, n2_lo_second = swap(n2[:half], "tensor"), swap(n2[half:], "lo")
    order.mark = n2
    ff_lo_yy = order.done(ff_lo_yy)
    ff_hi_yy = [swap(order.after(part), "yy") for part in ff_hi]
    n2_x_second, n2_lo_first = order.done((n2_x_second, n2_lo_first))
    n2_both = swap(n2_lo_first, "tensor"), swap(n2_x_second, "lo")
    n2_x_first, n2_lo_second = order.done((n2_x_first, n2_lo_second))
    n2_near = jnp.concatenate([n2_x_first, n2_x_second, n2_lo_first, n2_lo_second])
    n2_core_near, n2_core = swap(n2_near, "core"), swap(n2, "core")
    ff_lo_hi_gu = others_of(order.done(ff_lo_hi_gu))
    n2_both = jnp.concatenate(order.done(n2_both))
    n2_core_near, n2_core = order.done((n2_core_near, n2_core))
    n2_core_both = swap(n2_both, "core")
    cot_lo = swap(order.after(cotangent), "lo")
    ff_lo_hi_yy_gu = [swap(order.after(part), "yy") for part in ff_lo_hi_gu]
    ff_lo_hi_d = [turn(order.after(ff_lo[2]), "hi", k) for k in steps]
    ff_hi_yy = order.done(ff_hi_yy)
    cot_both_lo = swap(cot_x[half:], "lo")
    cot_core = swap(order.after(cotangent), "core")
    n2_core_both = order.done(n2_core_both)
    ff_lo_hi_yy_gu = order.done(ff_lo_hi_yy_gu)
    n2_parts = [n2, n2_near, n2_both, n2_core, n2_core_near, n2_core_both]

    whole = [ff_own, ff_lo, ff_yy, ff_lo_yy, *ff_hi, *ff_hi_yy]
    gu_pieces = [*whole, *ff_lo_hi_gu, *ff_lo_hi_yy_gu]
    ff_chips = [chip_at(0, l, y) for y in (0, 1) for l in (0, 1)]
    ff_chips += [chip_at(-k, l, y) for l in (0, 1) for y in (0, 1) for k in steps]
    ff_chips = jnp.stack(ff_chips).astype(jnp.int32)
    gates, n2_t = gate_up(ff_chips, order.after(n2_parts), gu_pieces)
    order.mark = gates
    cot_lo = order.done(cot_lo)
    cot_both_x = swap(cot_lo[:half], "tensor")
    cot_near = jnp.concatenate([cot_x, cot_lo])
    cot_core_near = swap(cot_near, "core")
    ff_lo_hi_d = order.done(ff_lo_hi_d)
    ff_lo_hi_yy_d = [swap(part, "yy") for part in ff_lo_hi_d]
    cot_core, cot_both_lo = order.done((cot_core, cot_both_lo))
    cot_both = jnp.concatenate([order.done(cot_both_x), cot_both_lo])
    cot_core_both = swap(cot_both, "core")
    cot_core_near = order.done(cot_core_near)
    ff_lo_hi_yy_d = order.done(ff_lo_hi_yy_d)
    cot_core_both = order.done(cot_core_both)
    cot_parts = [cotangent, cot_near, cot_both, cot_core, cot_core_near, cot_core_both]
    d_pieces = [*whole, *ff_lo_hi_d, *ff_lo_hi_yy_d]
    *dn2_parts, hidden, gate_grad, up_grad, cot_t, w_down = feed_forward(
        ff_chips, gates, order.after(cot_parts), gu_pieces, d_pieces
    )
    order.mark = w_down

    place = jnp.stack([hi, lo, yy]).astype(jnp.int32)

    def grad_of(left, right):
        keep, send = weight_grad(place, order.after(left), right)
        order.mark = keep
        return GradSum(keep, send)

    ff_squares = 0.0
    rows_of = lambda value, which, axis: lax.dynamic_slice_in_dim(
        value, which * shard_rows, shard_rows, axis
    )

    def summed_up(grad):
        nonlocal ff_squares
        total = order.after(grad.total())
        ff_squares = ff_squares + jnp.sum(total * total)
        low = total.astype(BF)
        order.mark = low
        return low[0], swap(low[1], "lo")

    def own_rows_of(low, other):
        other = order.done(other)
        cols = jnp.where(
            lo == 0,
            jnp.concatenate([low, other], axis=1),
            jnp.concatenate([other, low], axis=1),
        )
        theirs = rows_of(cols, 1 - core, 0)
        order.mark = theirs
        return rows_of(cols, core, 0), swap(theirs, "core")

    dn2 = EightSum(dn2_parts)
    d_sum = grad_of(cot_t, hidden)
    dn2.second(order)
    g_sum = grad_of(n2_t, gate_grad)
    dn2.third(order)
    u_sum = grad_of(n2_t, up_grad)
    d_sum.across(order, True)
    norm_two_in, gain_two_grad = norm_backward(residual, scale_two, gain_two, dn2.total(order))
    residual_grad = cotangent.astype(F32) + norm_two_in
    da = residual_grad.astype(BF)
    da_x = [swap(da[:half], "tensor"), swap(da[half:], "tensor")]
    da_core = swap(da, "core")
    order.mark = da
    branch_parts = down(*order.after((hidden, w_down)))
    order.mark = branch_parts[0]
    branch = BranchSum(*branch_parts)
    da_x = order.done(da_x)
    da_core_x = [swap(part, "core") for part in da_x]
    da_core, da_core_x = order.done((da_core, da_core_x))
    g_sum.across(order, False)

    _, bias_grad, *parts = attention_back(
        sum_order(),
        order.after((da, *da_x, da_core, *da_core_x)),
        n1_parts,
        qkv,
        attn_rows,
        lse,
        att_weight,
        tables,
    )
    order.mark = bias_grad
    d_sum.arrived(order)
    dn1 = FourSum(*parts[:6])
    att = ChipSum(*parts[6:])
    dn1.second(order)
    norm_one_in, gain_one_grad = norm_backward(rows_in, scale_one, gain_one, dn1.total(order))
    g_sum.arrived(order)
    branch.along_x(order)
    u_sum.across(order, False)
    att.far_yy(order)
    bias_grad = order.after(bias_grad)[0]
    bias_slots = lax.dynamic_update_slice_in_dim(
        jnp.zeros_like(bias_all), bias_grad[:Q_COLS], q_at, 0
    )
    bias_slots = lax.dynamic_update_slice_in_dim(bias_slots, bias_grad[Q_COLS:], kv_at, 0)
    att.far_hi(order)
    d_low, d_way = summed_up(d_sum)
    g_low, g_way = summed_up(g_sum)
    att.near_yy(order)
    input_grad = residual_grad + norm_one_in
    branch.along_lo(order)
    u_sum.arrived(order)
    att_sum = att.total(order)
    att_low = att_sum.astype(BF)
    other_att = swap(rows_of(att_low, 1 - core, 0), "core")
    u_low, u_way = summed_up(u_sum)
    other_att = order.done(other_att)
    d_rows = own_rows_of(d_low, d_way)
    g_rows = own_rows_of(g_low, g_way)
    branch.arrived(order)

    own_att = rows_of(att_low, core, 0)
    first_att = jnp.where(core == 0, own_att, other_att).astype(F32)
    second_att = jnp.where(core == 0, other_att, own_att).astype(F32)
    kv_sum = first_att[:, Q_COLS:QKV_COLS] + second_att[:, Q_COLS:QKV_COLS]
    qkv_owned = jnp.concatenate([first_att[:, :Q_COLS], second_att[:, :Q_COLS], kv_sum], axis=1)
    out_owned = jnp.concatenate([first_att[:, QKV_COLS:], second_att[:, QKV_COLS:]], axis=1).T
    owned_squares = (
        jnp.sum(qkv_owned * qkv_owned) + jnp.sum(out_owned * out_owned) + ff_squares
    )
    summed = jnp.concatenate(
        [gain_one_grad, gain_two_grad, bias_slots, jnp.full((128,), owned_squares)]
    )
    summed = summed + order.done(swap(summed, "core"))
    summed = summed + order.done(swap(summed, "tensor"))
    summed = summed + order.done(swap(summed, "yy"))
    summed = summed + order.done(swap(summed, "lo"))
    step = 1
    while step < hi_count:
        moved = lax.ppermute(summed, "hi", [(i, i ^ step) for i in range(hi_count)])
        summed = summed + order.done(moved)
        step *= 2
    order.mark = summed
    u_rows = own_rows_of(u_low, u_way)
    block_out = (residual + order.after(branch.total())).astype(BF)

    def owned(rows):
        mine, other = rows
        return both_cores(mine, other, 1)[:, :FF_LOCAL].astype(F32)

    gateup_owned = jnp.stack([owned(g_rows), owned(u_rows)])
    down_owned = owned(d_rows).T
    small_grad = summed[:-128]
    squares = summed[-1] + jnp.sum(small_grad * small_grad)
    grad_norm = jnp.sqrt(squares)
    clip_factor = jnp.minimum(1.0, MAX_NORM / (grad_norm + 1e-06))
    new_small, new_small_first, new_small_second = adam_update(
        small_params, small_first, small_second, clip_factor * small_grad, 0.5, 0.0
    )
    new_qkv, new_qkv_first, new_qkv_second = adam_update(
        qkv_weight, qkv_first, qkv_second, clip_factor * qkv_owned, 2.0 / math.sqrt(D), WEIGHT_DECAY
    )
    new_out, new_out_first, new_out_second = adam_update(
        out_weight,
        out_first,
        out_second,
        clip_factor * out_owned,
        8.0 / math.sqrt(QUERY_HEADS * HEAD_WIDTH),
        WEIGHT_DECAY,
    )
    new_gateup, new_gateup_first, new_gateup_second = adam_update(
        gateup_weight,
        gateup_first,
        gateup_second,
        clip_factor * gateup_owned,
        2.0 / math.sqrt(D),
        WEIGHT_DECAY,
    )
    new_down, new_down_first, new_down_second = adam_update(
        down_weight,
        down_first,
        down_second,
        clip_factor * down_owned,
        3.0 / math.sqrt(FF),
        WEIGHT_DECAY,
    )
    return (
        block_out,
        input_grad,
        grad_norm,
        new_small,
        new_small_first,
        new_small_second,
        new_qkv,
        new_qkv_first,
        new_qkv_second,
        new_out,
        new_out_first,
        new_out_second,
        new_gateup,
        new_gateup_first,
        new_gateup_second,
        new_down,
        new_down_first,
        new_down_second,
    )


def solution(mesh):
    count = mesh.shape["dp"]
    fine = Mesh(
        mesh.devices.reshape(count // 8, 2, 2, 2, mesh.shape["tensor"]),
        CHIP + ("core", "tensor"),
    )
    dp = CHIP + ("core",)
    rows = P(dp + ("tensor",), None)
    by_rows = P(dp, "tensor")
    by_cols = P("tensor", dp)
    stacked = P(None, dp, "tensor")
    weights = (by_rows,) * 3 + (by_cols,) * 3 + (stacked,) * 3 + (by_cols,) * 3
    return jax.shard_map(
        body,
        mesh=fine,
        in_specs=(rows, rows, P(dp), P(), P(), P()) + weights,
        out_specs=(rows, rows, P(), P(), P(), P()) + weights,
        check_vma=False,
    )
```

```python
import functools
import math

import jax
import jax.numpy as jnp
import numpy as np
from jax import lax
from jax.experimental import pallas as pl
from jax.experimental.pallas import tpu as pltpu
from jax.sharding import Mesh
from jax.sharding import PartitionSpec as P

D = 1536
FF = 8960
QUERY_HEADS = 12
KEY_VALUE_HEADS = 2
HEAD_WIDTH = 128
STEP = 10

EPSILON = 1e-06
ROPE_BASE = 1000000.0
BETA_ONE = 0.9
BETA_TWO = 0.999
ADAM_EPS = 1e-08
WEIGHT_DECAY = 0.1
MAX_NORM = 1.0
NEGATIVE = -1e30

BF = jnp.bfloat16
F32 = jnp.float32
HEADS = 3
Q_COLS = HEADS * HEAD_WIDTH
QKV_COLS = Q_COLS + 2 * HEAD_WIDTH
ATT_COLS = QKV_COLS + Q_COLS
FF_LOCAL = FF // 2
FF_PAD = 4608
FF_CORE = FF_PAD // 2
FF_OWN = FF_PAD // 4
TILE = 256
VMEM_LIMIT = 60 * 2**20
CHIP = ("hi", "lo", "yy")


def dot_ab(a, b):
    return lax.dot_general(a, b, (((1,), (0,)), ((), ())), preferred_element_type=F32)


def dot_abt(a, b):
    return lax.dot_general(a, b, (((1,), (1,)), ((), ())), preferred_element_type=F32)


def dot_atb(a, b):
    return lax.dot_general(a, b, (((0,), (0,)), ((), ())), preferred_element_type=F32)


def rms_scale(inputs):
    return lax.rsqrt(jnp.mean(inputs * inputs, axis=-1, keepdims=True) + EPSILON)


def norm_backward(inputs, inv_rms, gain_vec, upstream):
    normed = inputs * inv_rms
    normed_grad = upstream * gain_vec
    input_part = inv_rms * (
        normed_grad - normed * jnp.mean(normed_grad * normed, axis=-1, keepdims=True)
    )
    return (input_part, jnp.sum(upstream * normed, axis=0))


def adam_update(weight, moment_one, moment_two, gradient, step_rate, decay_rate):
    first_new = BETA_ONE * moment_one + (1.0 - BETA_ONE) * gradient
    second_new = BETA_TWO * moment_two + (1.0 - BETA_TWO) * gradient * gradient
    corrected = first_new / (1.0 - BETA_ONE**STEP)
    spread = jnp.sqrt(second_new / (1.0 - BETA_TWO**STEP)) + ADAM_EPS
    return (
        weight * (1.0 - step_rate * decay_rate) - step_rate * corrected / spread,
        first_new,
        second_new,
    )


def swap(value, axis):
    return lax.ppermute(value, axis, [(0, 1), (1, 0)])


class Order:
    def __init__(self):
        self.mark = None

    def after(self, value):
        if self.mark is None:
            return value
        return lax.optimization_barrier((value, self.mark))[0]

    def done(self, value):
        value = self.after(value)
        self.mark = value
        return value


def chip_at(step, other_lo, other_yy):
    count = lax.axis_size("hi")
    hi = (lax.axis_index("hi") + step) % count
    return (hi * 2 + (lax.axis_index("lo") ^ other_lo)) * 2 + (lax.axis_index("yy") ^ other_yy)


def turn(value, axis, steps):
    count = lax.axis_size(axis)
    return lax.ppermute(value, axis, [(i, (i + steps) % count) for i in range(count)])


def others_of(every):
    count = lax.axis_size("hi")
    hi = lax.axis_index("hi")
    return [
        lax.dynamic_index_in_dim(every, (hi - k) % count, 0, keepdims=False)
        for k in range(1, count)
    ]


def tree_order(sign):
    steps = [(0, 0), (0, 1)] + [(k, l) for k in range(1, lax.axis_size("hi")) for l in (0, 1)]
    return jnp.stack([chip_at(sign * k, l, y) for y in (0, 1) for k, l in steps]).astype(jnp.int32)


def sum_order():
    steps = range(1, lax.axis_size("hi"))
    chips = [chip_at(k, l, y) for l in (1, 0) for ks in (steps, (0,)) for k in ks for y in (1, 0)]
    return jnp.stack(chips).astype(jnp.int32)


class ChipSum:
    def __init__(self, lo_far, lo_near, far, near):
        self.far, self.near, self.lo_near = far, near, lo_near
        self.lo_far = swap(lo_far, "lo")

    def far_yy(self, order):
        self.far = self.far.astype(F32) + order.done(self.lo_far).astype(F32)
        theirs = self.far[0::2].astype(BF)
        self.yy_far = swap(theirs, "yy")
        order.mark = theirs
        self.lo_near = swap(order.after(self.lo_near), "lo")

    def far_hi(self, order):
        far = (self.far[1::2] + order.done(self.yy_far).astype(F32)).astype(BF)
        self.hi = [turn(far[k - 1], "hi", k) for k in range(1, lax.axis_size("hi"))]
        order.mark = far

    def near_yy(self, order):
        self.near = self.near.astype(F32) + order.done(self.lo_near).astype(F32)
        theirs = self.near[0].astype(BF)
        self.yy_near = swap(theirs, "yy")
        order.mark = theirs

    def total(self, order):
        hi = order.done(self.hi)
        total = self.near[1] + order.done(self.yy_near).astype(F32)
        for part in hi:
            total = total + part.astype(F32)
        return total


def cost(flops, bytes_accessed, transcendentals):
    part = 4096
    return pl.CostEstimate(
        flops=flops // part,
        bytes_accessed=bytes_accessed // part,
        transcendentals=transcendentals // part,
    )


ANYWHERE = pl.BlockSpec(memory_space=pl.ANY)
WHOLE = pl.BlockSpec(memory_space=pltpu.VMEM)


def turn_halves(features, cos_both, sin_both):
    return features * cos_both + pltpu.roll(features, HEAD_WIDTH // 2, 1) * sin_both


def scores_t(keys, queries, key_place, place, start):
    scores = dot_abt(keys, queries) * (1.0 / math.sqrt(HEAD_WIDTH))
    return jnp.where((key_place <= place) & (key_place >= start), scores, NEGATIVE)


def rows_from(refs):
    begin = 0
    for ref in refs:
        yield slice(begin, begin + ref.shape[0]), ref
        begin += ref.shape[0]


def attention_kernel(blocks, parts, rows, chips_ref, *refs):
    n1_refs, refs = refs[:blocks], refs[blocks:]
    bias_ref, cos_ref, sin_ref, key_place_ref, place_ref, start_ref, *refs = refs
    shards, refs = refs[:parts], refs[parts:]
    qkv_ref, o_ref, lse_ref, *out_refs, weight_ref, weights, sems, out_sem = refs
    length = qkv_ref.shape[0]
    copies = [
        pltpu.make_async_copy(
            shards[i],
            weights.at[pl.ds(pl.multiple_of(chips_ref[i] * rows, rows), rows), :],
            sems.at[i],
        )
        for i in range(parts)
    ]
    for copy in copies:
        copy.start()
    for copy in copies:
        copy.wait()
    save = pltpu.make_async_copy(weights, weight_ref, out_sem)
    save.start()
    for at, ref in rows_from(n1_refs):
        projected = dot_ab(ref[...], weights[:, :QKV_COLS]) + bias_ref[...]
        cos_both, sin_both = cos_ref[at, :], sin_ref[at, :]
        for j in range(HEADS + 1):
            cols = slice(j * HEAD_WIDTH, (j + 1) * HEAD_WIDTH)
            qkv_ref[at, cols] = turn_halves(projected[:, cols], cos_both, sin_both).astype(BF)
        cols = slice(Q_COLS + HEAD_WIDTH, QKV_COLS)
        qkv_ref[at, cols] = projected[:, cols].astype(BF)
    keys = qkv_ref[:, Q_COLS : Q_COLS + HEAD_WIDTH]
    values_t = qkv_ref[:, Q_COLS + HEAD_WIDTH : QKV_COLS].T
    lse_ref[...] = jnp.zeros_like(lse_ref)
    key_place = key_place_ref[...]
    for at in range(0, length, TILE):
        block = slice(at, at + TILE)
        place, start = place_ref[:, block], start_ref[:, block]
        for h in range(HEADS):
            cols = slice(h * HEAD_WIDTH, (h + 1) * HEAD_WIDTH)
            scores = scores_t(keys, qkv_ref[block, cols], key_place, place, start)
            top = jnp.max(scores, axis=0, keepdims=True)
            weights_exp = jnp.exp(scores - top)
            total = jnp.sum(weights_exp, axis=0, keepdims=True)
            lse_ref[h : h + 1, block] = top + jnp.log(total)
            prob = (weights_exp * (1.0 / total)).astype(BF)
            o_ref[block, cols] = dot_ab(values_t, prob).astype(BF).T
    for at, ref in rows_from(out_refs):
        ref[...] = dot_abt(o_ref[at, :], weights[:, QKV_COLS:]).astype(BF)
    save.wait()


def documents_kernel(where_ref, ids_ref, other_ref, frequency_ref, angle_ref, key_place_ref, place_ref, start_ref):
    core, place_x = where_ref[0], where_ref[1]
    one = ids_ref.shape[1]

    def in_order(ref):
        rows = [ref[k : k + 1, :] for k in range(2)]
        return [
            jnp.where(place_x == 0, rows[0], rows[1]),
            jnp.where(place_x == 0, rows[1], rows[0]),
        ]

    ids = jnp.concatenate(in_order(ids_ref) + in_order(other_ref), axis=1)
    index = lax.broadcasted_iota(jnp.int32, (1, 4 * one), 1)
    block = index // one
    mine = core * 2 + place_x
    place = jnp.bitwise_xor(mine, block) * one + index - block * one

    def column(row):
        return jnp.broadcast_to(row.astype(F32), (8, 4 * one)).T[:, :1]

    ids_col, place_col = column(ids), column(place)
    ids_row, place_row = ids.astype(F32), place.astype(F32)
    start_row = jnp.min(
        jnp.where(ids_col == ids_row, place_col, 4.0 * one), axis=0, keepdims=True
    )
    place_ref[...] = place
    start_ref[...] = start_row.astype(jnp.int32)
    key_place_ref[...] = place_col.astype(jnp.int32)
    angle_ref[...] = column(place_row - start_row) * frequency_ref[...]


def documents(core, place_x, ids, other_ids):
    one = ids.shape[0] // 2
    exponent = np.arange(0, HEAD_WIDTH, 2, dtype=np.float32) / np.float32(HEAD_WIDTH)
    frequency = np.float32(1.0) / np.float32(ROPE_BASE) ** exponent
    return pl.pallas_call(
        documents_kernel,
        grid_spec=pltpu.PrefetchScalarGridSpec(
            num_scalar_prefetch=1,
            grid=(),
            in_specs=[WHOLE] * 3,
            out_specs=[WHOLE] * 4,
        ),
        out_shape=[
            jax.ShapeDtypeStruct((4 * one, HEAD_WIDTH), F32),
            jax.ShapeDtypeStruct((4 * one, 1), jnp.int32),
            jax.ShapeDtypeStruct((1, 4 * one), jnp.int32),
            jax.ShapeDtypeStruct((1, 4 * one), jnp.int32),
        ],
        compiler_params=pltpu.CompilerParams(vmem_limit_bytes=VMEM_LIMIT),
        cost_estimate=cost(flops=2**20, bytes_accessed=2**20, transcendentals=0),
        name="documents",
    )(
        jnp.stack([core, place_x]).astype(jnp.int32),
        ids.reshape(2, one),
        other_ids.reshape(2, one),
        jnp.asarray(np.concatenate([frequency, frequency])[None]),
    )


def four_shapes(rows):
    return [jax.ShapeDtypeStruct((r, D), BF) for r in (rows, rows // 2, rows // 2) * 2]


def attention(chips, n1, bias, tables, shards):
    length = tables[0].shape[0]
    parts = len(shards)
    rows = shards[0].shape[0]
    return pl.pallas_call(
        functools.partial(attention_kernel, len(n1), parts, rows),
        grid_spec=pltpu.PrefetchScalarGridSpec(
            num_scalar_prefetch=1,
            grid=(),
            in_specs=[WHOLE] * (len(n1) + 6) + [ANYWHERE] * parts,
            out_specs=[WHOLE] * 9 + [ANYWHERE],
            scratch_shapes=[
                pltpu.VMEM((D, ATT_COLS), BF),
                pltpu.SemaphoreType.DMA((parts,)),
                pltpu.SemaphoreType.DMA,
            ],
        ),
        out_shape=[
            jax.ShapeDtypeStruct((length, QKV_COLS), BF),
            jax.ShapeDtypeStruct((length, Q_COLS), BF),
            jax.ShapeDtypeStruct((8, length), F32),
            *four_shapes(length // 4),
            jax.ShapeDtypeStruct((D, ATT_COLS), BF),
        ],
        compiler_params=pltpu.CompilerParams(vmem_limit_bytes=VMEM_LIMIT),
        cost_estimate=cost(
            flops=2 * length * D * ATT_COLS + 4 * HEADS * length * length * HEAD_WIDTH,
            bytes_accessed=16 * 2**20,
            transcendentals=HEADS * length * length,
        ),
        name="attention",
    )(chips, *n1, bias, *tables, *shards)


def attention_back_kernel(das, n1s, count, rows, chips_ref, *refs):
    da_refs, n1_refs, refs = refs[:das], refs[das : das + n1s], refs[das + n1s :]
    qkv_ref, o_ref, lse_ref, weight_ref, *refs = refs
    cos_ref, sin_ref, key_place_ref, place_ref, start_ref, *refs = refs
    dqkv_ref, bias_ref, *refs = refs
    dn1_refs, block_refs, (mixed, left_t, grads) = refs[:6], refs[6:10], refs[10:]
    length = qkv_ref.shape[0]
    scale = 1.0 / math.sqrt(HEAD_WIDTH)
    for at, ref in rows_from(da_refs):
        mixed[at, :] = dot_ab(ref[...], weight_ref[:, QKV_COLS:]).astype(BF)
    key_cols = slice(Q_COLS, Q_COLS + HEAD_WIDTH)
    value_cols = slice(Q_COLS + HEAD_WIDTH, QKV_COLS)
    keys, values = qkv_ref[:, key_cols], qkv_ref[:, value_cols]
    keys_t = keys.T
    key_place = key_place_ref[...]
    keys_grad = jnp.zeros((length, HEAD_WIDTH), F32)
    values_grad = jnp.zeros((length, HEAD_WIDTH), F32)
    for at in range(0, length, TILE):
        block = slice(at, at + TILE)
        place, start = place_ref[:, block], start_ref[:, block]
        for h in range(HEADS):
            cols = slice(h * HEAD_WIDTH, (h + 1) * HEAD_WIDTH)
            queries, up = qkv_ref[block, cols], mixed[block, cols]
            scores = scores_t(keys, queries, key_place, place, start)
            prob = jnp.exp(scores - lse_ref[h : h + 1, block])
            prob_grad = dot_abt(values, up)
            inner = jnp.sum(prob * prob_grad, axis=0, keepdims=True)
            score_grad = (prob * (prob_grad - inner)).astype(BF)
            values_grad += dot_ab(prob.astype(BF), up)
            keys_grad += dot_ab(score_grad, queries)
            query_grad = dot_ab(keys_t, score_grad).T * scale
            dqkv_ref[block, cols] = turn_halves(
                query_grad, cos_ref[block, :], -sin_ref[block, :]
            ).astype(BF)
    dqkv_ref[:, key_cols] = turn_halves(keys_grad * scale, cos_ref[...], -sin_ref[...]).astype(BF)
    dqkv_ref[:, value_cols] = values_grad.astype(BF)
    bias_ref[...] = jnp.sum(dqkv_ref[...].astype(F32), axis=0, keepdims=True)
    for cols, left_refs, right_ref in (
        (slice(0, QKV_COLS), n1_refs, dqkv_ref),
        (slice(QKV_COLS, ATT_COLS), da_refs, o_ref),
    ):
        for at, ref in rows_from(left_refs):
            left_t[:, at] = ref[...].T
        grads[:, :, cols] = (
            dot_ab(left_t[...], right_ref[...]).astype(BF).reshape(4 * count, rows, -1)
        )
    at = 0
    for ref in block_refs:
        for k in range(ref.shape[0]):
            ref[k] = grads[chips_ref[at]]
            at += 1
    for at, ref in rows_from(dn1_refs):
        ref[...] = dot_abt(dqkv_ref[at, :], weight_ref[:, :QKV_COLS]).astype(BF)


def attention_back(chips, da, n1, qkv, o, lse, weight, tables):
    length = qkv.shape[0]
    count = chips.shape[0] // 4
    rows = D // (4 * count)
    blocks = [
        jax.ShapeDtypeStruct((2 * k, rows, ATT_COLS), BF) for k in (count - 1, 1, count - 1, 1)
    ]
    return pl.pallas_call(
        functools.partial(attention_back_kernel, len(da), len(n1), count, rows),
        grid_spec=pltpu.PrefetchScalarGridSpec(
            num_scalar_prefetch=1,
            grid=(),
            in_specs=[WHOLE] * (len(da) + len(n1) + 9),
            out_specs=[WHOLE] * 12,
            scratch_shapes=[
                pltpu.VMEM((length, Q_COLS), BF),
                pltpu.VMEM((D, length), BF),
                pltpu.VMEM((4 * count, rows, ATT_COLS), BF),
            ],
        ),
        out_shape=[
            jax.ShapeDtypeStruct((length, QKV_COLS), BF),
            jax.ShapeDtypeStruct((1, QKV_COLS), F32),
            *four_shapes(length // 4),
            *blocks,
        ],
        compiler_params=pltpu.CompilerParams(vmem_limit_bytes=VMEM_LIMIT),
        cost_estimate=cost(
            flops=2 * length * D * 2 * ATT_COLS + 10 * HEADS * length * length * HEAD_WIDTH,
            bytes_accessed=24 * 2**20,
            transcendentals=HEADS * length * length,
        ),
        name="attention_back",
    )(chips, *da, *n1, qkv, o, lse, weight, *tables)


def tile_copies(j, taken, tiles, sems, one):
    part, row = divmod(j, 4)
    ref, at = ((0, 0), (1, 0), (1, one), (2, 0))[row]
    return pltpu.make_async_copy(
        taken[3 * part + ref].at[pl.ds(at, one), :], tiles.at[j % 2], sems.at[j % 2]
    )


def take_tile(step, taken, tiles, sems, one):
    for j in range(8):

        @pl.when(step == j)
        def _(j=j):
            if j < 7:
                tile_copies(j + 1, taken, tiles, sems, one).start()
            tile_copies(j, taken, tiles, sems, one).wait()


def weight_copies(pieces, chips_ref, rows, wide, there, sems):
    for i, piece in enumerate(pieces):
        at = pl.ds(pl.multiple_of(chips_ref[i] * rows, rows), rows)
        for j in range(wide):
            here = piece if piece.ndim == 2 else piece.at[j if wide > 1 else 2]
            yield pltpu.make_async_copy(
                here, there.at[at, pl.ds(j * FF_OWN, FF_OWN)], sems.at[i, j]
            )


def gate_up_kernel(count, rows, chips_ref, *refs):
    n2_refs, pieces, refs = refs[:6], refs[6 : 6 + count], refs[6 + count :]
    gate_up_ref, n2_t_ref, weights, tiles, tile_sems, sems = refs
    step = pl.program_id(0)
    one = tiles.shape[1]
    copies = list(weight_copies(pieces, chips_ref, rows, 2, weights, sems))

    @pl.when(step == 0)
    def _():
        for copy in copies:
            copy.start()
        tile_copies(0, n2_refs, tiles, tile_sems, one).start()
        for copy in copies:
            copy.wait()

    take_tile(step, n2_refs, tiles, tile_sems, one)
    n2 = tiles[step % 2]
    n2_t_ref[...] = n2.T
    gate_up_ref[...] = dot_ab(n2, weights[...]).astype(BF)


def gate_up(chips, n2, pieces):
    rows = pieces[0].shape[1]
    one = n2[0].shape[0]
    length = 8 * one
    return pl.pallas_call(
        functools.partial(gate_up_kernel, len(pieces), rows),
        grid_spec=pltpu.PrefetchScalarGridSpec(
            num_scalar_prefetch=1,
            grid=(8,),
            in_specs=[ANYWHERE] * (6 + len(pieces)),
            out_specs=[
                pl.BlockSpec((one, 2 * FF_OWN), lambda i, c: (i, 0)),
                pl.BlockSpec((D, one), lambda i, c: (0, i)),
            ],
            scratch_shapes=[
                pltpu.VMEM((D, 2 * FF_OWN), BF),
                pltpu.VMEM((2, one, D), BF),
                pltpu.SemaphoreType.DMA((2,)),
                pltpu.SemaphoreType.DMA((len(pieces), 2)),
            ],
        ),
        out_shape=[
            jax.ShapeDtypeStruct((length, 2 * FF_OWN), BF),
            jax.ShapeDtypeStruct((D, length), BF),
        ],
        compiler_params=pltpu.CompilerParams(vmem_limit_bytes=VMEM_LIMIT),
        cost_estimate=cost(
            flops=4 * length * D * FF_OWN, bytes_accessed=30 * 2**20, transcendentals=0
        ),
        name="gate_up",
    )(chips, *n2, *pieces)


def feed_forward_kernel(count, rows, chips_ref, gate_up_ref, *refs):
    dy_refs, refs = refs[:6], refs[6:]
    gu_pieces, d_pieces, refs = refs[:count], refs[count : 2 * count], refs[2 * count :]
    dn2_refs, refs = refs[:8], refs[8:]
    u_ref, dgate_ref, dup_ref, dy_t_ref, down_ref, *refs = refs
    gu_w, d_w, tiles, tile_sems, gu_sems, d_sems, out_sem = refs
    step = pl.program_id(0)
    one = tiles.shape[1]
    gu_copies = list(weight_copies(gu_pieces, chips_ref, rows, 2, gu_w, gu_sems))
    d_copies = list(weight_copies(d_pieces, chips_ref, rows, 1, d_w, d_sems))
    save = pltpu.make_async_copy(d_w, down_ref, out_sem)

    @pl.when(step == 0)
    def _():
        for copy in d_copies:
            copy.start()
        tile_copies(0, dy_refs, tiles, tile_sems, one).start()
        for copy in gu_copies:
            copy.start()
        for copy in d_copies:
            copy.wait()
        save.start()

    take_tile(step, dy_refs, tiles, tile_sems, one)
    dy = tiles[step % 2]
    dy_t_ref[...] = dy.T
    du = dot_ab(dy, d_w[...])
    gate = gate_up_ref[:, :FF_OWN].astype(F32)
    up = gate_up_ref[:, FF_OWN:].astype(F32)
    sig = jax.nn.sigmoid(gate)
    silu = gate * sig
    u_ref[...] = (silu * up).astype(BF)
    dup = (du * silu).astype(BF)
    dgate = (du * up * sig * (1.0 + gate * (1.0 - sig))).astype(BF)
    dup_ref[...] = dup
    dgate_ref[...] = dgate

    @pl.when(step == 0)
    def _():
        for copy in gu_copies:
            copy.wait()

    dn2 = dot_abt(jnp.concatenate([dgate, dup], axis=1), gu_w[...]).astype(BF)
    for j in range(8):

        @pl.when(step == j)
        def _(j=j):
            dn2_refs[j][...] = dn2

    @pl.when(step == pl.num_programs(0) - 1)
    def _():
        save.wait()


def feed_forward(chips, gates, dy, gu_pieces, d_pieces):
    count = len(d_pieces)
    rows = d_pieces[0].shape[-2]
    one = dy[0].shape[0]
    length = 8 * one
    tile = lambda width: pl.BlockSpec((one, width), lambda i, c: (i, 0))
    kept = pl.BlockSpec((one, D), lambda i, c: (0, 0))
    return pl.pallas_call(
        functools.partial(feed_forward_kernel, count, rows),
        grid_spec=pltpu.PrefetchScalarGridSpec(
            num_scalar_prefetch=1,
            grid=(8,),
            in_specs=[tile(2 * FF_OWN)] + [ANYWHERE] * (6 + 2 * count),
            out_specs=[kept] * 8
            + [tile(FF_OWN)] * 3
            + [pl.BlockSpec((D, one), lambda i, c: (0, i)), ANYWHERE],
            scratch_shapes=[
                pltpu.VMEM((D, 2 * FF_OWN), BF),
                pltpu.VMEM((D, FF_OWN), BF),
                pltpu.VMEM((2, one, D), BF),
                pltpu.SemaphoreType.DMA((2,)),
                pltpu.SemaphoreType.DMA((count, 2)),
                pltpu.SemaphoreType.DMA((count, 1)),
                pltpu.SemaphoreType.DMA,
            ],
        ),
        out_shape=[jax.ShapeDtypeStruct((one, D), BF)] * 8
        + [jax.ShapeDtypeStruct((length, FF_OWN), BF)] * 3
        + [jax.ShapeDtypeStruct((D, length), BF), jax.ShapeDtypeStruct((D, FF_OWN), BF)],
        compiler_params=pltpu.CompilerParams(vmem_limit_bytes=VMEM_LIMIT),
        cost_estimate=cost(
            flops=6 * length * D * FF_OWN,
            bytes_accessed=50 * 2**20,
            transcendentals=length * FF_OWN,
        ),
        name="feed_forward",
    )(chips, gates, *dy, *gu_pieces, *d_pieces)


def weight_grad_kernel(rows, place_ref, left_ref, right_ref, *refs):
    keep_ref, send_ref, total = refs
    width = right_ref.shape[1]
    for at in range(0, width, 256):
        to = min(at + 256, width)
        total[:, :, at:to] = dot_ab(left_ref[...], right_ref[:, at:to]).reshape(
            4, rows, to - at
        )
    lo, yy = place_ref[1], place_ref[2]
    for k in range(2):
        row = jnp.where(lo == 0, k, 1 - k) * 2
        keep_ref[0, k] = total[row + yy].astype(BF)
        send_ref[0, k] = total[row + 1 - yy].astype(BF)


def weight_grad(place, left, right):
    count = lax.axis_size("hi")
    length, width = right.shape
    rows = left.shape[0] // (4 * count)
    block = pl.BlockSpec((1, 2, rows, width), lambda i, p: (i, 0, 0, 0))
    out = jax.ShapeDtypeStruct((count, 2, rows, width), BF)
    return pl.pallas_call(
        functools.partial(weight_grad_kernel, rows),
        grid_spec=pltpu.PrefetchScalarGridSpec(
            num_scalar_prefetch=1,
            grid=(count,),
            in_specs=[
                pl.BlockSpec((4 * rows, length), lambda i, p: (lax.rem(i + p[0], count), 0)),
                pl.BlockSpec((length, width), lambda i, p: (0, 0)),
            ],
            out_specs=[block] * 2,
            scratch_shapes=[pltpu.VMEM((4, rows, width), F32)],
        ),
        out_shape=[out] * 2,
        compiler_params=pltpu.CompilerParams(vmem_limit_bytes=VMEM_LIMIT),
        cost_estimate=cost(
            flops=2 * length * D * width, bytes_accessed=16 * 2**20, transcendentals=0
        ),
        name="weight_grad",
    )(place, left, right)


def down_kernel(left_ref, right_ref, *out_refs):
    step = pl.program_id(0)
    product = dot_abt(left_ref[...], right_ref[...]).astype(BF)
    for k, ref in enumerate(out_refs):

        @pl.when((step % 2 == k % 2) & (step // 4 == k // 2))
        def _(ref=ref):
            ref[...] = product


def down(left, right):
    length, width = left.shape
    one = length // 8
    parts = [
        pl.BlockSpec((one, D), lambda i, j=j: (jnp.clip((i - j) // 2, 0, 1), 0)) for j in (0, 0, 4, 4)
    ]
    return pl.pallas_call(
        down_kernel,
        grid=(8,),
        in_specs=[
            pl.BlockSpec((one, width), lambda i: (i, 0)),
            pl.BlockSpec((D, width), lambda i: (0, 0)),
        ],
        out_specs=parts,
        out_shape=[jax.ShapeDtypeStruct((2 * one, D), BF)] * 4,
        compiler_params=pltpu.CompilerParams(vmem_limit_bytes=VMEM_LIMIT),
        cost_estimate=cost(
            flops=2 * length * D * width, bytes_accessed=14 * 2**20, transcendentals=0
        ),
        name="down",
    )(left, right)


def total_of(*parts):
    return sum(part.astype(F32) for part in parts)


class EightSum:
    def __init__(self, parts):
        self.keep = parts[:4]
        self.core = [None] * 4
        for k in (3, 1, 2, 0):
            self.core[k] = swap(parts[4 + k], "core")
        self.half = parts[0].shape[0] // 2

    def second(self, order):
        self.core = order.done(self.core)
        half = self.half
        both, by_x, by_lo = [total_of(self.keep[k], self.core[k]) for k in (3, 1, 2)]
        self.to_lo = swap(both[:half].astype(BF), "tensor")
        self.to_x = swap(both[half:].astype(BF), "lo")
        self.x_first = swap(by_x[:half].astype(BF), "tensor")
        self.lo_second = swap(by_lo[half:].astype(BF), "lo")
        self.by_x, self.by_lo = by_x[half:], by_lo[:half]

    def third(self, order):
        to_lo, to_x, self.x_first, self.lo_second = order.done(
            (self.to_lo, self.to_x, self.x_first, self.lo_second)
        )
        self.x_second = swap(total_of(self.by_x, to_x).astype(BF), "tensor")
        self.lo_first = swap(total_of(self.by_lo, to_lo).astype(BF), "lo")

    def total(self, order):
        x_second, lo_first = order.done((self.x_second, self.lo_first))
        return (
            total_of(self.keep[0], self.core[0])
            + jnp.concatenate([self.x_first, x_second], axis=0).astype(F32)
            + jnp.concatenate([lo_first, self.lo_second], axis=0).astype(F32)
        )


class BranchSum:
    def __init__(self, near, by_x, core_near, core_by_x):
        self.near, self.by_x = near, by_x
        self.core = swap(core_by_x, "core"), swap(core_near, "core")

    def along_x(self, order):
        by_x, near = order.done(self.core)
        self.near = total_of(self.near, near)
        self.x = swap(total_of(self.by_x, by_x).astype(BF), "tensor")

    def along_lo(self, order):
        total = self.near + order.done(self.x).astype(F32)
        half = total.shape[0] // 2
        self.own = total[:half]
        self.lo = swap(total[half:].astype(BF), "lo")

    def arrived(self, order):
        self.lo = order.done(self.lo)

    def total(self):
        return self.own + self.lo.astype(F32)


class FourSum:
    def __init__(self, own, first, second, core_own, core_first, core_second):
        self.own, self.x = own, (first, second)
        self.core_x = swap(core_first, "core"), swap(core_second, "core")
        self.core_own = swap(core_own, "core")

    def second(self, order):
        core_x = order.done(self.core_x)
        by_x = [total_of(*pair).astype(BF) for pair in zip(self.x, core_x)]
        self.x = [swap(part, "tensor") for part in by_x]

    def total(self, order):
        self.core_own = order.done(self.core_own)
        x = order.done(self.x)
        return total_of(self.own, self.core_own, jnp.concatenate(x, axis=0))


class GradSum:
    def __init__(self, keep, send):
        self.keep = keep
        self.other = swap(send, "yy")

    def across(self, order, by_gather):
        self.other = order.done(self.other)
        count = lax.axis_size("hi")
        far = [total_of(self.keep[k], self.other[k]).astype(BF) for k in range(1, count)]
        if by_gather:
            self.every = [lax.all_gather(part, "hi") for part in far]
        else:
            self.every = None
            self.far = [turn(part, "hi", k + 1) for k, part in enumerate(far)]

    def arrived(self, order):
        if self.every is None:
            self.far = order.done(self.far)
        else:
            every = order.done(self.every)
            self.far = [others_of(part)[k] for k, part in enumerate(every)]

    def total(self):
        total = self.keep[0].astype(F32) + self.other[0].astype(F32)
        for far in self.far:
            total = total + far.astype(F32)
        return total


def body(
    tokens,
    cotangent,
    segments,
    small_params,
    small_first,
    small_second,
    qkv_weight,
    qkv_first,
    qkv_second,
    out_weight,
    out_first,
    out_second,
    gateup_weight,
    gateup_first,
    gateup_second,
    down_weight,
    down_first,
    down_second,
):
    hi_count = lax.axis_size("hi")
    hi, lo, yy = lax.axis_index("hi"), lax.axis_index("lo"), lax.axis_index("yy")
    core = lax.axis_index("core")
    place_x = lax.axis_index("tensor")
    own_rows = tokens.shape[0]
    shard_rows = qkv_weight.shape[0]
    gain_one = small_params[:D]
    gain_two = small_params[D : 2 * D]
    bias_all = small_params[2 * D :]
    q_at = place_x * (bias_all.shape[0] // 2) + core * Q_COLS
    kv_at = place_x * (bias_all.shape[0] // 2) + 2 * Q_COLS
    bias_local = jnp.concatenate(
        [
            lax.dynamic_slice_in_dim(bias_all, q_at, Q_COLS),
            lax.dynamic_slice_in_dim(bias_all, kv_at, 2 * HEAD_WIDTH),
        ]
    )

    order = Order()
    steps = range(1, hi_count)

    def both_cores(mine, other, axis):
        return jnp.where(
            core == 0,
            jnp.concatenate([mine, other], axis=axis),
            jnp.concatenate([other, mine], axis=axis),
        )

    other_ids = swap(segments, "core")
    qkv_low = qkv_weight.astype(BF)
    out_low = out_weight.astype(BF).T

    def attention_pack(which):
        return jnp.concatenate(
            [
                lax.dynamic_slice_in_dim(qkv_low, which * Q_COLS, Q_COLS, 1),
                qkv_low[:, 2 * Q_COLS :],
                lax.dynamic_slice_in_dim(out_low, which * Q_COLS, Q_COLS, 1),
            ],
            axis=1,
        )

    att_theirs = attention_pack(1 - core)
    att_core = swap(att_theirs, "core")
    order.mark = att_theirs
    rows_in = order.after(tokens).astype(F32)
    scale_one = rms_scale(rows_in)
    n1 = (rows_in * scale_one * gain_one).astype(BF)
    n1_x = swap(n1, "tensor")
    order.mark = n1
    att_shard = both_cores(attention_pack(core), order.done(att_core), 0)
    order.mark = att_shard
    att_hi = [turn(att_shard, "hi", k) for k in steps]
    att_yy = swap(att_shard, "yy")
    att_lo = swap(att_shard, "lo")

    gateup_in, down_in = order.after((gateup_weight, down_weight))
    ff_low = jnp.pad(
        jnp.concatenate([gateup_in.astype(BF), down_in.astype(BF).T[None]], axis=0),
        ((0, 0), (0, 0), (0, FF_PAD - FF_LOCAL)),
    )
    ff_mine = lax.dynamic_slice_in_dim(ff_low, core * FF_CORE, FF_CORE, 2)
    ff_theirs = lax.dynamic_slice_in_dim(ff_low, (1 - core) * FF_CORE, FF_CORE, 2)
    ff_core = swap(ff_theirs, "core")
    order.mark = ff_theirs

    ff_shard = both_cores(ff_mine, order.done(ff_core), 1)
    ff_own = lax.dynamic_slice_in_dim(ff_shard, lo * FF_OWN, FF_OWN, 2)
    ff_theirs = lax.dynamic_slice_in_dim(ff_shard, (1 - lo) * FF_OWN, FF_OWN, 2)
    order.mark = ff_theirs
    att_lo = order.done(att_lo)
    att_lo_yy = swap(att_lo, "yy")
    att_yy = order.done(att_yy)
    att_hi = order.done(att_hi)
    att_hi_lo = [swap(part, "lo") for part in att_hi]
    att_hi_yy = [swap(part, "yy") for part in att_hi]
    n1_core = swap(order.after(n1), "core")
    att_lo_yy = order.done(att_lo_yy)
    att_hi_lo = order.done(att_hi_lo)
    att_hi_lo_yy = [swap(part, "yy") for part in att_hi_lo]
    ff_lo = swap(order.after(ff_theirs), "lo")
    ff_hi = lax.all_gather(order.after(ff_own), "hi")
    n1_core = order.done(n1_core)
    other_ids = order.done(other_ids)
    angles, key_place, row_place, row_start = documents(core, place_x, segments, other_ids)
    sign = jnp.where(jnp.arange(HEAD_WIDTH) < HEAD_WIDTH // 2, -1.0, 1.0)
    tables = order.after((jnp.cos(angles), jnp.sin(angles) * sign, key_place, row_place, row_start))
    order.mark = tables[0]
    att_hi_yy = order.done(att_hi_yy)
    n1_x = order.done(n1_x)
    n1_core_x = swap(n1_x, "core")
    cot_x = swap(order.after(cotangent), "tensor")
    n1_core_x = order.done(n1_core_x)
    att_hi_lo_yy = order.done(att_hi_lo_yy)
    ff_yy = swap(order.after(ff_own), "yy")

    near_parts = [att_shard, att_lo]
    yy_parts = [att_yy, att_lo_yy]
    for k in range(hi_count - 1):
        near_parts += [att_hi[k], att_hi_lo[k]]
        yy_parts += [att_hi_yy[k], att_hi_lo_yy[k]]
    att_parts = near_parts + yy_parts
    n1_parts = order.after((n1, n1_x, n1_core, n1_core_x))
    qkv, attn_rows, lse, *out_parts, att_weight = attention(
        tree_order(-1), n1_parts, bias_local[None], tables, att_parts
    )
    order.mark = lse

    out = FourSum(*out_parts)
    half = own_rows // 2
    cot_x = order.done(cot_x)
    ff_lo = order.done(ff_lo)
    ff_lo_hi_gu = lax.all_gather(ff_lo[:2], "hi")
    ff_yy = order.done(ff_yy)
    ff_lo_yy = swap(ff_lo, "yy")
    out.second(order)
    ff_hi = others_of(order.done(ff_hi))
    order.mark = ff_hi
    residual = rows_in + out.total(order)
    scale_two = rms_scale(residual)
    n2 = (residual * scale_two * gain_two).astype(BF)
    n2_x_second, n2_lo_first = swap(n2[half:], "tensor"), swap(n2[:half], "lo")
    n2_x_first, n2_lo_second = swap(n2[:half], "tensor"), swap(n2[half:], "lo")
    order.mark = n2
    ff_lo_yy = order.done(ff_lo_yy)
    ff_hi_yy = [swap(order.after(part), "yy") for part in ff_hi]
    n2_x_second, n2_lo_first = order.done((n2_x_second, n2_lo_first))
    n2_both = swap(n2_lo_first, "tensor"), swap(n2_x_second, "lo")
    n2_x_first, n2_lo_second = order.done((n2_x_first, n2_lo_second))
    n2_near = jnp.concatenate([n2_x_first, n2_x_second, n2_lo_first, n2_lo_second])
    n2_core_near, n2_core = swap(n2_near, "core"), swap(n2, "core")
    ff_lo_hi_gu = others_of(order.done(ff_lo_hi_gu))
    n2_both = jnp.concatenate(order.done(n2_both))
    n2_core_near, n2_core = order.done((n2_core_near, n2_core))
    n2_core_both = swap(n2_both, "core")
    cot_lo = swap(order.after(cotangent), "lo")
    ff_lo_hi_yy_gu = [swap(order.after(part), "yy") for part in ff_lo_hi_gu]
    ff_lo_hi_d = [turn(order.after(ff_lo[2]), "hi", k) for k in steps]
    ff_hi_yy = order.done(ff_hi_yy)
    cot_both_lo = swap(cot_x[half:], "lo")
    cot_core = swap(order.after(cotangent), "core")
    n2_core_both = order.done(n2_core_both)
    ff_lo_hi_yy_gu = order.done(ff_lo_hi_yy_gu)
    n2_parts = [n2, n2_near, n2_both, n2_core, n2_core_near, n2_core_both]

    whole = [ff_own, ff_lo, ff_yy, ff_lo_yy, *ff_hi, *ff_hi_yy]
    gu_pieces = [*whole, *ff_lo_hi_gu, *ff_lo_hi_yy_gu]
    ff_chips = [chip_at(0, l, y) for y in (0, 1) for l in (0, 1)]
    ff_chips += [chip_at(-k, l, y) for l in (0, 1) for y in (0, 1) for k in steps]
    ff_chips = jnp.stack(ff_chips).astype(jnp.int32)
    gates, n2_t = gate_up(ff_chips, order.after(n2_parts), gu_pieces)
    order.mark = gates
    cot_lo = order.done(cot_lo)
    cot_both_x = swap(cot_lo[:half], "tensor")
    cot_near = jnp.concatenate([cot_x, cot_lo])
    cot_core_near = swap(cot_near, "core")
    ff_lo_hi_d = order.done(ff_lo_hi_d)
    ff_lo_hi_yy_d = [swap(part, "yy") for part in ff_lo_hi_d]
    cot_core, cot_both_lo = order.done((cot_core, cot_both_lo))
    cot_both = jnp.concatenate([order.done(cot_both_x), cot_both_lo])
    cot_core_both = swap(cot_both, "core")
    cot_core_near = order.done(cot_core_near)
    ff_lo_hi_yy_d = order.done(ff_lo_hi_yy_d)
    cot_core_both = order.done(cot_core_both)
    cot_parts = [cotangent, cot_near, cot_both, cot_core, cot_core_near, cot_core_both]
    d_pieces = [*whole, *ff_lo_hi_d, *ff_lo_hi_yy_d]
    *dn2_parts, hidden, gate_grad, up_grad, cot_t, w_down = feed_forward(
        ff_chips, gates, order.after(cot_parts), gu_pieces, d_pieces
    )
    order.mark = w_down

    place = jnp.stack([hi, lo, yy]).astype(jnp.int32)

    def grad_of(left, right):
        keep, send = weight_grad(place, order.after(left), right)
        order.mark = keep
        return GradSum(keep, send)

    ff_squares = 0.0
    rows_of = lambda value, which, axis: lax.dynamic_slice_in_dim(
        value, which * shard_rows, shard_rows, axis
    )

    def summed_up(grad):
        nonlocal ff_squares
        total = order.after(grad.total())
        ff_squares = ff_squares + jnp.sum(total * total)
        low = total.astype(BF)
        order.mark = low
        return low[0], swap(low[1], "lo")

    def own_rows_of(low, other):
        other = order.done(other)
        cols = jnp.where(
            lo == 0,
            jnp.concatenate([low, other], axis=1),
            jnp.concatenate([other, low], axis=1),
        )
        theirs = rows_of(cols, 1 - core, 0)
        order.mark = theirs
        return rows_of(cols, core, 0), swap(theirs, "core")

    dn2 = EightSum(dn2_parts)
    d_sum = grad_of(cot_t, hidden)
    dn2.second(order)
    g_sum = grad_of(n2_t, gate_grad)
    dn2.third(order)
    u_sum = grad_of(n2_t, up_grad)
    d_sum.across(order, True)
    norm_two_in, gain_two_grad = norm_backward(residual, scale_two, gain_two, dn2.total(order))
    residual_grad = cotangent.astype(F32) + norm_two_in
    da = residual_grad.astype(BF)
    da_x = [swap(da[:half], "tensor"), swap(da[half:], "tensor")]
    da_core = swap(da, "core")
    order.mark = da
    branch_parts = down(*order.after((hidden, w_down)))
    order.mark = branch_parts[0]
    branch = BranchSum(*branch_parts)
    da_x = order.done(da_x)
    da_core_x = [swap(part, "core") for part in da_x]
    da_core, da_core_x = order.done((da_core, da_core_x))
    g_sum.across(order, False)

    _, bias_grad, *parts = attention_back(
        sum_order(),
        order.after((da, *da_x, da_core, *da_core_x)),
        n1_parts,
        qkv,
        attn_rows,
        lse,
        att_weight,
        tables,
    )
    order.mark = bias_grad
    d_sum.arrived(order)
    dn1 = FourSum(*parts[:6])
    att = ChipSum(*parts[6:])
    dn1.second(order)
    g_sum.arrived(order)
    norm_one_in, gain_one_grad = norm_backward(rows_in, scale_one, gain_one, dn1.total(order))
    u_sum.across(order, False)
    att.far_yy(order)
    bias_grad = order.after(bias_grad)[0]
    bias_slots = lax.dynamic_update_slice_in_dim(
        jnp.zeros_like(bias_all), bias_grad[:Q_COLS], q_at, 0
    )
    bias_slots = lax.dynamic_update_slice_in_dim(bias_slots, bias_grad[Q_COLS:], kv_at, 0)
    att.far_hi(order)
    branch.along_x(order)
    d_low, d_way = summed_up(d_sum)
    g_low, g_way = summed_up(g_sum)
    att.near_yy(order)
    input_grad = residual_grad + norm_one_in
    branch.along_lo(order)
    u_sum.arrived(order)
    att_sum = att.total(order)
    att_low = att_sum.astype(BF)
    other_att = swap(rows_of(att_low, 1 - core, 0), "core")
    u_low, u_way = summed_up(u_sum)
    other_att = order.done(other_att)
    d_rows = own_rows_of(d_low, d_way)
    g_rows = own_rows_of(g_low, g_way)
    branch.arrived(order)

    own_att = rows_of(att_low, core, 0)
    first_att = jnp.where(core == 0, own_att, other_att).astype(F32)
    second_att = jnp.where(core == 0, other_att, own_att).astype(F32)
    kv_sum = first_att[:, Q_COLS:QKV_COLS] + second_att[:, Q_COLS:QKV_COLS]
    qkv_owned = jnp.concatenate([first_att[:, :Q_COLS], second_att[:, :Q_COLS], kv_sum], axis=1)
    out_owned = jnp.concatenate([first_att[:, QKV_COLS:], second_att[:, QKV_COLS:]], axis=1).T
    owned_squares = (
        jnp.sum(qkv_owned * qkv_owned) + jnp.sum(out_owned * out_owned) + ff_squares
    )
    summed = jnp.concatenate(
        [gain_one_grad, gain_two_grad, bias_slots, jnp.full((128,), owned_squares)]
    )
    summed = summed + order.done(swap(summed, "core"))
    summed = summed + order.done(swap(summed, "tensor"))
    summed = summed + order.done(swap(summed, "yy"))
    summed = summed + order.done(swap(summed, "lo"))
    step = 1
    while step < hi_count:
        moved = lax.ppermute(summed, "hi", [(i, i ^ step) for i in range(hi_count)])
        summed = summed + order.done(moved)
        step *= 2
    order.mark = summed
    u_rows = own_rows_of(u_low, u_way)
    block_out = (residual + order.after(branch.total())).astype(BF)

    def owned(rows):
        mine, other = rows
        return both_cores(mine, other, 1)[:, :FF_LOCAL].astype(F32)

    gateup_owned = jnp.stack([owned(g_rows), owned(u_rows)])
    down_owned = owned(d_rows).T
    small_grad = summed[:-128]
    squares = summed[-1] + jnp.sum(small_grad * small_grad)
    grad_norm = jnp.sqrt(squares)
    clip_factor = jnp.minimum(1.0, MAX_NORM / (grad_norm + 1e-06))
    new_small, new_small_first, new_small_second = adam_update(
        small_params, small_first, small_second, clip_factor * small_grad, 0.5, 0.0
    )
    new_qkv, new_qkv_first, new_qkv_second = adam_update(
        qkv_weight, qkv_first, qkv_second, clip_factor * qkv_owned, 2.0 / math.sqrt(D), WEIGHT_DECAY
    )
    new_out, new_out_first, new_out_second = adam_update(
        out_weight,
        out_first,
        out_second,
        clip_factor * out_owned,
        8.0 / math.sqrt(QUERY_HEADS * HEAD_WIDTH),
        WEIGHT_DECAY,
    )
    new_gateup, new_gateup_first, new_gateup_second = adam_update(
        gateup_weight,
        gateup_first,
        gateup_second,
        clip_factor * gateup_owned,
        2.0 / math.sqrt(D),
        WEIGHT_DECAY,
    )
    new_down, new_down_first, new_down_second = adam_update(
        down_weight,
        down_first,
        down_second,
        clip_factor * down_owned,
        3.0 / math.sqrt(FF),
        WEIGHT_DECAY,
    )
    return (
        block_out,
        input_grad,
        grad_norm,
        new_small,
        new_small_first,
        new_small_second,
        new_qkv,
        new_qkv_first,
        new_qkv_second,
        new_out,
        new_out_first,
        new_out_second,
        new_gateup,
        new_gateup_first,
        new_gateup_second,
        new_down,
        new_down_first,
        new_down_second,
    )


def solution(mesh):
    count = mesh.shape["dp"]
    fine = Mesh(
        mesh.devices.reshape(count // 8, 2, 2, 2, mesh.shape["tensor"]),
        CHIP + ("core", "tensor"),
    )
    dp = CHIP + ("core",)
    rows = P(dp + ("tensor",), None)
    by_rows = P(dp, "tensor")
    by_cols = P("tensor", dp)
    stacked = P(None, dp, "tensor")
    weights = (by_rows,) * 3 + (by_cols,) * 3 + (stacked,) * 3 + (by_cols,) * 3
    return jax.shard_map(
        body,
        mesh=fine,
        in_specs=(rows, rows, P(dp), P(), P(), P()) + weights,
        out_specs=(rows, rows, P(), P(), P(), P()) + weights,
        check_vma=False,
    )
```
